512 devices in a mesh: sim: 128 (over y, z, core), grp: 4 (over x).
Axes of the slice: x: 4, y: 4, z: 16, core: 2. Of those that a mesh axis runs over, the one named last changes fastest.
Arguments:
- species: float32 [2, 512, 128, 1024], P(None, ('sim', 'grp')), may hold values from 0 to 1
Outputs:
- species_next: float32 [2, 512, 128, 1024], P(None, ('sim', 'grp'))
- frame: float32 [4, 256, 2048], P(None, 'sim', 'grp')
The draws below stay inside these ranges and needn't reach their ends.
All inputs are finite; a program needn't handle non-finite values.
Results may differ from the reference program's by a relative error of at most 0.000034.
Values sent between devices are 32-bit elements; how exact they have to be, the bound alone decides.
A program may use at most 192 MiB of HBM per device.

```python
import jax
import jax.numpy as jnp
from jax import lax

NX = 128
NY = 1024
NZ = 512


def block_levels(key, shape, split, smallest, largest):
    def one(dim, shards_of):
        steps = jax.random.uniform(jax.random.fold_in(jax.random.fold_in(key, 6), dim), (shards_of,), jnp.float32, smallest / len(split), largest / len(split))
        return jnp.repeat(jnp.exp(steps), shape[dim] // shards_of).reshape((-1,) + (1,) * (len(shape) - dim - 1))

    loudness = one(*split[0])
    for cut in split[1:]:
        loudness = loudness * one(*cut)
    return loudness


def setup_inputs(seed: int = 0) -> dict:
    seeds = jax.random.split(jax.random.key(seed), 2)
    return {
        "species": jnp.clip(1.0 * jax.random.uniform(seeds[0], (2, NZ, NX, NY), jnp.float32) ** block_levels(seeds[0], (2, NZ, NX, NY), ((1, 512),), -0.2, 0.2), 0.0, 1.0),
    }


diff_substrate = 0.16
diff_catalyst = 0.08
feed_rate = 0.035
kill_rate = 0.065


def react_diffuse(padded_z):
    padded = jnp.pad(padded_z, ((0, 0), (0, 0), (1, 1), (1, 1)))
    center = padded[:, 1:-1, 1:-1, 1:-1]
    neighbours = padded[:, 2:, 1:-1, 1:-1] + padded[:, :-2, 1:-1, 1:-1]
    neighbours = neighbours + padded[:, 1:-1, 2:, 1:-1] + padded[:, 1:-1, :-2, 1:-1]
    neighbours = neighbours + padded[:, 1:-1, 1:-1, 2:] + padded[:, 1:-1, 1:-1, :-2]
    laplace_term = neighbours - 6.0 * center
    substrate = center[0]
    catalyst = center[1]
    reaction = substrate * catalyst * catalyst
    new_substrate = substrate + diff_substrate * laplace_term[0] - reaction + feed_rate * (1.0 - substrate)
    new_catalyst = catalyst + diff_catalyst * laplace_term[1] + reaction - (feed_rate + kill_rate) * catalyst
    return jnp.stack([new_substrate, new_catalyst])


def refine(values, axis_num):
    length = values.shape[axis_num]
    lower_side = jnp.concatenate([lax.slice_in_dim(values, 0, 1, axis=axis_num), lax.slice_in_dim(values, 0, length - 1, axis=axis_num)], axis_num)
    upper_side = jnp.concatenate([lax.slice_in_dim(values, 1, length, axis=axis_num), lax.slice_in_dim(values, length - 1, length, axis=axis_num)], axis_num)
    even_part = 0.75 * values + 0.25 * lower_side
    odd_part = 0.75 * values + 0.25 * upper_side
    paired = jnp.stack([even_part, odd_part], axis=axis_num + 1)
    new_shape = list(values.shape)
    new_shape[axis_num] = 2 * length
    return paired.reshape(new_shape)


def shade(sample, extinct):
    opacity = 1.0 - jnp.exp(-extinct * sample * sample)
    red_part = jax.nn.sigmoid(6.0 * (sample - 0.5))
    green_part = jnp.exp(-8.0 * (sample - 0.5) * (sample - 0.5))
    blue_part = jax.nn.sigmoid(-6.0 * (sample - 0.3))
    return jnp.stack([opacity * red_part, opacity * green_part, opacity * blue_part, opacity], axis=-3)


def over(front_part, back_part):
    return front_part + (1.0 - front_part[..., 3:4, :, :]) * back_part


def reference(species):
    padded_z = jnp.pad(species, ((0, 0), (1, 1), (0, 0), (0, 0)))
    extinct = 6.0 / NZ

    def advance(picture, index):
        window = lax.dynamic_slice_in_dim(padded_z, index, 3, axis=1)
        fresh = react_diffuse(window)
        sample = refine(refine(fresh[1, 0], 0), 1)
        picture = over(picture, shade(sample, extinct))
        return picture, fresh[:, 0]

    start = jnp.zeros((4, 2 * NX, 2 * NY), jnp.float32)
    picture, planes = lax.scan(advance, start, jnp.arange(NZ, dtype=jnp.int32))
    return jnp.transpose(planes, (1, 0, 2, 3)), picture
```

```python
import jax
import jax.numpy as jnp
from jax import lax
from jax.experimental import pallas as pl
from jax.experimental.pallas import tpu as pltpu
from jax.sharding import PartitionSpec as P

MESH = pl.DeviceIdType.MESH

ROWS = 128
COLS = 1024
GRP = 4
SIMS = 128
SUB = 8
BLOCKS = SIMS // SUB
MEMBERS = GRP * SUB
REGION = ROWS // SUB
CHUNKS = 8
CHUNK = ROWS // CHUNKS
SLOT = 40
PIECE = 32

DIFF_S, DIFF_C, FEED, KILL = 0.16, 0.08, 0.035, 0.065


def to(sim, grp):
    return {"sim": sim, "grp": grp}


def laplacian(buf, up, dn, r):
    window = buf[pl.ds(r, 24), :]
    center = window[8:16]
    lane = lax.broadcasted_iota(jnp.int32, (8, COLS), 1)
    left = jnp.where(lane == 0, 0.0, pltpu.roll(center, 1, 1))
    right = jnp.where(lane == COLS - 1, 0.0, pltpu.roll(center, COLS - 1, 1))
    total = up[pl.ds(r, 8), :] + dn[pl.ds(r, 8), :]
    total = total + window[7:15] + window[9:17] + left + right
    return center, total - 6.0 * center


def kernel(
    species, next_out, frame_out,
    sbuf, cbuf, s_up, s_dn, c_up, c_dn, s_new, c_new, edge_cols, sendbuf, recvbuf, pack, parts,
    load_sem, store_sem, halo_send, halo_recv, own_sem, mix_send, mix_recv, part_own, part_send, part_recv,
):
    sim, grp = lax.axis_index("sim"), lax.axis_index("grp")
    plane = sim * GRP + grp
    block, member = lax.div(sim, SUB), lax.rem(sim, SUB)
    seat = member * GRP + grp
    turn = lax.div(block, 4) + lax.rem(block, 4)

    def region_of(m, turn):
        return 2 * lax.rem(lax.div(m, 2) + 8 - turn, 4) + lax.rem(m, 2)

    def member_of(q, turn):
        return 2 * lax.rem(lax.div(q, 2) + turn, 4) + lax.rem(q, 2)

    region = region_of(member, turn)

    def source(b):
        t = lax.div(b, 4) + lax.rem(b, 4)
        return b * SUB + member_of(lax.div(sim, REGION), t)

    loads = [
        pltpu.make_async_copy(species.at[i, 0], buf.at[pl.ds(8, ROWS), :], load_sem.at[i])
        for i, buf in ((0, sbuf), (1, cbuf))
    ]
    loads[1].start()
    loads[0].start()

    has_prev, has_next = plane > 0, plane < SIMS * GRP - 1
    prev = to(lax.div(plane - 1, GRP), lax.rem(plane - 1 + GRP, GRP))
    nxt = to(lax.div(plane + 1, GRP), lax.rem(plane + 1, GRP))
    barrier = pltpu.get_barrier_semaphore()

    @pl.when(has_prev)
    def _():
        pl.semaphore_signal(barrier, inc=1, device_id=prev, device_id_type=MESH)

    @pl.when(has_next)
    def _():
        pl.semaphore_signal(barrier, inc=1, device_id=nxt, device_id_type=MESH)

    def greet_member(d, _):
        other = lax.rem(seat + d, MEMBERS)
        there = to(block * SUB + lax.div(other, GRP), lax.rem(other, GRP))
        pl.semaphore_signal(barrier, inc=1, device_id=there, device_id_type=MESH)
        return 0

    lax.fori_loop(1, MEMBERS, greet_member, 0)

    def greet_source(b, _):
        there = source(b)

        @pl.when(there != sim)
        def _():
            pl.semaphore_signal(barrier, inc=1, device_id=to(there, grp), device_id_type=MESH)

        return 0

    lax.fori_loop(0, BLOCKS, greet_source, 0)

    for buf in (sbuf, cbuf):
        buf[0:8, :] = jnp.zeros((8, COLS), jnp.float32)
        buf[ROWS + 8 : ROWS + 16, :] = jnp.zeros((8, COLS), jnp.float32)

    @pl.when(plane == 0)
    def _():
        s_up[...] = jnp.zeros_like(s_up)
        c_up[...] = jnp.zeros_like(c_up)

    @pl.when(plane == SIMS * GRP - 1)
    def _():
        s_dn[...] = jnp.zeros_like(s_dn)
        c_dn[...] = jnp.zeros_like(c_dn)

    self_part = lax.div(sim, REGION) == region
    expected = MEMBERS - 1 + BLOCKS - self_part.astype(jnp.int32)
    expected = expected + has_prev.astype(jnp.int32) + has_next.astype(jnp.int32)
    pl.semaphore_wait(barrier, expected)

    def halo(i, way, rows):
        target = ((s_up, s_dn), (c_up, c_dn))[i][way]
        return lambda chunk: pltpu.make_async_remote_copy(
            src_ref=species.at[i, 0, rows, :],
            dst_ref=target.at[rows, :],
            send_sem=halo_send.at[i, way],
            recv_sem=halo_recv.at[i, way, chunk],
            device_id=(nxt, prev)[way],
            device_id_type=MESH,
        )

    def chunk_rows(k):
        return pl.ds(pl.multiple_of(k * CHUNK, CHUNK), CHUNK)

    whole = pl.ds(0, ROWS)

    def send_catalyst(k, _):
        @pl.when(has_next)
        def _():
            halo(1, 0, chunk_rows(k))(k).start()

        @pl.when(has_prev)
        def _():
            halo(1, 1, chunk_rows(k))(k).start()

        return 0

    lax.fori_loop(0, CHUNKS, send_catalyst, 0)
    loads[1].wait()

    loads[0].wait()
    lane = lax.broadcasted_iota(jnp.int32, (8, 128), 1)
    beside = [(0, 0), (2, 0), (1, 127), (4, 0), (3, 127), (6, 0), (5, 127), (7, 127)]

    def catalyst_chunk(k, _):
        @pl.when(has_prev)
        def _():
            halo(1, 0, chunk_rows(k))(k).wait_recv()

        @pl.when(has_next)
        def _():
            halo(1, 1, chunk_rows(k))(k).wait_recv()

        for h in range(CHUNK // 8):
            r = pl.multiple_of(k * CHUNK + 8 * h, 8)
            c, lap = laplacian(cbuf, c_up, c_dn, r)
            s = sbuf[pl.ds(pl.multiple_of(r + 8, 8), 8), :]
            new = c + DIFF_C * lap + s * c * c - (FEED + KILL) * c
            c_new[pl.ds(r, 8), :] = new
            columns = jnp.zeros((8, 128), jnp.float32)
            for n, (tile, at) in enumerate(beside):
                moved = pltpu.roll(new[:, tile * 128 : tile * 128 + 128], (n - at) % 128, 1)
                columns = jnp.where(lane == n, moved, columns)
            edge_cols[pl.ds(r, 8), :] = columns
            for tile in range(COLS // 128):
                slot = (k * GRP + tile // 2) * SLOT + (h * 2 + tile % 2) * 8
                sendbuf[pl.ds(pl.multiple_of(slot, 8), 8), :] = new[:, tile * 128 : tile * 128 + 128]
        return 0

    lax.fori_loop(0, CHUNKS, catalyst_chunk, 0)

    store_c = pltpu.make_async_copy(c_new, next_out.at[1, 0], store_sem.at[1])
    store_c.start()

    beside_t = jnp.transpose(edge_cols[...])[0:8]

    for q in range(SUB):
        above, below = max(q * REGION - 1, 0), min(q * REGION + REGION, ROWS - 1)
        cols = pltpu.roll(beside_t, (1 - q * REGION) % ROWS, 1)
        if q == 0:
            cols = jnp.where(lane == 0, beside_t, cols)
        if q == SUB - 1:
            cols = jnp.where(lane == REGION + 1, pltpu.roll(beside_t, REGION + 2, 1), cols)
        for x in range(GRP):
            base = (q * GRP + x) * SLOT + 32
            for t in range(2):
                col = (2 * x + t) * 128
                sendbuf[base + t : base + t + 1, :] = c_new[above : above + 1, col : col + 128]
                sendbuf[base + 2 + t : base + 3 + t, :] = c_new[below : below + 1, col : col + 128]
            sendbuf[base + 4 : base + 6, :] = cols[2 * x : 2 * x + 2]
            sendbuf[base + 6 : base + 8, :] = jnp.zeros((2, 128), jnp.float32)

    def slot_rows(n):
        return pl.ds(pl.multiple_of(n * SLOT, SLOT), SLOT)

    def mix(other):
        m, x = lax.div(other, GRP), lax.rem(other, GRP)
        return pltpu.make_async_remote_copy(
            src_ref=sendbuf.at[slot_rows(region_of(m, turn) * GRP + x), :],
            dst_ref=recvbuf.at[slot_rows(seat), :],
            send_sem=mix_send,
            recv_sem=mix_recv,
            device_id=to(block * SUB + m, x),
            device_id_type=MESH,
        )

    def send_region(d, _):
        mix(lax.rem(seat + d, MEMBERS)).start()
        return 0

    lax.fori_loop(1, MEMBERS, send_region, 0)
    own = pltpu.make_async_copy(
        sendbuf.at[slot_rows(region * GRP + grp), :], recvbuf.at[slot_rows(seat), :], own_sem
    )
    own.start()

    @pl.when(has_next)
    def _():
        halo(0, 0, whole)(0).start()

    @pl.when(has_prev)
    def _():
        halo(0, 1, whole)(0).start()

    own.wait()
    others = pl.ds(0, (MEMBERS - 1) * SLOT)
    all_mixed = pltpu.make_async_remote_copy(
        src_ref=sendbuf.at[others, :], dst_ref=recvbuf.at[others, :],
        send_sem=mix_send, recv_sem=mix_recv, device_id=to(sim, grp), device_id_type=MESH,
    )
    all_mixed.wait_recv()

    sides = jnp.concatenate(
        [
            recvbuf[pl.ds(36, MEMBERS, stride=SLOT), :],
            recvbuf[pl.ds(37, MEMBERS, stride=SLOT), :],
            jnp.zeros((128 - 2 * MEMBERS, 128), jnp.float32),
        ],
        axis=0,
    )
    sides = jnp.transpose(sides)
    row = lax.broadcasted_iota(jnp.int32, (8, 128), 0)
    extinct = 6.0 / (BLOCKS * MEMBERS)

    for h in range(2):
        for par in range(2):
            near = 2 * par
            side = 0.75 * sides[1 + 8 * h : 9 + 8 * h] + 0.25 * sides[near + 8 * h : near + 8 * h + 8]

            def layer(p, totals, h=h, par=par, side=side):
                base = pl.multiple_of(p * SLOT, 8)
                rim = recvbuf[pl.ds(base + 32, 8), :]
                rows = []
                for t in range(2):
                    mine = recvbuf[pl.ds(base + (2 * h + t) * 8, 8), :]
                    across = recvbuf[pl.ds(base + (2 - 2 * h + t) * 8, 8), :]
                    if par == 0:
                        beyond = rim[t : t + 1] if h == 0 else across[7:8]
                        shifted = jnp.where(row == 0, beyond, pltpu.roll(mine, 1, 0))
                    else:
                        beyond = rim[2 + t : 3 + t] if h == 1 else across[0:1]
                        shifted = jnp.where(row == 7, beyond, pltpu.roll(mine, 7, 0))
                    rows.append(0.75 * mine + 0.25 * shifted)
                leftmost = pltpu.roll(side, lax.rem(128 - p, 128), 1)
                rightmost = pltpu.roll(side, 127 - MEMBERS - p, 1)
                fwd = [pltpu.roll(v, 1, 1) for v in rows]
                bwd = [pltpu.roll(v, 127, 1) for v in rows]
                low = [jnp.where(lane == 0, leftmost, fwd[0]), jnp.where(lane == 0, fwd[0], fwd[1])]
                high = [jnp.where(lane == 127, bwd[1], bwd[0]), jnp.where(lane == 127, rightmost, bwd[1])]
                result = []
                for cpar in range(2):
                    for t in range(2):
                        q = 0.75 * rows[t] + 0.25 * (low, high)[cpar][t]
                        red, green, blue, clear = totals[(cpar * 2 + t) * 4 : (cpar * 2 + t) * 4 + 4]
                        after = clear * jnp.exp(-extinct * (q * q))
                        weight = clear - after
                        mid = q - 0.5
                        red = red + weight * jnp.tanh(3.0 * mid)
                        green = green + weight * jnp.exp(-8.0 * (mid * mid))
                        blue = blue + weight * jnp.tanh(3.0 * (q - 0.3))
                        result += [red, green, blue, after]
                return tuple(result)

            zero, one = jnp.zeros((8, 128), jnp.float32), jnp.ones((8, 128), jnp.float32)
            totals = lax.fori_loop(0, MEMBERS, layer, (zero, zero, zero, one) * 4)
            for cpar in range(2):
                for t in range(2):
                    for ch in range(4):
                        at = 8 * h * PIECE + ch * 8 + cpar * 4 + par * 2 + t
                        pack[pl.ds(at, 8, stride=PIECE), :] = totals[(cpar * 2 + t) * 4 + ch]

    def piece_rows(n):
        return pl.ds(pl.multiple_of(n * PIECE, PIECE), PIECE)

    def send_piece(n, _):
        j = lax.rem(n + sim, REGION)
        there = region * REGION + j

        @pl.when(there != sim)
        def _():
            pltpu.make_async_remote_copy(
                src_ref=pack.at[piece_rows(j), :],
                dst_ref=parts.at[piece_rows(block), :],
                send_sem=part_send,
                recv_sem=part_recv,
                device_id=to(there, grp),
                device_id_type=MESH,
            ).start()

        return 0

    lax.fori_loop(0, REGION, send_piece, 0)

    @pl.when(self_part)
    def _():
        mine = pltpu.make_async_copy(
            pack.at[piece_rows(lax.rem(sim, REGION)), :], parts.at[piece_rows(block), :], part_own
        )
        mine.start()
        mine.wait()

    @pl.when(has_prev)
    def _():
        halo(0, 0, whole)(0).wait_recv()

    @pl.when(has_next)
    def _():
        halo(0, 1, whole)(0).wait_recv()

    def substrate_rows(k, _):
        r = pl.multiple_of(8 * k, 8)
        s, lap = laplacian(sbuf, s_up, s_dn, r)
        c = cbuf[pl.ds(pl.multiple_of(r + 8, 8), 8), :]
        s_new[pl.ds(r, 8), :] = s + DIFF_S * lap - s * c * c + FEED * (1.0 - s)
        return 0

    lax.fori_loop(0, ROWS // 8, substrate_rows, 0)
    store_s = pltpu.make_async_copy(s_new, next_out.at[0, 0], store_sem.at[0])
    store_s.start()

    def wait_parts(count):
        some = pl.ds(0, count * PIECE)
        return pltpu.make_async_remote_copy(
            src_ref=pack.at[some, :], dst_ref=parts.at[some, :],
            send_sem=part_send, recv_sem=part_recv, device_id=to(sim, grp), device_id_type=MESH,
        )

    @pl.when(self_part)
    def _():
        wait_parts(BLOCKS - 1).wait_recv()

    @pl.when(jnp.logical_not(self_part))
    def _():
        wait_parts(BLOCKS).wait_recv()

    def add_block(b, totals):
        base = pl.multiple_of(b * PIECE, 8)
        red, green, blue, clear = totals
        got = [parts[pl.ds(base + 8 * ch, 8), :] for ch in range(4)]
        return (
            red + clear * got[0], green + clear * got[1], blue + clear * got[2], clear * got[3],
        )

    zero, one = jnp.zeros((8, 128), jnp.float32), jnp.ones((8, 128), jnp.float32)
    red, green, blue, clear = lax.fori_loop(0, BLOCKS, add_block, (zero, zero, zero, one))
    opaque = 1.0 - clear
    channels = [0.5 * (opaque + red), green, 0.5 * (opaque - blue), opaque]
    flat = jnp.concatenate([jnp.concatenate([v[0:4], v[4:8]], axis=1) for v in channels], axis=0)
    old = lax.broadcasted_iota(jnp.int32, (256, 256), 0)
    new = lax.broadcasted_iota(jnp.int32, (256, 256), 1)
    spread = jnp.where(new == 2 * lax.rem(old, 128) + lax.div(old, 128), 1.0, 0.0)
    mixed = jnp.dot(flat, spread, precision=lax.Precision.HIGHEST, preferred_element_type=jnp.float32)
    for ch in range(4):
        for par in range(2):
            for t in range(2):
                n = ch * 4 + par * 2 + t
                frame_out[ch, par : par + 1, t * 256 : t * 256 + 256] = mixed[n : n + 1]

    for i in range(2):
        @pl.when(has_next)
        def _(i=i):
            halo(i, 0, whole)(0).wait_send()

        @pl.when(has_prev)
        def _(i=i):
            halo(i, 1, whole)(0).wait_send()

    all_mixed.wait_send()

    @pl.when(self_part)
    def _():
        wait_parts(BLOCKS - 1).wait_send()

    @pl.when(jnp.logical_not(self_part))
    def _():
        wait_parts(BLOCKS).wait_send()

    store_c.wait()
    store_s.wait()


def shards(species):
    f32 = jnp.float32
    plane = pltpu.VMEM((ROWS, COLS), f32)
    padded = pltpu.VMEM((ROWS + 16, COLS), f32)
    dma = pltpu.SemaphoreType.DMA
    fresh, frame = pl.pallas_call(
        kernel,
        out_shape=(
            jax.ShapeDtypeStruct((2, 1, ROWS, COLS), f32),
            jax.ShapeDtypeStruct((4, 2 * ROWS // SIMS, 2 * COLS // GRP), f32),
        ),
        in_specs=[pl.BlockSpec(memory_space=pl.ANY)],
        out_specs=(pl.BlockSpec(memory_space=pl.ANY), pl.BlockSpec(memory_space=pltpu.VMEM)),
        scratch_shapes=[
            padded, padded, plane, plane, plane, plane,
            plane, plane,
            pltpu.VMEM((ROWS, 128), f32),
            pltpu.VMEM((MEMBERS * SLOT, 128), f32),
            pltpu.VMEM((MEMBERS * SLOT, 128), f32),
            pltpu.VMEM((REGION * PIECE, 128), f32),
            pltpu.VMEM((BLOCKS * PIECE, 128), f32),
            dma((2,)), dma((2,)), dma((2, 2)), dma((2, 2, CHUNKS)),
            dma, dma, dma, dma, dma, dma,
        ],
        compiler_params=pltpu.CompilerParams(
            collective_id=0, has_side_effects=True, vmem_limit_bytes=32 * 1024 * 1024
        ),
        cost_estimate=pl.CostEstimate(flops=20_000_000, bytes_accessed=4_000_000, transcendentals=2_000_000),
    )(species)
    return fresh, frame


def solution(mesh):
    return jax.shard_map(
        shards,
        mesh=mesh,
        in_specs=(P(None, ("sim", "grp"), None, None),),
        out_specs=(P(None, ("sim", "grp"), None, None), P(None, "sim", "grp")),
        check_vma=False,
    )
```

```python
import math

import jax
import jax.numpy as jnp
from jax import lax
from jax.experimental import pallas as pl
from jax.experimental.pallas import tpu as pltpu
from jax.sharding import PartitionSpec as P

MESH = pl.DeviceIdType.MESH

ROWS = 128
COLS = 1024
GRP = 4
SIMS = 128
SUB = 8
BLOCKS = SIMS // SUB
MEMBERS = GRP * SUB
REGION = ROWS // SUB
CHUNKS = 8
CHUNK = ROWS // CHUNKS
SLOT = 40
PIECE = 32
TEAM = MEMBERS // 4
TOTALS = 64 * 8

DIFF_S, DIFF_C, FEED, KILL = 0.16, 0.08, 0.035, 0.065


def to(sim, grp):
    return {"sim": sim, "grp": grp}


def laplacian(buf, up, dn, r):
    window = buf[pl.ds(r, 24), :]
    center = window[8:16]
    lane = lax.broadcasted_iota(jnp.int32, (8, COLS), 1)
    left = jnp.where(lane == 0, 0.0, pltpu.roll(center, 1, 1))
    right = jnp.where(lane == COLS - 1, 0.0, pltpu.roll(center, COLS - 1, 1))
    total = up[pl.ds(r, 8), :] + dn[pl.ds(r, 8), :]
    total = total + window[7:15] + window[9:17] + left + right
    return center, total - 6.0 * center


def kernel(
    species, next_out, frame_out,
    sbuf, cbuf, s_up, s_dn, c_up, c_dn, s_new, c_new, edge_cols, sendbuf, recvbuf, totals, pack, parts,
    load_sem, store_sem, halo_send, halo_recv, own_sem, mix_send, mix_recv, part_own, part_send, part_recv,
):
    sim, grp = lax.axis_index("sim"), lax.axis_index("grp")
    plane = sim * GRP + grp
    block, member = lax.div(sim, SUB), lax.rem(sim, SUB)
    seat = member * GRP + grp
    turn = lax.div(block, 4) + lax.rem(block, 4)

    def region_of(m, turn):
        return 2 * lax.rem(lax.div(m, 2) + 8 - turn, 4) + lax.rem(m, 2)

    def member_of(q, turn):
        return 2 * lax.rem(lax.div(q, 2) + turn, 4) + lax.rem(q, 2)

    def first_chunk(sim):
        block = lax.div(sim, SUB)
        place = lax.div(lax.rem(sim, SUB), 2) + 1 + 8 - lax.div(block, 4) - lax.rem(block, 4)
        return 2 * lax.rem(place, 4)

    region = region_of(member, turn)
    team = lax.div(member, 2)

    def source(b):
        t = lax.div(b, 4) + lax.rem(b, 4)
        return b * SUB + member_of(lax.div(sim, REGION), t)

    loads = [
        pltpu.make_async_copy(species.at[i, 0], buf.at[pl.ds(8, ROWS), :], load_sem.at[i])
        for i, buf in ((0, sbuf), (1, cbuf))
    ]
    loads[1].start()
    loads[0].start()

    has_prev, has_next = plane > 0, plane < SIMS * GRP - 1
    prev = to(lax.div(plane - 1, GRP), lax.rem(plane - 1 + GRP, GRP))
    nxt = to(lax.div(plane + 1, GRP), lax.rem(plane + 1, GRP))
    barrier = pltpu.get_barrier_semaphore()

    @pl.when(has_prev)
    def _():
        pl.semaphore_signal(barrier, inc=1, device_id=prev, device_id_type=MESH)

    @pl.when(has_next)
    def _():
        pl.semaphore_signal(barrier, inc=1, device_id=nxt, device_id_type=MESH)

    def greet_member(d, _):
        other = lax.rem(seat + d, MEMBERS)
        there = to(block * SUB + lax.div(other, GRP), lax.rem(other, GRP))
        pl.semaphore_signal(barrier, inc=1, device_id=there, device_id_type=MESH)
        return 0

    lax.fori_loop(1, MEMBERS, greet_member, 0)

    def greet_source(b, _):
        there = source(b)

        @pl.when(there != sim)
        def _():
            pl.semaphore_signal(barrier, inc=1, device_id=to(there, grp), device_id_type=MESH)

        return 0

    lax.fori_loop(0, BLOCKS, greet_source, 0)

    for buf in (sbuf, cbuf):
        buf[0:8, :] = jnp.zeros((8, COLS), jnp.float32)
        buf[ROWS + 8 : ROWS + 16, :] = jnp.zeros((8, COLS), jnp.float32)

    @pl.when(plane == 0)
    def _():
        s_up[...] = jnp.zeros_like(s_up)
        c_up[...] = jnp.zeros_like(c_up)

    @pl.when(plane == SIMS * GRP - 1)
    def _():
        s_dn[...] = jnp.zeros_like(s_dn)
        c_dn[...] = jnp.zeros_like(c_dn)

    self_part = lax.div(sim, REGION) == region
    expected = MEMBERS - 1 + BLOCKS - self_part.astype(jnp.int32)
    expected = expected + has_prev.astype(jnp.int32) + has_next.astype(jnp.int32)
    pl.semaphore_wait(barrier, expected)

    def halo(i, way, rows):
        target = ((s_up, s_dn), (c_up, c_dn))[i][way]
        return lambda chunk: pltpu.make_async_remote_copy(
            src_ref=species.at[i, 0, rows, :],
            dst_ref=target.at[rows, :],
            send_sem=halo_send.at[i, way],
            recv_sem=halo_recv.at[i, way, chunk],
            device_id=(nxt, prev)[way],
            device_id_type=MESH,
        )

    def chunk_rows(k):
        return pl.ds(pl.multiple_of(k * CHUNK, CHUNK), CHUNK)

    whole = pl.ds(0, ROWS)

    first_next, first_prev = first_chunk(nxt["sim"]), first_chunk(prev["sim"])

    def send_catalyst(n, _):
        @pl.when(has_next)
        def _():
            k = lax.rem(first_next + n, CHUNKS)
            halo(1, 0, chunk_rows(k))(k).start()

        @pl.when(has_prev)
        def _():
            k = lax.rem(first_prev + n, CHUNKS)
            halo(1, 1, chunk_rows(k))(k).start()

        return 0

    lax.fori_loop(0, CHUNKS, send_catalyst, 0)
    loads[1].wait()
    loads[0].wait()

    lane = lax.broadcasted_iota(jnp.int32, (8, 128), 1)
    row = lax.broadcasted_iota(jnp.int32, (8, 128), 0)
    beside = [(0, 0), (2, 0), (1, 127), (4, 0), (3, 127), (6, 0), (5, 127), (7, 127)]

    def mix(k, x, start, length):
        m = member_of(k, turn)
        source_rows = pl.ds(pl.multiple_of((k * GRP + x) * SLOT + start, 8), length)
        target_rows = pl.ds(pl.multiple_of(seat * SLOT + start, 8), length)
        away = pltpu.make_async_remote_copy(
            src_ref=sendbuf.at[source_rows, :],
            dst_ref=recvbuf.at[target_rows, :],
            send_sem=mix_send,
            recv_sem=mix_recv.at[team],
            device_id=to(block * SUB + m, x),
            device_id_type=MESH,
        )
        here = pltpu.make_async_copy(sendbuf.at[source_rows, :], recvbuf.at[target_rows, :], own_sem)
        return away, here, m * GRP + x == seat

    def send_tiles(k, start, length):
        for dx in range(1, GRP + 1):
            away, here, stays = mix(k, lax.rem(grp + dx, GRP), start, length)

            @pl.when(stays)
            def _(here=here):
                here.start()

            @pl.when(jnp.logical_not(stays))
            def _(away=away):
                away.start()

    def send_rim(k):
        top = c_new[pl.ds(pl.multiple_of(jnp.maximum(k * REGION - 8, 0), 8), 8), :]
        bottom = c_new[pl.ds(pl.multiple_of(jnp.minimum(k * REGION + REGION, ROWS - 8), 8), 8), :]
        above = jnp.where(k == 0, top[0:1], top[7:8])
        below = jnp.where(k == SUB - 1, bottom[7:8], bottom[0:1])
        window = edge_cols[pl.ds(pl.multiple_of(k * REGION, 8), 32), :]
        window = jnp.concatenate([window, jnp.zeros((96, 128), jnp.float32)], axis=0)
        cols = pltpu.roll(jnp.transpose(window)[0:8], 121, 1)
        for x in range(GRP):
            c = 2 * x * 128
            tile = pltpu.roll(cols, (4 - 2 * x) % 8, 0)
            tile = jnp.where(row == 0, above[:, c : c + 128], tile)
            tile = jnp.where(row == 1, above[:, c + 128 : c + 256], tile)
            tile = jnp.where(row == 2, below[:, c : c + 128], tile)
            tile = jnp.where(row == 3, below[:, c + 128 : c + 256], tile)
            sendbuf[pl.ds(pl.multiple_of((k * GRP + x) * SLOT + 32, 8), 8), :] = tile
        send_tiles(k, 32, 8)

    first = first_chunk(sim)

    def catalyst_chunk(n, _):
        k = lax.rem(first + n, CHUNKS)

        @pl.when(has_prev)
        def _():
            halo(1, 0, chunk_rows(k))(k).wait_recv()

        @pl.when(has_next)
        def _():
            halo(1, 1, chunk_rows(k))(k).wait_recv()

        for h in range(CHUNK // 8):
            r = pl.multiple_of(k * CHUNK + 8 * h, 8)
            c, lap = laplacian(cbuf, c_up, c_dn, r)
            s = sbuf[pl.ds(pl.multiple_of(r + 8, 8), 8), :]
            new = c + DIFF_C * lap + s * c * c - (FEED + KILL) * c
            c_new[pl.ds(r, 8), :] = new
            columns = jnp.zeros((8, 128), jnp.float32)
            for i, (tile, at) in enumerate(beside):
                moved = pltpu.roll(new[:, tile * 128 : tile * 128 + 128], (i - at) % 128, 1)
                columns = jnp.where(lane == i, moved, columns)
            edge_cols[pl.ds(pl.multiple_of(r + 8, 8), 8), :] = columns
            if h == 0:
                @pl.when(k == 0)
                def _(columns=columns):
                    edge_cols[0:8, :] = jnp.broadcast_to(columns[0:1], (8, 128))
            else:
                @pl.when(k == CHUNKS - 1)
                def _(columns=columns):
                    edge_cols[ROWS + 8 : ROWS + 16, :] = jnp.broadcast_to(columns[7:8], (8, 128))
            for tile in range(COLS // 128):
                slot = (k * GRP + tile // 2) * SLOT + (h * 2 + tile % 2) * 8
                sendbuf[pl.ds(pl.multiple_of(slot, 8), 8), :] = new[:, tile * 128 : tile * 128 + 128]

        send_tiles(k, 0, 32)

        @pl.when(n >= 2)
        def _():
            send_rim(lax.rem(first + n - 1, CHUNKS))

        return 0

    lax.fori_loop(0, CHUNKS, catalyst_chunk, 0)
    last_rims = lambda n, _: (send_rim(lax.rem(first + CHUNKS - 1 + n, CHUNKS)), 0)[1]
    lax.fori_loop(0, 2, last_rims, 0)

    store_c = pltpu.make_async_copy(c_new, next_out.at[1, 0], store_sem.at[1])
    store_c.start()

    @pl.when(has_next)
    def _():
        halo(0, 0, whole)(0).start()

    @pl.when(has_prev)
    def _():
        halo(0, 1, whole)(0).start()

    def wait_mixed(count, t):
        some = pl.ds(0, count * SLOT)
        return pltpu.make_async_remote_copy(
            src_ref=sendbuf.at[some, :], dst_ref=recvbuf.at[some, :],
            send_sem=mix_send, recv_sem=mix_recv.at[t], device_id=to(sim, grp), device_id_type=MESH,
        )

    extinct = 6.0 / (BLOCKS * MEMBERS)
    log2e = math.log2(math.e)
    thin, narrow = -extinct * log2e / 256.0, -8.0 * log2e / 256.0

    def render(i, _):
        t_now = lax.rem(team + 6 - i, 4)

        @pl.when(t_now == team)
        def _():
            one_slot = pl.ds(0, SLOT)
            pltpu.make_async_copy(sendbuf.at[one_slot, :], recvbuf.at[one_slot, :], own_sem).wait()
            wait_mixed(TEAM - 1, team).wait_recv()

        @pl.when(t_now != team)
        def _():
            wait_mixed(TEAM, t_now).wait_recv()

        base = t_now * (TEAM * SLOT)
        sides = jnp.concatenate(
            [
                recvbuf[pl.ds(base + 36, TEAM, stride=SLOT), :],
                recvbuf[pl.ds(base + 37, TEAM, stride=SLOT), :],
                jnp.zeros((128 - 2 * TEAM, 128), jnp.float32),
            ],
            axis=0,
        )
        sides = jnp.transpose(sides)

        for h in range(2):
            for par in range(2):
                near = 2 * par + 8 * h
                side = 3.0 * sides[1 + 8 * h : 9 + 8 * h] + sides[near : near + 8]

                def layer(p, sums, h=h, par=par, side=side):
                    at = pl.multiple_of(base + p * SLOT, 8)
                    rim = recvbuf[pl.ds(at + 32, 8), :]
                    rows = []
                    for t in range(2):
                        mine = recvbuf[pl.ds(at + (2 * h + t) * 8, 8), :]
                        across = recvbuf[pl.ds(at + (2 - 2 * h + t) * 8, 8), :]
                        if par == 0:
                            beyond = rim[t : t + 1] if h == 0 else across[7:8]
                            shifted = jnp.where(row == 0, beyond, pltpu.roll(mine, 1, 0))
                        else:
                            beyond = rim[2 + t : 3 + t] if h == 1 else across[0:1]
                            shifted = jnp.where(row == 7, beyond, pltpu.roll(mine, 7, 0))
                        rows.append(3.0 * mine + shifted)
                    leftmost = pltpu.roll(side, lax.rem(128 - p, 128), 1)
                    rightmost = pltpu.roll(side, 127 - TEAM - p, 1)
                    fwd = [pltpu.roll(v, 1, 1) for v in rows]
                    bwd = [pltpu.roll(v, 127, 1) for v in rows]
                    low = [jnp.where(lane == 0, leftmost, fwd[0]), jnp.where(lane == 0, fwd[0], fwd[1])]
                    high = [jnp.where(lane == 127, bwd[1], bwd[0]), jnp.where(lane == 127, rightmost, bwd[1])]
                    result = []
                    for cpar in range(2):
                        for t in range(2):
                            q = 3.0 * rows[t] + (low, high)[cpar][t]
                            red, green, blue, clear = sums[(cpar * 2 + t) * 4 : (cpar * 2 + t) * 4 + 4]
                            after = clear * jnp.exp2((q * q) * thin)
                            weight = clear - after
                            mid = q - 8.0
                            warm = mid * (3.0 / 16.0)
                            red = red + weight * jnp.tanh(warm)
                            green = green + weight * jnp.exp2((mid * mid) * narrow)
                            blue = blue + weight * jnp.tanh(warm + 0.6)
                            result += [red, green, blue, after]
                    return tuple(result)

                zero, one = jnp.zeros((8, 128), jnp.float32), jnp.ones((8, 128), jnp.float32)
                sums = lax.fori_loop(0, TEAM, layer, (zero, zero, zero, one) * 4, unroll=True)
                for j in range(16):
                    at = t_now * TOTALS + ((h * 2 + par) * 16 + j) * 8
                    totals[pl.ds(pl.multiple_of(at, 8), 8), :] = sums[j]
        return 0

    lax.fori_loop(0, 4, render, 0)

    for h in range(2):
        for par in range(2):
            for cpar in range(2):
                for t in range(2):
                    base = ((h * 2 + par) * 16 + (cpar * 2 + t) * 4) * 8
                    got = [[totals[i * TOTALS + base + 8 * ch : i * TOTALS + base + 8 * ch + 8, :] for ch in range(4)] for i in range(4)]
                    red, green, blue, clear = got[0]
                    for i in range(1, 4):
                        red = red + clear * got[i][0]
                        green = green + clear * got[i][1]
                        blue = blue + clear * got[i][2]
                        clear = clear * got[i][3]
                    for ch, value in enumerate((red, green, blue, clear)):
                        at = 8 * h * PIECE + ch * 8 + cpar * 4 + par * 2 + t
                        pack[pl.ds(at, 8, stride=PIECE), :] = value

    def piece_rows(n):
        return pl.ds(pl.multiple_of(n * PIECE, PIECE), PIECE)

    def send_piece(n, _):
        j = lax.rem(n + sim, REGION)
        there = region * REGION + j

        @pl.when(there != sim)
        def _():
            pltpu.make_async_remote_copy(
                src_ref=pack.at[piece_rows(j), :],
                dst_ref=parts.at[piece_rows(block), :],
                send_sem=part_send,
                recv_sem=part_recv,
                device_id=to(there, grp),
                device_id_type=MESH,
            ).start()

        return 0

    lax.fori_loop(0, REGION, send_piece, 0)

    @pl.when(self_part)
    def _():
        mine = pltpu.make_async_copy(
            pack.at[piece_rows(lax.rem(sim, REGION)), :], parts.at[piece_rows(block), :], part_own
        )
        mine.start()
        mine.wait()

    @pl.when(has_prev)
    def _():
        halo(0, 0, whole)(0).wait_recv()

    @pl.when(has_next)
    def _():
        halo(0, 1, whole)(0).wait_recv()

    def substrate_rows(k, _):
        r = pl.multiple_of(8 * k, 8)
        s, lap = laplacian(sbuf, s_up, s_dn, r)
        c = cbuf[pl.ds(pl.multiple_of(r + 8, 8), 8), :]
        s_new[pl.ds(r, 8), :] = s + DIFF_S * lap - s * c * c + FEED * (1.0 - s)
        return 0

    lax.fori_loop(0, ROWS // 8, substrate_rows, 0, unroll=4)
    store_s = pltpu.make_async_copy(s_new, next_out.at[0, 0], store_sem.at[0])
    store_s.start()

    def wait_parts(count):
        some = pl.ds(0, count * PIECE)
        return pltpu.make_async_remote_copy(
            src_ref=pack.at[some, :], dst_ref=parts.at[some, :],
            send_sem=part_send, recv_sem=part_recv, device_id=to(sim, grp), device_id_type=MESH,
        )

    @pl.when(self_part)
    def _():
        wait_parts(BLOCKS - 1).wait_recv()

    @pl.when(jnp.logical_not(self_part))
    def _():
        wait_parts(BLOCKS).wait_recv()

    def add_block(b, totals):
        base = pl.multiple_of(b * PIECE, 8)
        red, green, blue, clear = totals
        got = [parts[pl.ds(base + 8 * ch, 8), :] for ch in range(4)]
        return (
            red + clear * got[0], green + clear * got[1], blue + clear * got[2], clear * got[3],
        )

    zero, one = jnp.zeros((8, 128), jnp.float32), jnp.ones((8, 128), jnp.float32)
    red, green, blue, clear = lax.fori_loop(0, BLOCKS, add_block, (zero, zero, zero, one), unroll=True)
    opaque = 1.0 - clear
    channels = [0.5 * (opaque + red), green, 0.5 * (opaque - blue), opaque]
    flat = jnp.concatenate([jnp.concatenate([v[0:4], v[4:8]], axis=1) for v in channels], axis=0)
    old = lax.broadcasted_iota(jnp.int32, (256, 256), 0)
    new = lax.broadcasted_iota(jnp.int32, (256, 256), 1)
    spread = jnp.where(new == 2 * lax.rem(old, 128) + lax.div(old, 128), 1.0, 0.0)
    mixed = jnp.dot(flat, spread, precision=lax.Precision.HIGHEST, preferred_element_type=jnp.float32)
    for ch in range(4):
        for par in range(2):
            for t in range(2):
                n = ch * 4 + par * 2 + t
                frame_out[ch, par : par + 1, t * 256 : t * 256 + 256] = mixed[n : n + 1]

    for i in range(2):
        @pl.when(has_next)
        def _(i=i):
            halo(i, 0, whole)(0).wait_send()

        @pl.when(has_prev)
        def _(i=i):
            halo(i, 1, whole)(0).wait_send()

    wait_mixed(MEMBERS - 1, team).wait_send()

    @pl.when(self_part)
    def _():
        wait_parts(BLOCKS - 1).wait_send()

    @pl.when(jnp.logical_not(self_part))
    def _():
        wait_parts(BLOCKS).wait_send()

    store_c.wait()
    store_s.wait()


def shards(species):
    f32 = jnp.float32
    plane = pltpu.VMEM((ROWS, COLS), f32)
    padded = pltpu.VMEM((ROWS + 16, COLS), f32)
    dma = pltpu.SemaphoreType.DMA
    fresh, frame = pl.pallas_call(
        kernel,
        out_shape=(
            jax.ShapeDtypeStruct((2, 1, ROWS, COLS), f32),
            jax.ShapeDtypeStruct((4, 2 * ROWS // SIMS, 2 * COLS // GRP), f32),
        ),
        in_specs=[pl.BlockSpec(memory_space=pltpu.HBM)],
        out_specs=(pl.BlockSpec(memory_space=pl.ANY), pl.BlockSpec(memory_space=pltpu.VMEM)),
        scratch_shapes=[
            padded, padded, plane, plane, plane, plane,
            plane, plane,
            pltpu.VMEM((ROWS + 16, 128), f32),
            pltpu.VMEM((MEMBERS * SLOT, 128), f32),
            pltpu.VMEM((MEMBERS * SLOT, 128), f32),
            pltpu.VMEM((4 * TOTALS, 128), f32),
            pltpu.VMEM((REGION * PIECE, 128), f32),
            pltpu.VMEM((BLOCKS * PIECE, 128), f32),
            dma((2,)), dma((2,)), dma((2, 2)), dma((2, 2, CHUNKS)),
            dma, dma, dma((4,)), dma, dma, dma,
        ],
        compiler_params=pltpu.CompilerParams(
            collective_id=0, has_side_effects=True, vmem_limit_bytes=32 * 1024 * 1024
        ),
        cost_estimate=pl.CostEstimate(flops=20_000_000, bytes_accessed=4_000_000, transcendentals=2_000_000),
    )(species)
    return fresh, frame


def solution(mesh):
    return jax.shard_map(
        shards,
        mesh=mesh,
        in_specs=(P(None, ("sim", "grp"), None, None),),
        out_specs=(P(None, ("sim", "grp"), None, None), P(None, "sim", "grp")),
        check_vma=False,
    )
```

```python
import math

import jax
import jax.numpy as jnp
from jax import lax
from jax.experimental import pallas as pl
from jax.experimental.pallas import tpu as pltpu
from jax.sharding import PartitionSpec as P

MESH = pl.DeviceIdType.MESH

ROWS = 128
COLS = 1024
GRP = 4
SIMS = 128
SUB = 8
BLOCKS = SIMS // SUB
MEMBERS = GRP * SUB
REGION = ROWS // SUB
CHUNKS = 8
CHUNK = ROWS // CHUNKS
SLOT = 40
PIECE = 32
TEAM = MEMBERS // 4
TOTALS = 64 * 8

DIFF_S, DIFF_C, FEED, KILL = 0.16, 0.08, 0.035, 0.065


def to(sim, grp):
    return {"sim": sim, "grp": grp}


def laplacian(buf, up, dn, r):
    window = buf[pl.ds(r, 24), :]
    center = window[8:16]
    lane = lax.broadcasted_iota(jnp.int32, (8, COLS), 1)
    left = jnp.where(lane == 0, 0.0, pltpu.roll(center, 1, 1))
    right = jnp.where(lane == COLS - 1, 0.0, pltpu.roll(center, COLS - 1, 1))
    total = up[pl.ds(r, 8), :] + dn[pl.ds(r, 8), :]
    total = total + window[7:15] + window[9:17] + left + right
    return center, total - 6.0 * center


def kernel(
    species, next_out, frame_out,
    sbuf, cbuf, s_up, s_dn, c_up, c_dn, rs_up, rs_dn, rc_up, rc_dn, s_new, c_new, edge_cols, sendbuf, recvbuf, totals, pack, parts,
    load_sem, store_sem, halo_send, halo_recv, relay_send, relay_recv, own_sem, mix_send, mix_recv, part_own, part_send, part_recv,
):
    sim, grp = lax.axis_index("sim"), lax.axis_index("grp")
    plane = sim * GRP + grp
    block, member = lax.div(sim, SUB), lax.rem(sim, SUB)
    seat = member * GRP + grp
    turn = lax.div(block, 4) + lax.rem(block, 4)

    def region_of(m, turn):
        return 2 * lax.rem(lax.div(m, 2) + 8 - turn, 4) + lax.rem(m, 2)

    def member_of(q, turn):
        return 2 * lax.rem(lax.div(q, 2) + turn, 4) + lax.rem(q, 2)

    def first_chunk(sim):
        block = lax.div(sim, SUB)
        place = lax.div(lax.rem(sim, SUB), 2) + 1 + 8 - lax.div(block, 4) - lax.rem(block, 4)
        return 2 * lax.rem(place, 4)

    region = region_of(member, turn)
    team = lax.div(member, 2)

    def source(b):
        t = lax.div(b, 4) + lax.rem(b, 4)
        return b * SUB + member_of(lax.div(sim, REGION), t)

    loads = [
        pltpu.make_async_copy(species.at[i, 0], buf.at[pl.ds(8, ROWS), :], load_sem.at[i])
        for i, buf in ((0, sbuf), (1, cbuf))
    ]
    loads[1].start()
    loads[0].start()

    has_prev, has_next = plane > 0, plane < SIMS * GRP - 1
    prev = to(lax.div(plane - 1, GRP), lax.rem(plane - 1 + GRP, GRP))
    nxt = to(lax.div(plane + 1, GRP), lax.rem(plane + 1, GRP))

    odd = lax.rem(sim, 2)
    sim_a = sim + odd - 1
    sim_b = sim_a + 1
    edge = ((grp == 0) | (grp == GRP - 1)) & (sim_a >= 0) & (sim_b < SIMS)
    is_a = edge & (odd == 1) & (grp == GRP - 1)
    is_b = edge & (odd == 0) & (grp == 0)
    is_relay = edge & jnp.logical_not(is_a | is_b)
    relays = (to(sim_a, 0), to(sim_b, GRP - 1))
    ends = (to(sim_b, 0), to(sim_a, GRP - 1))
    my_half = lax.div(grp, GRP - 1)
    straight_next = has_next & jnp.logical_not(is_a)
    straight_prev = has_prev & jnp.logical_not(is_b)
    barrier = pltpu.get_barrier_semaphore()
    for wanted, other in (
        (straight_prev, prev), (straight_next, nxt), (edge, to(sim_a + sim_b - sim, grp)),
    ):
        @pl.when(wanted)
        def _(other=other):
            pl.semaphore_signal(barrier, inc=1, device_id=other, device_id_type=MESH)

    def greet_member(d, _):
        other = lax.rem(seat + d, MEMBERS)
        there = to(block * SUB + lax.div(other, GRP), lax.rem(other, GRP))
        pl.semaphore_signal(barrier, inc=1, device_id=there, device_id_type=MESH)
        return 0

    lax.fori_loop(1, MEMBERS, greet_member, 0)

    def greet_source(b, _):
        there = source(b)

        @pl.when(there != sim)
        def _():
            pl.semaphore_signal(barrier, inc=1, device_id=to(there, grp), device_id_type=MESH)

        return 0

    lax.fori_loop(0, BLOCKS, greet_source, 0)

    for buf in (sbuf, cbuf):
        buf[0:8, :] = jnp.zeros((8, COLS), jnp.float32)
        buf[ROWS + 8 : ROWS + 16, :] = jnp.zeros((8, COLS), jnp.float32)

    @pl.when(plane == 0)
    def _():
        s_up[...] = jnp.zeros_like(s_up)
        c_up[...] = jnp.zeros_like(c_up)

    @pl.when(plane == SIMS * GRP - 1)
    def _():
        s_dn[...] = jnp.zeros_like(s_dn)
        c_dn[...] = jnp.zeros_like(c_dn)

    self_part = lax.div(sim, REGION) == region
    expected = MEMBERS - 1 + BLOCKS - self_part.astype(jnp.int32)
    for wanted in (straight_prev, straight_next, edge):
        expected = expected + wanted.astype(jnp.int32)
    pl.semaphore_wait(barrier, expected)

    targets, passing = ((s_up, s_dn), (c_up, c_dn)), ((rs_up, rs_dn), (rc_up, rc_dn))

    def halo(i, way, rows):
        return lambda chunk: pltpu.make_async_remote_copy(
            src_ref=species.at[i, 0, rows, :],
            dst_ref=targets[i][way].at[rows, :],
            send_sem=halo_send.at[i, way],
            recv_sem=halo_recv.at[i, way, chunk],
            device_id=(nxt, prev)[way],
            device_id_type=MESH,
        )

    def to_relay(i, way, rows, there, chunk, half):
        return pltpu.make_async_remote_copy(
            src_ref=species.at[i, 0, rows, :],
            dst_ref=passing[i][way].at[there, :],
            send_sem=halo_send.at[i, way],
            recv_sem=relay_recv.at[i, way, chunk],
            device_id=relays[half],
            device_id_type=MESH,
        )

    def from_relay(i, way, rows, there, chunk):
        return pltpu.make_async_remote_copy(
            src_ref=passing[i][way].at[rows, :],
            dst_ref=targets[i][way].at[there, :],
            send_sem=relay_send.at[i, way],
            recv_sem=halo_recv.at[i, way, chunk],
            device_id=ends[way],
            device_id_type=MESH,
        )

    def chunk_rows(k):
        return pl.ds(pl.multiple_of(k * CHUNK, CHUNK), CHUNK)

    def half_chunk(k, half):
        return pl.ds(pl.multiple_of(k * CHUNK + half * 8, 8), 8)

    def relay_rows(k):
        return pl.ds(pl.multiple_of(k * 8, 8), 8)

    whole = pl.ds(0, ROWS)
    half_rows = (pl.ds(0, ROWS // 2), pl.ds(ROWS // 2, ROWS // 2))
    firsts = (first_chunk(nxt["sim"]), first_chunk(prev["sim"]))

    def send_catalyst(n, _):
        for way, straight, end in ((0, straight_next, is_a), (1, straight_prev, is_b)):
            k = lax.rem(firsts[way] + n, CHUNKS)

            @pl.when(straight)
            def _(way=way, k=k):
                halo(1, way, chunk_rows(k))(k).start()

            @pl.when(end)
            def _(way=way, k=k):
                for half in range(2):
                    to_relay(1, way, half_chunk(k, half), relay_rows(k), k, half).start()

        return 0

    def pass_catalyst(n):
        for way in range(2):
            k = lax.rem(first_chunk((sim_b, sim_a)[way]) + n, CHUNKS)
            to_relay(1, way, half_chunk(k, 0), relay_rows(k), k, 0).wait_recv()
            from_relay(1, way, relay_rows(k), half_chunk(k, my_half), k).start()

    ahead = CHUNKS // 2
    lax.fori_loop(0, ahead, send_catalyst, 0)

    def send_substrate(early):
        for way, end in ((0, is_a), (1, is_b)):
            half = 1 - way if early else way

            @pl.when(end)
            def _(way=way, half=half):
                to_relay(0, way, half_rows[half], half_rows[0], 0, half).start()

    send_substrate(True)
    loads[1].wait()
    loads[0].wait()

    lane = lax.broadcasted_iota(jnp.int32, (8, 128), 1)
    row = lax.broadcasted_iota(jnp.int32, (8, 128), 0)
    beside = [(0, 0), (2, 0), (1, 127), (4, 0), (3, 127), (6, 0), (5, 127), (7, 127)]

    def mix(k, x, start, length):
        m = member_of(k, turn)
        source_rows = pl.ds(pl.multiple_of((k * GRP + x) * SLOT + start, 8), length)
        target_rows = pl.ds(pl.multiple_of(seat * SLOT + start, 8), length)
        away = pltpu.make_async_remote_copy(
            src_ref=sendbuf.at[source_rows, :],
            dst_ref=recvbuf.at[target_rows, :],
            send_sem=mix_send,
            recv_sem=mix_recv.at[team],
            device_id=to(block * SUB + m, x),
            device_id_type=MESH,
        )
        here = pltpu.make_async_copy(sendbuf.at[source_rows, :], recvbuf.at[target_rows, :], own_sem)
        return away, here, m * GRP + x == seat

    def send_tiles(k, start, length):
        for dx in range(1, GRP + 1):
            away, here, stays = mix(k, lax.rem(grp + dx, GRP), start, length)

            @pl.when(stays)
            def _(here=here):
                here.start()

            @pl.when(jnp.logical_not(stays))
            def _(away=away):
                away.start()

    def send_rim(k):
        top = c_new[pl.ds(pl.multiple_of(jnp.maximum(k * REGION - 8, 0), 8), 8), :]
        bottom = c_new[pl.ds(pl.multiple_of(jnp.minimum(k * REGION + REGION, ROWS - 8), 8), 8), :]
        above = jnp.where(k == 0, top[0:1], top[7:8])
        below = jnp.where(k == SUB - 1, bottom[7:8], bottom[0:1])
        window = edge_cols[pl.ds(pl.multiple_of(k * REGION, 8), 32), :]
        window = jnp.concatenate([window, jnp.zeros((96, 128), jnp.float32)], axis=0)
        cols = pltpu.roll(jnp.transpose(window)[0:8], 121, 1)
        for x in range(GRP):
            c = 2 * x * 128
            tile = pltpu.roll(cols, (4 - 2 * x) % 8, 0)
            tile = jnp.where(row == 0, above[:, c : c + 128], tile)
            tile = jnp.where(row == 1, above[:, c + 128 : c + 256], tile)
            tile = jnp.where(row == 2, below[:, c : c + 128], tile)
            tile = jnp.where(row == 3, below[:, c + 128 : c + 256], tile)
            sendbuf[pl.ds(pl.multiple_of((k * GRP + x) * SLOT + 32, 8), 8), :] = tile
        send_tiles(k, 32, 8)

    first = first_chunk(sim)

    def catalyst_chunk(n, _):
        k = lax.rem(first + n, CHUNKS)

        @pl.when(n < CHUNKS - ahead)
        def _():
            send_catalyst(n + ahead, 0)

        @pl.when(is_relay)
        def _():
            pass_catalyst(n)

        @pl.when(has_prev)
        def _():
            halo(1, 0, chunk_rows(k))(k).wait_recv()

        @pl.when(has_next)
        def _():
            halo(1, 1, chunk_rows(k))(k).wait_recv()

        for h in range(CHUNK // 8):
            r = pl.multiple_of(k * CHUNK + 8 * h, 8)
            c, lap = laplacian(cbuf, c_up, c_dn, r)
            s = sbuf[pl.ds(pl.multiple_of(r + 8, 8), 8), :]
            new = c + DIFF_C * lap + s * c * c - (FEED + KILL) * c
            c_new[pl.ds(r, 8), :] = new
            columns = jnp.zeros((8, 128), jnp.float32)
            for i, (tile, at) in enumerate(beside):
                moved = pltpu.roll(new[:, tile * 128 : tile * 128 + 128], (i - at) % 128, 1)
                columns = jnp.where(lane == i, moved, columns)
            edge_cols[pl.ds(pl.multiple_of(r + 8, 8), 8), :] = columns
            if h == 0:
                @pl.when(k == 0)
                def _(columns=columns):
                    edge_cols[0:8, :] = jnp.broadcast_to(columns[0:1], (8, 128))
            else:
                @pl.when(k == CHUNKS - 1)
                def _(columns=columns):
                    edge_cols[ROWS + 8 : ROWS + 16, :] = jnp.broadcast_to(columns[7:8], (8, 128))
            for tile in range(COLS // 128):
                slot = (k * GRP + tile // 2) * SLOT + (h * 2 + tile % 2) * 8
                sendbuf[pl.ds(pl.multiple_of(slot, 8), 8), :] = new[:, tile * 128 : tile * 128 + 128]

        send_tiles(k, 0, 32)

        @pl.when(n >= 2)
        def _():
            send_rim(lax.rem(first + n - 1, CHUNKS))

        return 0

    lax.fori_loop(0, CHUNKS, catalyst_chunk, 0)
    last_rims = lambda n, _: (send_rim(lax.rem(first + CHUNKS - 1 + n, CHUNKS)), 0)[1]
    lax.fori_loop(0, 2, last_rims, 0)

    store_c = pltpu.make_async_copy(c_new, next_out.at[1, 0], store_sem.at[1])
    store_c.start()

    @pl.when(straight_next)
    def _():
        halo(0, 0, whole)(0).start()

    @pl.when(straight_prev)
    def _():
        halo(0, 1, whole)(0).start()

    send_substrate(False)

    def wait_mixed(count, t):
        some = pl.ds(0, count * SLOT)
        return pltpu.make_async_remote_copy(
            src_ref=sendbuf.at[some, :], dst_ref=recvbuf.at[some, :],
            send_sem=mix_send, recv_sem=mix_recv.at[t], device_id=to(sim, grp), device_id_type=MESH,
        )

    extinct = 6.0 / (BLOCKS * MEMBERS)
    log2e = math.log2(math.e)
    thin, narrow = -extinct * log2e / 256.0, -8.0 * log2e / 256.0

    def render(i, _):
        t_now = lax.rem(team + 6 - i, 4)

        @pl.when(t_now == team)
        def _():
            one_slot = pl.ds(0, SLOT)
            pltpu.make_async_copy(sendbuf.at[one_slot, :], recvbuf.at[one_slot, :], own_sem).wait()
            wait_mixed(TEAM - 1, team).wait_recv()

        @pl.when(t_now != team)
        def _():
            wait_mixed(TEAM, t_now).wait_recv()

        base = t_now * (TEAM * SLOT)
        sides = jnp.concatenate(
            [
                recvbuf[pl.ds(base + 36, TEAM, stride=SLOT), :],
                recvbuf[pl.ds(base + 37, TEAM, stride=SLOT), :],
                jnp.zeros((128 - 2 * TEAM, 128), jnp.float32),
            ],
            axis=0,
        )
        sides = jnp.transpose(sides)

        for h in range(2):
            for par in range(2):
                near = 2 * par + 8 * h
                side = 3.0 * sides[1 + 8 * h : 9 + 8 * h] + sides[near : near + 8]

                def layer(p, sums, h=h, par=par, side=side):
                    at = pl.multiple_of(base + p * SLOT, 8)
                    rim = recvbuf[pl.ds(at + 32, 8), :]
                    rows = []
                    for t in range(2):
                        mine = recvbuf[pl.ds(at + (2 * h + t) * 8, 8), :]
                        across = recvbuf[pl.ds(at + (2 - 2 * h + t) * 8, 8), :]
                        if par == 0:
                            beyond = rim[t : t + 1] if h == 0 else across[7:8]
                            shifted = jnp.where(row == 0, beyond, pltpu.roll(mine, 1, 0))
                        else:
                            beyond = rim[2 + t : 3 + t] if h == 1 else across[0:1]
                            shifted = jnp.where(row == 7, beyond, pltpu.roll(mine, 7, 0))
                        rows.append(3.0 * mine + shifted)
                    leftmost = pltpu.roll(side, lax.rem(128 - p, 128), 1)
                    rightmost = pltpu.roll(side, 127 - TEAM - p, 1)
                    fwd = [pltpu.roll(v, 1, 1) for v in rows]
                    bwd = [pltpu.roll(v, 127, 1) for v in rows]
                    low = [jnp.where(lane == 0, leftmost, fwd[0]), jnp.where(lane == 0, fwd[0], fwd[1])]
                    high = [jnp.where(lane == 127, bwd[1], bwd[0]), jnp.where(lane == 127, rightmost, bwd[1])]
                    result = []
                    for cpar in range(2):
                        for t in range(2):
                            q = 3.0 * rows[t] + (low, high)[cpar][t]
                            red, green, blue, clear = sums[(cpar * 2 + t) * 4 : (cpar * 2 + t) * 4 + 4]
                            after = clear * jnp.exp2((q * q) * thin)
                            weight = clear - after
                            mid = q - 8.0
                            warm = mid * (3.0 / 16.0)
                            red = red + weight * jnp.tanh(warm)
                            green = green + weight * jnp.exp2((mid * mid) * narrow)
                            blue = blue + weight * jnp.tanh(warm + 0.6)
                            result += [red, green, blue, after]
                    return tuple(result)

                zero, one = jnp.zeros((8, 128), jnp.float32), jnp.ones((8, 128), jnp.float32)
                sums = lax.fori_loop(0, TEAM, layer, (zero, zero, zero, one) * 4, unroll=True)
                for j in range(16):
                    at = t_now * TOTALS + ((h * 2 + par) * 16 + j) * 8
                    totals[pl.ds(pl.multiple_of(at, 8), 8), :] = sums[j]
        return 0

    lax.fori_loop(0, 4, render, 0)

    for h in range(2):
        for par in range(2):
            for cpar in range(2):
                for t in range(2):
                    base = ((h * 2 + par) * 16 + (cpar * 2 + t) * 4) * 8
                    got = [[totals[i * TOTALS + base + 8 * ch : i * TOTALS + base + 8 * ch + 8, :] for ch in range(4)] for i in range(4)]
                    red, green, blue, clear = got[0]
                    for i in range(1, 4):
                        red = red + clear * got[i][0]
                        green = green + clear * got[i][1]
                        blue = blue + clear * got[i][2]
                        clear = clear * got[i][3]
                    for ch, value in enumerate((red, green, blue, clear)):
                        at = 8 * h * PIECE + ch * 8 + cpar * 4 + par * 2 + t
                        pack[pl.ds(at, 8, stride=PIECE), :] = value

    def piece_rows(n):
        return pl.ds(pl.multiple_of(n * PIECE, PIECE), PIECE)

    def send_piece(n, _):
        j = lax.rem(n + sim, REGION)
        there = region * REGION + j

        @pl.when(there != sim)
        def _():
            pltpu.make_async_remote_copy(
                src_ref=pack.at[piece_rows(j), :],
                dst_ref=parts.at[piece_rows(block), :],
                send_sem=part_send,
                recv_sem=part_recv,
                device_id=to(there, grp),
                device_id_type=MESH,
            ).start()

        return 0

    lax.fori_loop(0, REGION, send_piece, 0)

    @pl.when(self_part)
    def _():
        mine = pltpu.make_async_copy(
            pack.at[piece_rows(lax.rem(sim, REGION)), :], parts.at[piece_rows(block), :], part_own
        )
        mine.start()
        mine.wait()

    @pl.when(is_relay)
    def _():
        for way in range(2):
            to_relay(0, way, half_rows[0], half_rows[0], 0, 0).wait_recv()
            there = pl.ds(pl.multiple_of(my_half * (ROWS // 2), 8), ROWS // 2)
            from_relay(0, way, half_rows[0], there, 0).start()

    @pl.when(has_prev)
    def _():
        halo(0, 0, whole)(0).wait_recv()

    @pl.when(has_next)
    def _():
        halo(0, 1, whole)(0).wait_recv()

    def substrate_rows(k, _):
        r = pl.multiple_of(8 * k, 8)
        s, lap = laplacian(sbuf, s_up, s_dn, r)
        c = cbuf[pl.ds(pl.multiple_of(r + 8, 8), 8), :]
        s_new[pl.ds(r, 8), :] = s + DIFF_S * lap - s * c * c + FEED * (1.0 - s)
        return 0

    lax.fori_loop(0, ROWS // 8, substrate_rows, 0, unroll=4)
    store_s = pltpu.make_async_copy(s_new, next_out.at[0, 0], store_sem.at[0])
    store_s.start()

    def wait_parts(count):
        some = pl.ds(0, count * PIECE)
        return pltpu.make_async_remote_copy(
            src_ref=pack.at[some, :], dst_ref=parts.at[some, :],
            send_sem=part_send, recv_sem=part_recv, device_id=to(sim, grp), device_id_type=MESH,
        )

    @pl.when(self_part)
    def _():
        wait_parts(BLOCKS - 1).wait_recv()

    @pl.when(jnp.logical_not(self_part))
    def _():
        wait_parts(BLOCKS).wait_recv()

    def add_block(b, totals):
        base = pl.multiple_of(b * PIECE, 8)
        red, green, blue, clear = totals
        got = [parts[pl.ds(base + 8 * ch, 8), :] for ch in range(4)]
        return (
            red + clear * got[0], green + clear * got[1], blue + clear * got[2], clear * got[3],
        )

    zero, one = jnp.zeros((8, 128), jnp.float32), jnp.ones((8, 128), jnp.float32)
    red, green, blue, clear = lax.fori_loop(0, BLOCKS, add_block, (zero, zero, zero, one), unroll=True)
    opaque = 1.0 - clear
    channels = [0.5 * (opaque + red), green, 0.5 * (opaque - blue), opaque]
    flat = jnp.concatenate([jnp.concatenate([v[0:4], v[4:8]], axis=1) for v in channels], axis=0)
    old = lax.broadcasted_iota(jnp.int32, (256, 256), 0)
    new = lax.broadcasted_iota(jnp.int32, (256, 256), 1)
    spread = jnp.where(new == 2 * lax.rem(old, 128) + lax.div(old, 128), 1.0, 0.0)
    mixed = jnp.dot(flat, spread, precision=lax.Precision.HIGHEST, preferred_element_type=jnp.float32)
    for ch in range(4):
        for par in range(2):
            for t in range(2):
                n = ch * 4 + par * 2 + t
                frame_out[ch, par : par + 1, t * 256 : t * 256 + 256] = mixed[n : n + 1]

    for i in range(2):
        @pl.when(has_next)
        def _(i=i):
            halo(i, 0, whole)(0).wait_send()

        @pl.when(has_prev)
        def _(i=i):
            halo(i, 1, whole)(0).wait_send()

    @pl.when(is_relay)
    def _():
        for i in range(2):
            for way in range(2):
                from_relay(i, way, half_rows[0], half_rows[0], 0).wait_send()

    wait_mixed(MEMBERS - 1, team).wait_send()

    @pl.when(self_part)
    def _():
        wait_parts(BLOCKS - 1).wait_send()

    @pl.when(jnp.logical_not(self_part))
    def _():
        wait_parts(BLOCKS).wait_send()

    store_c.wait()
    store_s.wait()


def shards(species):
    f32 = jnp.float32
    plane = pltpu.VMEM((ROWS, COLS), f32)
    padded = pltpu.VMEM((ROWS + 16, COLS), f32)
    half_plane = pltpu.VMEM((ROWS // 2, COLS), f32)
    dma = pltpu.SemaphoreType.DMA
    fresh, frame = pl.pallas_call(
        kernel,
        out_shape=(
            jax.ShapeDtypeStruct((2, 1, ROWS, COLS), f32),
            jax.ShapeDtypeStruct((4, 2 * ROWS // SIMS, 2 * COLS // GRP), f32),
        ),
        in_specs=[pl.BlockSpec(memory_space=pltpu.HBM)],
        out_specs=(pl.BlockSpec(memory_space=pl.ANY), pl.BlockSpec(memory_space=pltpu.VMEM)),
        scratch_shapes=[
            padded, padded, plane, plane, plane, plane,
            half_plane, half_plane, half_plane, half_plane,
            plane, plane,
            pltpu.VMEM((ROWS + 16, 128), f32),
            pltpu.VMEM((MEMBERS * SLOT, 128), f32),
            pltpu.VMEM((MEMBERS * SLOT, 128), f32),
            pltpu.VMEM((4 * TOTALS, 128), f32),
            pltpu.VMEM((REGION * PIECE, 128), f32),
            pltpu.VMEM((BLOCKS * PIECE, 128), f32),
            dma((2,)), dma((2,)), dma((2, 2)), dma((2, 2, CHUNKS)), dma((2, 2)), dma((2, 2, CHUNKS)),
            dma, dma, dma((4,)), dma, dma, dma,
        ],
        compiler_params=pltpu.CompilerParams(
            collective_id=0, has_side_effects=True, vmem_limit_bytes=32 * 1024 * 1024
        ),
        cost_estimate=pl.CostEstimate(flops=20_000_000, bytes_accessed=4_000_000, transcendentals=2_000_000),
    )(pltpu.with_memory_space_constraint(species, pltpu.HBM))
    return fresh, frame


def solution(mesh):
    return jax.shard_map(
        shards,
        mesh=mesh,
        in_specs=(P(None, ("sim", "grp"), None, None),),
        out_specs=(P(None, ("sim", "grp"), None, None), P(None, "sim", "grp")),
        check_vma=False,
    )
```

```python
import math

import jax
import jax.numpy as jnp
from jax import lax
from jax.experimental import pallas as pl
from jax.experimental.pallas import tpu as pltpu
from jax.sharding import PartitionSpec as P

MESH = pl.DeviceIdType.MESH

ROWS = 128
COLS = 1024
GRP = 4
SIMS = 128
SUB = 8
BLOCKS = SIMS // SUB
MEMBERS = GRP * SUB
REGION = ROWS // SUB
CHUNKS = 8
CHUNK = ROWS // CHUNKS
SLOT = 40
PIECE = 32
TEAM = MEMBERS // 4
TOTALS = 64 * 8

DIFF_S, DIFF_C, FEED, KILL = 0.16, 0.08, 0.035, 0.065


def to(sim, grp):
    return {"sim": sim, "grp": grp}


def in_plane(buf, r):
    window = buf[pl.ds(r, 24), :]
    center = window[8:16]
    lane = lax.broadcasted_iota(jnp.int32, (8, COLS), 1)
    left = jnp.where(lane == 0, 0.0, pltpu.roll(center, 1, 1))
    right = jnp.where(lane == COLS - 1, 0.0, pltpu.roll(center, COLS - 1, 1))
    return center, window[7:15] + window[9:17] + left + right - 6.0 * center


def kernel(
    species, next_out, frame_out,
    sbuf, cbuf, s_up, s_dn, c_up, c_dn, s_new, c_new, edge_cols, sendbuf, recvbuf, totals, pack, parts,
    load_sem, store_sem, halo_send, halo_recv, own_sem, mix_send, mix_recv, part_own, part_send, part_recv,
):
    sim, grp = lax.axis_index("sim"), lax.axis_index("grp")
    plane = sim * GRP + grp
    block, member = lax.div(sim, SUB), lax.rem(sim, SUB)
    seat = member * GRP + grp
    turn = lax.div(block, 4) + lax.rem(block, 4)

    def region_of(m, turn):
        return 2 * lax.rem(lax.div(m, 2) + 8 - turn, 4) + lax.rem(m, 2)

    def member_of(q, turn):
        return 2 * lax.rem(lax.div(q, 2) + turn, 4) + lax.rem(q, 2)

    def first_chunk(sim):
        block = lax.div(sim, SUB)
        place = lax.div(lax.rem(sim, SUB), 2) + 1 + 8 - lax.div(block, 4) - lax.rem(block, 4)
        return 2 * lax.rem(place, 4)

    region = region_of(member, turn)
    team = lax.div(member, 2)

    def source(b):
        t = lax.div(b, 4) + lax.rem(b, 4)
        return b * SUB + member_of(lax.div(sim, REGION), t)

    loads = [
        pltpu.make_async_copy(species.at[i, 0], buf.at[pl.ds(8, ROWS), :], load_sem.at[i])
        for i, buf in ((0, sbuf), (1, cbuf))
    ]
    loads[1].start()
    loads[0].start()

    has_prev, has_next = plane > 0, plane < SIMS * GRP - 1
    prev = to(lax.div(plane - 1, GRP), lax.rem(plane - 1 + GRP, GRP))
    nxt = to(lax.div(plane + 1, GRP), lax.rem(plane + 1, GRP))
    barrier = pltpu.get_barrier_semaphore()

    @pl.when(has_prev)
    def _():
        pl.semaphore_signal(barrier, inc=1, device_id=prev, device_id_type=MESH)

    @pl.when(has_next)
    def _():
        pl.semaphore_signal(barrier, inc=1, device_id=nxt, device_id_type=MESH)

    def greet_member(d, _):
        other = lax.rem(seat + d, MEMBERS)
        there = to(block * SUB + lax.div(other, GRP), lax.rem(other, GRP))
        pl.semaphore_signal(barrier, inc=1, device_id=there, device_id_type=MESH)
        return 0

    lax.fori_loop(1, MEMBERS, greet_member, 0)

    def greet_source(b, _):
        there = source(b)

        @pl.when(there != sim)
        def _():
            pl.semaphore_signal(barrier, inc=1, device_id=to(there, grp), device_id_type=MESH)

        return 0

    lax.fori_loop(0, BLOCKS, greet_source, 0)

    for buf in (sbuf, cbuf):
        buf[0:8, :] = jnp.zeros((8, COLS), jnp.float32)
        buf[ROWS + 8 : ROWS + 16, :] = jnp.zeros((8, COLS), jnp.float32)

    @pl.when(plane == 0)
    def _():
        s_up[...] = jnp.zeros_like(s_up)
        c_up[...] = jnp.zeros_like(c_up)

    @pl.when(plane == SIMS * GRP - 1)
    def _():
        s_dn[...] = jnp.zeros_like(s_dn)
        c_dn[...] = jnp.zeros_like(c_dn)

    self_part = lax.div(sim, REGION) == region
    expected = MEMBERS - 1 + BLOCKS - self_part.astype(jnp.int32)
    expected = expected + has_prev.astype(jnp.int32) + has_next.astype(jnp.int32)
    pl.semaphore_wait(barrier, expected)

    def halo(i, way, rows):
        target = ((s_up, s_dn), (c_up, c_dn))[i][way]
        return lambda chunk: pltpu.make_async_remote_copy(
            src_ref=species.at[i, 0, rows, :],
            dst_ref=target.at[rows, :],
            send_sem=halo_send.at[i, way],
            recv_sem=halo_recv.at[i, way, chunk],
            device_id=(nxt, prev)[way],
            device_id_type=MESH,
        )

    def chunk_rows(k):
        return pl.ds(pl.multiple_of(k * CHUNK, CHUNK), CHUNK)

    whole = pl.ds(0, ROWS)

    first_next, first_prev = first_chunk(nxt["sim"]), first_chunk(prev["sim"])

    def send_catalyst(n, _):
        @pl.when(has_next)
        def _():
            k = lax.rem(first_next + n, CHUNKS)
            halo(1, 0, chunk_rows(k))(k).start()

        @pl.when(has_prev)
        def _():
            k = lax.rem(first_prev + n, CHUNKS)
            halo(1, 1, chunk_rows(k))(k).start()

        return 0

    lax.fori_loop(0, CHUNKS, send_catalyst, 0)
    loads[1].wait()
    loads[0].wait()

    def catalyst_rows(i, _):
        r = pl.multiple_of(8 * i, 8)
        c, lap = in_plane(cbuf, r)
        s = sbuf[pl.ds(pl.multiple_of(r + 8, 8), 8), :]
        c_new[pl.ds(r, 8), :] = c + DIFF_C * lap + s * c * c - (FEED + KILL) * c
        return 0

    lax.fori_loop(0, ROWS // 8, catalyst_rows, 0, unroll=4)

    lane = lax.broadcasted_iota(jnp.int32, (8, 128), 1)
    row = lax.broadcasted_iota(jnp.int32, (8, 128), 0)
    beside = [(0, 0), (2, 0), (1, 127), (4, 0), (3, 127), (6, 0), (5, 127), (7, 127)]

    def mix(k, x, start, length):
        m = member_of(k, turn)
        source_rows = pl.ds(pl.multiple_of((k * GRP + x) * SLOT + start, 8), length)
        target_rows = pl.ds(pl.multiple_of(seat * SLOT + start, 8), length)
        away = pltpu.make_async_remote_copy(
            src_ref=sendbuf.at[source_rows, :],
            dst_ref=recvbuf.at[target_rows, :],
            send_sem=mix_send,
            recv_sem=mix_recv.at[team],
            device_id=to(block * SUB + m, x),
            device_id_type=MESH,
        )
        here = pltpu.make_async_copy(sendbuf.at[source_rows, :], recvbuf.at[target_rows, :], own_sem)
        return away, here

    def send_tiles(k, start, length):
        copies = [mix(k, lax.rem(grp + dx, GRP), start, length) for dx in range(1, GRP + 1)]

        @pl.when(k != region)
        def _():
            for away, _ in copies:
                away.start()

        @pl.when(k == region)
        def _():
            for away, _ in copies[:-1]:
                away.start()
            copies[-1][1].start()

    def rim(k):
        top = c_new[pl.ds(pl.multiple_of(jnp.maximum(k * REGION - 8, 0), 8), 8), :]
        bottom = c_new[pl.ds(pl.multiple_of(jnp.minimum(k * REGION + REGION, ROWS - 8), 8), 8), :]
        above = jnp.where(k == 0, top[0:1], top[7:8])
        below = jnp.where(k == SUB - 1, bottom[7:8], bottom[0:1])
        window = edge_cols[pl.ds(pl.multiple_of(k * REGION, 8), 32), :]
        window = jnp.concatenate([window, jnp.zeros((96, 128), jnp.float32)], axis=0)
        raw = jnp.transpose(window)[0:8]
        cols = pltpu.roll(raw, 121, 1)
        cols = jnp.where((lane == 0) & (k == 0), pltpu.roll(raw, 120, 1), cols)
        cols = jnp.where((lane == REGION + 1) & (k == SUB - 1), pltpu.roll(raw, 122, 1), cols)
        for x in range(GRP):
            c = 2 * x * 128
            tile = pltpu.roll(cols, (4 - 2 * x) % 8, 0)
            tile = jnp.where(row == 0, above[:, c : c + 128], tile)
            tile = jnp.where(row == 1, above[:, c + 128 : c + 256], tile)
            tile = jnp.where(row == 2, below[:, c : c + 128], tile)
            tile = jnp.where(row == 3, below[:, c + 128 : c + 256], tile)
            sendbuf[pl.ds(pl.multiple_of((k * GRP + x) * SLOT + 32, 8), 8), :] = tile

    first = first_chunk(sim)

    def chunk_at(n):
        return lax.rem(first + n, CHUNKS)

    def catalyst_chunk(n, _):
        k = chunk_at(n)

        @pl.when(has_prev)
        def _():
            halo(1, 0, chunk_rows(k))(k).wait_recv()

        @pl.when(has_next)
        def _():
            halo(1, 1, chunk_rows(k))(k).wait_recv()

        rim(chunk_at(n + CHUNKS - 2))
        for h in range(CHUNK // 8):
            r = pl.multiple_of(k * CHUNK + 8 * h, 8)
            rows = pl.ds(r, 8)
            new = c_new[rows, :] + DIFF_C * (c_up[rows, :] + c_dn[rows, :])
            c_new[rows, :] = new
            columns = jnp.zeros((8, 128), jnp.float32)
            for i, (tile, at) in enumerate(beside):
                moved = pltpu.roll(new[:, tile * 128 : tile * 128 + 128], (i - at) % 128, 1)
                columns = jnp.where(lane == i, moved, columns)
            edge_cols[pl.ds(pl.multiple_of(r + 8, 8), 8), :] = columns
            for tile in range(COLS // 128):
                slot = (k * GRP + tile // 2) * SLOT + (h * 2 + tile % 2) * 8
                sendbuf[pl.ds(pl.multiple_of(slot, 8), 8), :] = new[:, tile * 128 : tile * 128 + 128]

        send_tiles(k, 0, 32)

        @pl.when(n >= 3)
        def _():
            send_tiles(chunk_at(n - 2), 32, 8)

        return 0

    lax.fori_loop(0, CHUNKS, catalyst_chunk, 0)
    for n in (CHUNKS - 2, CHUNKS - 1, CHUNKS):
        rim(chunk_at(n))
    for n in (CHUNKS - 2, CHUNKS - 1, CHUNKS):
        send_tiles(chunk_at(n), 32, 8)

    store_c = pltpu.make_async_copy(c_new, next_out.at[1, 0], store_sem.at[1])
    store_c.start()

    @pl.when(has_next)
    def _():
        halo(0, 0, whole)(0).start()

    @pl.when(has_prev)
    def _():
        halo(0, 1, whole)(0).start()

    def wait_mixed(count, t):
        some = pl.ds(0, count * SLOT)
        return pltpu.make_async_remote_copy(
            src_ref=sendbuf.at[some, :], dst_ref=recvbuf.at[some, :],
            send_sem=mix_send, recv_sem=mix_recv.at[t], device_id=to(sim, grp), device_id_type=MESH,
        )

    extinct = 6.0 / (BLOCKS * MEMBERS)
    log2e = math.log2(math.e)
    thin, narrow = -extinct * log2e / 256.0, -8.0 * log2e / 256.0

    def render(i, _):
        t_now = lax.rem(team + 6 - i, 4)

        @pl.when(t_now == team)
        def _():
            one_slot = pl.ds(0, SLOT)
            pltpu.make_async_copy(sendbuf.at[one_slot, :], recvbuf.at[one_slot, :], own_sem).wait()
            wait_mixed(TEAM - 1, team).wait_recv()

        @pl.when(t_now != team)
        def _():
            wait_mixed(TEAM, t_now).wait_recv()

        base = t_now * (TEAM * SLOT)
        sides = jnp.concatenate(
            [
                recvbuf[pl.ds(base + 36, TEAM, stride=SLOT), :],
                recvbuf[pl.ds(base + 37, TEAM, stride=SLOT), :],
                jnp.zeros((128 - 2 * TEAM, 128), jnp.float32),
            ],
            axis=0,
        )
        sides = jnp.transpose(sides)

        for h in range(2):
            for par in range(2):
                near = 2 * par + 8 * h
                side = 3.0 * sides[1 + 8 * h : 9 + 8 * h] + sides[near : near + 8]

                def layer(p, sums, h=h, par=par, side=side):
                    at = pl.multiple_of(base + p * SLOT, 8)
                    rim = recvbuf[pl.ds(at + 32, 8), :]
                    rows = []
                    for t in range(2):
                        mine = recvbuf[pl.ds(at + (2 * h + t) * 8, 8), :]
                        across = recvbuf[pl.ds(at + (2 - 2 * h + t) * 8, 8), :]
                        if par == 0:
                            beyond = rim[t : t + 1] if h == 0 else across[7:8]
                            shifted = jnp.where(row == 0, beyond, pltpu.roll(mine, 1, 0))
                        else:
                            beyond = rim[2 + t : 3 + t] if h == 1 else across[0:1]
                            shifted = jnp.where(row == 7, beyond, pltpu.roll(mine, 7, 0))
                        rows.append(3.0 * mine + shifted)
                    leftmost = pltpu.roll(side, (128 - p) % 128, 1)
                    rightmost = pltpu.roll(side, 127 - TEAM - p, 1)
                    fwd = [pltpu.roll(v, 1, 1) for v in rows]
                    bwd = [pltpu.roll(v, 127, 1) for v in rows]
                    low = [jnp.where(lane == 0, leftmost, fwd[0]), jnp.where(lane == 0, fwd[0], fwd[1])]
                    high = [jnp.where(lane == 127, bwd[1], bwd[0]), jnp.where(lane == 127, rightmost, bwd[1])]
                    result = []
                    for cpar in range(2):
                        for t in range(2):
                            q = 3.0 * rows[t] + (low, high)[cpar][t]
                            red, green, blue, clear = sums[(cpar * 2 + t) * 4 : (cpar * 2 + t) * 4 + 4]
                            after = clear * jnp.exp2((q * q) * thin)
                            weight = clear - after
                            mid = q - 8.0
                            warm = mid * (3.0 / 16.0)
                            red = red + weight * jnp.tanh(warm)
                            green = green + weight * jnp.exp2((mid * mid) * narrow)
                            blue = blue + weight * jnp.tanh(warm + 0.6)
                            result += [red, green, blue, after]
                    return tuple(result)

                zero, one = jnp.zeros((8, 128), jnp.float32), jnp.ones((8, 128), jnp.float32)
                sums = (zero, zero, zero, one) * 4
                for p in range(TEAM):
                    sums = layer(p, sums)
                for j in range(16):
                    at = t_now * TOTALS + ((h * 2 + par) * 16 + j) * 8
                    totals[pl.ds(pl.multiple_of(at, 8), 8), :] = sums[j]
        return 0

    lax.fori_loop(0, 4, render, 0)

    def piece_rows(n):
        return pl.ds(pl.multiple_of(n * PIECE, PIECE), PIECE)

    for h in range(2):
        for par in range(2):
            for cpar in range(2):
                for t in range(2):
                    base = ((h * 2 + par) * 16 + (cpar * 2 + t) * 4) * 8
                    got = [[totals[i * TOTALS + base + 8 * ch : i * TOTALS + base + 8 * ch + 8, :] for ch in range(4)] for i in range(4)]
                    red, green, blue, clear = got[0]
                    for i in range(1, 4):
                        red = red + clear * got[i][0]
                        green = green + clear * got[i][1]
                        blue = blue + clear * got[i][2]
                        clear = clear * got[i][3]
                    for ch, value in enumerate((red, green, blue, clear)):
                        at = 8 * h * PIECE + ch * 8 + cpar * 4 + par * 2 + t
                        pack[pl.ds(at, 8, stride=PIECE), :] = value

        def send_piece(n, _, h=h):
            j = 8 * h + lax.rem(n + sim, 8)
            there = region * REGION + j

            @pl.when(there != sim)
            def _():
                pltpu.make_async_remote_copy(
                    src_ref=pack.at[piece_rows(j), :],
                    dst_ref=parts.at[piece_rows(block), :],
                    send_sem=part_send,
                    recv_sem=part_recv,
                    device_id=to(there, grp),
                    device_id_type=MESH,
                ).start()

            return 0

        lax.fori_loop(0, 8, send_piece, 0)

    @pl.when(self_part)
    def _():
        mine = pltpu.make_async_copy(
            pack.at[piece_rows(lax.rem(sim, REGION)), :], parts.at[piece_rows(block), :], part_own
        )
        mine.start()
        mine.wait()

    @pl.when(has_prev)
    def _():
        halo(0, 0, whole)(0).wait_recv()

    @pl.when(has_next)
    def _():
        halo(0, 1, whole)(0).wait_recv()

    def substrate_rows(k, _):
        r = pl.multiple_of(8 * k, 8)
        rows = pl.ds(r, 8)
        s, lap = in_plane(sbuf, r)
        lap = lap + s_up[rows, :] + s_dn[rows, :]
        c = cbuf[pl.ds(pl.multiple_of(r + 8, 8), 8), :]
        s_new[rows, :] = s + DIFF_S * lap - s * c * c + FEED * (1.0 - s)
        return 0

    lax.fori_loop(0, ROWS // 8, substrate_rows, 0, unroll=4)
    store_s = pltpu.make_async_copy(s_new, next_out.at[0, 0], store_sem.at[0])
    store_s.start()

    old = lax.broadcasted_iota(jnp.int32, (256, 256), 0)
    new = lax.broadcasted_iota(jnp.int32, (256, 256), 1)
    spread = jnp.where(new == 2 * lax.rem(old, 128) + lax.div(old, 128), 1.0, 0.0).astype(jnp.bfloat16)

    def wait_parts(count):
        some = pl.ds(0, count * PIECE)
        return pltpu.make_async_remote_copy(
            src_ref=pack.at[some, :], dst_ref=parts.at[some, :],
            send_sem=part_send, recv_sem=part_recv, device_id=to(sim, grp), device_id_type=MESH,
        )

    @pl.when(self_part)
    def _():
        wait_parts(BLOCKS - 1).wait_recv()

    @pl.when(jnp.logical_not(self_part))
    def _():
        wait_parts(BLOCKS).wait_recv()

    def add_block(b, totals):
        base = pl.multiple_of(b * PIECE, 8)
        red, green, blue, clear = totals
        got = [parts[pl.ds(base + 8 * ch, 8), :] for ch in range(4)]
        return (
            red + clear * got[0], green + clear * got[1], blue + clear * got[2], clear * got[3],
        )

    zero, one = jnp.zeros((8, 128), jnp.float32), jnp.ones((8, 128), jnp.float32)
    red, green, blue, clear = lax.fori_loop(0, BLOCKS, add_block, (zero, zero, zero, one), unroll=True)
    opaque = 1.0 - clear
    channels = [0.5 * (opaque + red), green, 0.5 * (opaque - blue), opaque]
    flat = jnp.concatenate([jnp.concatenate([v[0:4], v[4:8]], axis=1) for v in channels], axis=0)
    bf16 = jnp.bfloat16
    high = flat.astype(bf16)
    rest = flat - high.astype(jnp.float32)
    middle = rest.astype(bf16)
    low = (rest - middle.astype(jnp.float32)).astype(bf16)
    split = jnp.dot(
        jnp.concatenate([high, middle, low], axis=0), spread, preferred_element_type=jnp.float32
    )
    mixed = split[0:16] + (split[16:32] + split[32:48])
    for ch in range(4):
        for par in range(2):
            for t in range(2):
                n = ch * 4 + par * 2 + t
                frame_out[ch, par : par + 1, t * 256 : t * 256 + 256] = mixed[n : n + 1]

    for i in range(2):
        @pl.when(has_next)
        def _(i=i):
            halo(i, 0, whole)(0).wait_send()

        @pl.when(has_prev)
        def _(i=i):
            halo(i, 1, whole)(0).wait_send()

    wait_mixed(MEMBERS - 1, team).wait_send()

    @pl.when(self_part)
    def _():
        wait_parts(BLOCKS - 1).wait_send()

    @pl.when(jnp.logical_not(self_part))
    def _():
        wait_parts(BLOCKS).wait_send()

    store_c.wait()
    store_s.wait()


def shards(species):
    f32 = jnp.float32
    plane = pltpu.VMEM((ROWS, COLS), f32)
    padded = pltpu.VMEM((ROWS + 16, COLS), f32)
    dma = pltpu.SemaphoreType.DMA
    fresh, frame = pl.pallas_call(
        kernel,
        out_shape=(
            jax.ShapeDtypeStruct((2, 1, ROWS, COLS), f32),
            jax.ShapeDtypeStruct((4, 2 * ROWS // SIMS, 2 * COLS // GRP), f32),
        ),
        in_specs=[pl.BlockSpec(memory_space=pltpu.HBM)],
        out_specs=(pl.BlockSpec(memory_space=pl.ANY), pl.BlockSpec(memory_space=pltpu.VMEM)),
        scratch_shapes=[
            padded, padded, plane, plane, plane, plane,
            plane, plane,
            pltpu.VMEM((ROWS + 16, 128), f32),
            pltpu.VMEM((MEMBERS * SLOT, 128), f32),
            pltpu.VMEM((MEMBERS * SLOT, 128), f32),
            pltpu.VMEM((4 * TOTALS, 128), f32),
            pltpu.VMEM((REGION * PIECE, 128), f32),
            pltpu.VMEM((BLOCKS * PIECE, 128), f32),
            dma((2,)), dma((2,)), dma((2, 2)), dma((2, 2, CHUNKS)),
            dma, dma, dma((4,)), dma, dma, dma,
        ],
        compiler_params=pltpu.CompilerParams(
            collective_id=0, has_side_effects=True, vmem_limit_bytes=32 * 1024 * 1024
        ),
        cost_estimate=pl.CostEstimate(flops=20_000_000, bytes_accessed=4_000_000, transcendentals=2_000_000),
    )(pltpu.with_memory_space_constraint(species, pltpu.HBM))
    return fresh, frame


def solution(mesh):
    return jax.shard_map(
        shards,
        mesh=mesh,
        in_specs=(P(None, ("sim", "grp"), None, None),),
        out_specs=(P(None, ("sim", "grp"), None, None), P(None, "sim", "grp")),
        check_vma=False,
    )
```

```python
import math

import jax
import jax.numpy as jnp
from jax import lax
from jax.experimental import pallas as pl
from jax.experimental.pallas import tpu as pltpu
from jax.sharding import PartitionSpec as P

MESH = pl.DeviceIdType.MESH

ROWS = 128
COLS = 1024
GRP = 4
SIMS = 128
SUB = 8
BLOCKS = SIMS // SUB
MEMBERS = GRP * SUB
REGION = ROWS // SUB
CHUNKS = 8
CHUNK = ROWS // CHUNKS
SLOT = 40
PIECE = 32
TEAM = MEMBERS // 4
TOTALS = 64 * 8

DIFF_S, DIFF_C, FEED, KILL = 0.16, 0.08, 0.035, 0.065


def to(sim, grp):
    return {"sim": sim, "grp": grp}


def in_plane(buf, r):
    window = buf[pl.ds(r, 24), :]
    center = window[8:16]
    lane = lax.broadcasted_iota(jnp.int32, (8, COLS), 1)
    left = jnp.where(lane == 0, 0.0, pltpu.roll(center, 1, 1))
    right = jnp.where(lane == COLS - 1, 0.0, pltpu.roll(center, COLS - 1, 1))
    return center, window[7:15] + window[9:17] + left + right - 6.0 * center


def kernel(
    species, next_out, frame_out,
    sbuf, cbuf, s_up, s_dn, c_up, c_dn, s_new, c_new, edge_cols, sendbuf, recvbuf, totals, pack, parts,
    load_sem, store_sem, halo_send, halo_recv, own_sem, mix_send, mix_recv, part_own, part_send, part_recv,
):
    sim, grp = lax.axis_index("sim"), lax.axis_index("grp")
    plane = sim * GRP + grp
    block, member = lax.div(sim, SUB), lax.rem(sim, SUB)
    seat = member * GRP + grp
    turn = lax.div(block, 4) + lax.rem(block, 4)

    def region_of(m, turn):
        return 2 * lax.rem(lax.div(m, 2) + 8 - turn, 4) + lax.rem(m, 2)

    def member_of(q, turn):
        return 2 * lax.rem(lax.div(q, 2) + turn, 4) + lax.rem(q, 2)

    def first_chunk(sim):
        block = lax.div(sim, SUB)
        place = lax.div(lax.rem(sim, SUB), 2) + 1 + 8 - lax.div(block, 4) - lax.rem(block, 4)
        return 2 * lax.rem(place, 4)

    region = region_of(member, turn)
    team = lax.div(member, 2)

    def source(b):
        t = lax.div(b, 4) + lax.rem(b, 4)
        return b * SUB + member_of(lax.div(sim, REGION), t)

    loads = [
        pltpu.make_async_copy(species.at[i, 0], buf.at[pl.ds(8, ROWS), :], load_sem.at[i])
        for i, buf in ((0, sbuf), (1, cbuf))
    ]
    loads[1].start()
    loads[0].start()

    has_prev, has_next = plane > 0, plane < SIMS * GRP - 1
    prev = to(lax.div(plane - 1, GRP), lax.rem(plane - 1 + GRP, GRP))
    nxt = to(lax.div(plane + 1, GRP), lax.rem(plane + 1, GRP))
    barrier = pltpu.get_barrier_semaphore()

    @pl.when(has_prev)
    def _():
        pl.semaphore_signal(barrier, inc=1, device_id=prev, device_id_type=MESH)

    @pl.when(has_next)
    def _():
        pl.semaphore_signal(barrier, inc=1, device_id=nxt, device_id_type=MESH)

    def greet_member(d, _):
        other = lax.rem(seat + d, MEMBERS)
        there = to(block * SUB + lax.div(other, GRP), lax.rem(other, GRP))
        pl.semaphore_signal(barrier, inc=1, device_id=there, device_id_type=MESH)
        return 0

    lax.fori_loop(1, MEMBERS, greet_member, 0)

    def greet_source(b, _):
        there = source(b)

        @pl.when(there != sim)
        def _():
            pl.semaphore_signal(barrier, inc=1, device_id=to(there, grp), device_id_type=MESH)

        return 0

    lax.fori_loop(0, BLOCKS, greet_source, 0)

    for buf in (sbuf, cbuf):
        buf[0:8, :] = jnp.zeros((8, COLS), jnp.float32)
        buf[ROWS + 8 : ROWS + 16, :] = jnp.zeros((8, COLS), jnp.float32)

    @pl.when(plane == 0)
    def _():
        s_up[...] = jnp.zeros_like(s_up)
        c_up[...] = jnp.zeros_like(c_up)

    @pl.when(plane == SIMS * GRP - 1)
    def _():
        s_dn[...] = jnp.zeros_like(s_dn)
        c_dn[...] = jnp.zeros_like(c_dn)

    self_part = lax.div(sim, REGION) == region
    expected = MEMBERS - 1 + BLOCKS - self_part.astype(jnp.int32)
    expected = expected + has_prev.astype(jnp.int32) + has_next.astype(jnp.int32)
    pl.semaphore_wait(barrier, expected)

    def halo(i, way, rows):
        target = ((s_up, s_dn), (c_up, c_dn))[i][way]
        return lambda chunk: pltpu.make_async_remote_copy(
            src_ref=(sbuf, cbuf)[i].at[pl.ds(pl.multiple_of(rows.start + 8, 8), rows.size), :],
            dst_ref=target.at[rows, :],
            send_sem=halo_send.at[i, way],
            recv_sem=halo_recv.at[i, way, chunk],
            device_id=(nxt, prev)[way],
            device_id_type=MESH,
        )

    def chunk_rows(k):
        return pl.ds(pl.multiple_of(k * CHUNK, CHUNK), CHUNK)

    whole = pl.ds(0, ROWS)

    first_next, first_prev = first_chunk(nxt["sim"]), first_chunk(prev["sim"])

    def send_catalyst(n, _):
        @pl.when(has_next)
        def _():
            k = lax.rem(first_next + n, CHUNKS)
            halo(1, 0, chunk_rows(k))(k).start()

        @pl.when(has_prev)
        def _():
            k = lax.rem(first_prev + n, CHUNKS)
            halo(1, 1, chunk_rows(k))(k).start()

        return 0

    loads[1].wait()
    lax.fori_loop(0, CHUNKS, send_catalyst, 0)
    loads[0].wait()

    def catalyst_rows(i, _):
        r = pl.multiple_of(8 * i, 8)
        c, lap = in_plane(cbuf, r)
        s = sbuf[pl.ds(pl.multiple_of(r + 8, 8), 8), :]
        c_new[pl.ds(r, 8), :] = c + DIFF_C * lap + s * c * c - (FEED + KILL) * c
        return 0

    lax.fori_loop(0, ROWS // 8, catalyst_rows, 0, unroll=4)

    lane = lax.broadcasted_iota(jnp.int32, (8, 128), 1)
    row = lax.broadcasted_iota(jnp.int32, (8, 128), 0)
    beside = [(0, 0), (2, 0), (1, 127), (4, 0), (3, 127), (6, 0), (5, 127), (7, 127)]

    def mix(k, x, start, length):
        m = member_of(k, turn)
        source_rows = pl.ds(pl.multiple_of((k * GRP + x) * SLOT + start, 8), length)
        target_rows = pl.ds(pl.multiple_of(seat * SLOT + start, 8), length)
        away = pltpu.make_async_remote_copy(
            src_ref=sendbuf.at[source_rows, :],
            dst_ref=recvbuf.at[target_rows, :],
            send_sem=mix_send,
            recv_sem=mix_recv.at[team],
            device_id=to(block * SUB + m, x),
            device_id_type=MESH,
        )
        here = pltpu.make_async_copy(sendbuf.at[source_rows, :], recvbuf.at[target_rows, :], own_sem)
        return away, here

    def send_tiles(k, start, length):
        copies = [mix(k, lax.rem(grp + dx, GRP), start, length) for dx in range(1, GRP + 1)]

        @pl.when(k != region)
        def _():
            for away, _ in copies:
                away.start()

        @pl.when(k == region)
        def _():
            for away, _ in copies[:-1]:
                away.start()
            copies[-1][1].start()

    def rim(k):
        top = c_new[pl.ds(pl.multiple_of(jnp.maximum(k * REGION - 8, 0), 8), 8), :]
        bottom = c_new[pl.ds(pl.multiple_of(jnp.minimum(k * REGION + REGION, ROWS - 8), 8), 8), :]
        above = jnp.where(k == 0, top[0:1], top[7:8])
        below = jnp.where(k == SUB - 1, bottom[7:8], bottom[0:1])
        window = edge_cols[pl.ds(pl.multiple_of(k * REGION, 8), 32), :]
        window = jnp.concatenate([window, jnp.zeros((96, 128), jnp.float32)], axis=0)
        raw = jnp.transpose(window)[0:8]
        cols = pltpu.roll(raw, 121, 1)
        cols = jnp.where((lane == 0) & (k == 0), pltpu.roll(raw, 120, 1), cols)
        cols = jnp.where((lane == REGION + 1) & (k == SUB - 1), pltpu.roll(raw, 122, 1), cols)
        for x in range(GRP):
            c = 2 * x * 128
            tile = pltpu.roll(cols, (4 - 2 * x) % 8, 0)
            tile = jnp.where(row == 0, above[:, c : c + 128], tile)
            tile = jnp.where(row == 1, above[:, c + 128 : c + 256], tile)
            tile = jnp.where(row == 2, below[:, c : c + 128], tile)
            tile = jnp.where(row == 3, below[:, c + 128 : c + 256], tile)
            sendbuf[pl.ds(pl.multiple_of((k * GRP + x) * SLOT + 32, 8), 8), :] = tile

    first = first_chunk(sim)

    def chunk_at(n):
        return lax.rem(first + n, CHUNKS)

    def catalyst_chunk(n, _):
        k = chunk_at(n)

        @pl.when(has_prev)
        def _():
            halo(1, 0, chunk_rows(k))(k).wait_recv()

        @pl.when(has_next)
        def _():
            halo(1, 1, chunk_rows(k))(k).wait_recv()

        rim(chunk_at(n + CHUNKS - 2))
        for h in range(CHUNK // 8):
            r = pl.multiple_of(k * CHUNK + 8 * h, 8)
            rows = pl.ds(r, 8)
            new = c_new[rows, :] + DIFF_C * (c_up[rows, :] + c_dn[rows, :])
            c_new[rows, :] = new
            columns = jnp.zeros((8, 128), jnp.float32)
            for i, (tile, at) in enumerate(beside):
                moved = pltpu.roll(new[:, tile * 128 : tile * 128 + 128], (i - at) % 128, 1)
                columns = jnp.where(lane == i, moved, columns)
            edge_cols[pl.ds(pl.multiple_of(r + 8, 8), 8), :] = columns
            for tile in range(COLS // 128):
                slot = (k * GRP + tile // 2) * SLOT + (h * 2 + tile % 2) * 8
                sendbuf[pl.ds(pl.multiple_of(slot, 8), 8), :] = new[:, tile * 128 : tile * 128 + 128]

        send_tiles(k, 0, 32)

        @pl.when(n >= 3)
        def _():
            send_tiles(chunk_at(n - 2), 32, 8)

        return 0

    lax.fori_loop(0, CHUNKS, catalyst_chunk, 0)
    for n in (CHUNKS - 2, CHUNKS - 1, CHUNKS):
        rim(chunk_at(n))
    for n in (CHUNKS - 2, CHUNKS - 1, CHUNKS):
        send_tiles(chunk_at(n), 32, 8)

    store_c = pltpu.make_async_copy(c_new, next_out.at[1, 0], store_sem.at[1])
    store_c.start()

    def wait_mixed(count, t):
        some = pl.ds(0, count * SLOT)
        return pltpu.make_async_remote_copy(
            src_ref=sendbuf.at[some, :], dst_ref=recvbuf.at[some, :],
            send_sem=mix_send, recv_sem=mix_recv.at[t], device_id=to(sim, grp), device_id_type=MESH,
        )

    extinct = 6.0 / (BLOCKS * MEMBERS)
    log2e = math.log2(math.e)
    thin, narrow = -extinct * log2e / 256.0, -8.0 * log2e / 256.0

    def render(i, _):
        t_now = lax.rem(team + 6 - i, 4)

        @pl.when(t_now == team)
        def _():
            one_slot = pl.ds(0, SLOT)
            pltpu.make_async_copy(sendbuf.at[one_slot, :], recvbuf.at[one_slot, :], own_sem).wait()
            wait_mixed(TEAM - 1, team).wait_recv()

        @pl.when(t_now != team)
        def _():
            wait_mixed(TEAM, t_now).wait_recv()

        @pl.when((i == 3) & has_next)
        def _():
            halo(0, 0, whole)(0).start()

        @pl.when((i == 3) & has_prev)
        def _():
            halo(0, 1, whole)(0).start()

        base = t_now * (TEAM * SLOT)
        sides = jnp.concatenate(
            [
                recvbuf[pl.ds(base + 36, TEAM, stride=SLOT), :],
                recvbuf[pl.ds(base + 37, TEAM, stride=SLOT), :],
                jnp.zeros((128 - 2 * TEAM, 128), jnp.float32),
            ],
            axis=0,
        )
        sides = jnp.transpose(sides)

        for h in range(2):
            for par in range(2):
                near = 2 * par + 8 * h
                side = 3.0 * sides[1 + 8 * h : 9 + 8 * h] + sides[near : near + 8]

                def layer(p, sums, h=h, par=par, side=side):
                    at = pl.multiple_of(base + p * SLOT, 8)
                    rim = recvbuf[pl.ds(at + 32, 8), :]
                    rows = []
                    for t in range(2):
                        mine = recvbuf[pl.ds(at + (2 * h + t) * 8, 8), :]
                        across = recvbuf[pl.ds(at + (2 - 2 * h + t) * 8, 8), :]
                        if par == 0:
                            beyond = rim[t : t + 1] if h == 0 else across[7:8]
                            shifted = jnp.where(row == 0, beyond, pltpu.roll(mine, 1, 0))
                        else:
                            beyond = rim[2 + t : 3 + t] if h == 1 else across[0:1]
                            shifted = jnp.where(row == 7, beyond, pltpu.roll(mine, 7, 0))
                        rows.append(3.0 * mine + shifted)
                    leftmost = pltpu.roll(side, (128 - p) % 128, 1)
                    rightmost = pltpu.roll(side, 127 - TEAM - p, 1)
                    fwd = [pltpu.roll(v, 1, 1) for v in rows]
                    bwd = [pltpu.roll(v, 127, 1) for v in rows]
                    low = [jnp.where(lane == 0, leftmost, fwd[0]), jnp.where(lane == 0, fwd[0], fwd[1])]
                    high = [jnp.where(lane == 127, bwd[1], bwd[0]), jnp.where(lane == 127, rightmost, bwd[1])]
                    result = []
                    for cpar in range(2):
                        for t in range(2):
                            q = 3.0 * rows[t] + (low, high)[cpar][t]
                            red, green, blue, clear = sums[(cpar * 2 + t) * 4 : (cpar * 2 + t) * 4 + 4]
                            after = clear * jnp.exp2((q * q) * thin)
                            weight = clear - after
                            mid = q - 8.0
                            warm = mid * (3.0 / 16.0)
                            red = red + weight * jnp.tanh(warm)
                            green = green + weight * jnp.exp2((mid * mid) * narrow)
                            blue = blue + weight * jnp.tanh(warm + 0.6)
                            result += [red, green, blue, after]
                    return tuple(result)

                zero, one = jnp.zeros((8, 128), jnp.float32), jnp.ones((8, 128), jnp.float32)
                sums = (zero, zero, zero, one) * 4
                for p in range(TEAM):
                    sums = layer(p, sums)
                for j in range(16):
                    at = t_now * TOTALS + ((h * 2 + par) * 16 + j) * 8
                    totals[pl.ds(pl.multiple_of(at, 8), 8), :] = sums[j]
        return 0

    lax.fori_loop(0, 4, render, 0)

    def piece_rows(n):
        return pl.ds(pl.multiple_of(n * PIECE, PIECE), PIECE)

    for h in range(2):
        for par in range(2):
            for cpar in range(2):
                for t in range(2):
                    base = ((h * 2 + par) * 16 + (cpar * 2 + t) * 4) * 8
                    got = [[totals[i * TOTALS + base + 8 * ch : i * TOTALS + base + 8 * ch + 8, :] for ch in range(4)] for i in range(4)]
                    red, green, blue, clear = got[0]
                    for i in range(1, 4):
                        red = red + clear * got[i][0]
                        green = green + clear * got[i][1]
                        blue = blue + clear * got[i][2]
                        clear = clear * got[i][3]
                    for ch, value in enumerate((red, green, blue, clear)):
                        at = 8 * h * PIECE + ch * 8 + cpar * 4 + par * 2 + t
                        pack[pl.ds(at, 8, stride=PIECE), :] = value

        def send_piece(n, _, h=h):
            j = 8 * h + lax.rem(n + sim, 8)
            there = region * REGION + j

            @pl.when(there != sim)
            def _():
                pltpu.make_async_remote_copy(
                    src_ref=pack.at[piece_rows(j), :],
                    dst_ref=parts.at[piece_rows(block), :],
                    send_sem=part_send,
                    recv_sem=part_recv,
                    device_id=to(there, grp),
                    device_id_type=MESH,
                ).start()

            return 0

        lax.fori_loop(0, 8, send_piece, 0)

    @pl.when(self_part)
    def _():
        mine = pltpu.make_async_copy(
            pack.at[piece_rows(lax.rem(sim, REGION)), :], parts.at[piece_rows(block), :], part_own
        )
        mine.start()
        mine.wait()

    @pl.when(has_prev)
    def _():
        halo(0, 0, whole)(0).wait_recv()

    @pl.when(has_next)
    def _():
        halo(0, 1, whole)(0).wait_recv()

    def substrate_rows(k, _):
        r = pl.multiple_of(8 * k, 8)
        rows = pl.ds(r, 8)
        s, lap = in_plane(sbuf, r)
        lap = lap + s_up[rows, :] + s_dn[rows, :]
        c = cbuf[pl.ds(pl.multiple_of(r + 8, 8), 8), :]
        s_new[rows, :] = s + DIFF_S * lap - s * c * c + FEED * (1.0 - s)
        return 0

    lax.fori_loop(0, ROWS // 8, substrate_rows, 0, unroll=4)
    store_s = pltpu.make_async_copy(s_new, next_out.at[0, 0], store_sem.at[0])
    store_s.start()

    old = lax.broadcasted_iota(jnp.int32, (256, 256), 0)
    new = lax.broadcasted_iota(jnp.int32, (256, 256), 1)
    spread = jnp.where(new == 2 * lax.rem(old, 128) + lax.div(old, 128), 1.0, 0.0).astype(jnp.bfloat16)

    def wait_parts(count):
        some = pl.ds(0, count * PIECE)
        return pltpu.make_async_remote_copy(
            src_ref=pack.at[some, :], dst_ref=parts.at[some, :],
            send_sem=part_send, recv_sem=part_recv, device_id=to(sim, grp), device_id_type=MESH,
        )

    @pl.when(self_part)
    def _():
        wait_parts(BLOCKS - 1).wait_recv()

    @pl.when(jnp.logical_not(self_part))
    def _():
        wait_parts(BLOCKS).wait_recv()

    def add_block(b, totals):
        base = pl.multiple_of(b * PIECE, 8)
        red, green, blue, clear = totals
        got = [parts[pl.ds(base + 8 * ch, 8), :] for ch in range(4)]
        return (
            red + clear * got[0], green + clear * got[1], blue + clear * got[2], clear * got[3],
        )

    zero, one = jnp.zeros((8, 128), jnp.float32), jnp.ones((8, 128), jnp.float32)
    red, green, blue, clear = lax.fori_loop(0, BLOCKS, add_block, (zero, zero, zero, one), unroll=True)
    opaque = 1.0 - clear
    channels = [0.5 * (opaque + red), green, 0.5 * (opaque - blue), opaque]
    flat = jnp.concatenate([jnp.concatenate([v[0:4], v[4:8]], axis=1) for v in channels], axis=0)
    bf16 = jnp.bfloat16
    high = flat.astype(bf16)
    rest = flat - high.astype(jnp.float32)
    middle = rest.astype(bf16)
    low = (rest - middle.astype(jnp.float32)).astype(bf16)
    split = jnp.dot(
        jnp.concatenate([high, middle, low], axis=0), spread, preferred_element_type=jnp.float32
    )
    mixed = split[0:16] + (split[16:32] + split[32:48])
    for ch in range(4):
        for par in range(2):
            for t in range(2):
                n = ch * 4 + par * 2 + t
                frame_out[ch, par : par + 1, t * 256 : t * 256 + 256] = mixed[n : n + 1]

    for i in range(2):
        @pl.when(has_next)
        def _(i=i):
            halo(i, 0, whole)(0).wait_send()

        @pl.when(has_prev)
        def _(i=i):
            halo(i, 1, whole)(0).wait_send()

    wait_mixed(MEMBERS - 1, team).wait_send()

    @pl.when(self_part)
    def _():
        wait_parts(BLOCKS - 1).wait_send()

    @pl.when(jnp.logical_not(self_part))
    def _():
        wait_parts(BLOCKS).wait_send()

    store_c.wait()
    store_s.wait()


def shards(species):
    f32 = jnp.float32
    plane = pltpu.VMEM((ROWS, COLS), f32)
    padded = pltpu.VMEM((ROWS + 16, COLS), f32)
    dma = pltpu.SemaphoreType.DMA
    fresh, frame = pl.pallas_call(
        kernel,
        out_shape=(
            jax.ShapeDtypeStruct((2, 1, ROWS, COLS), f32),
            jax.ShapeDtypeStruct((4, 2 * ROWS // SIMS, 2 * COLS // GRP), f32),
        ),
        in_specs=[pl.BlockSpec(memory_space=pltpu.HBM)],
        out_specs=(pl.BlockSpec(memory_space=pl.ANY), pl.BlockSpec(memory_space=pltpu.VMEM)),
        scratch_shapes=[
            padded, padded, plane, plane, plane, plane,
            plane, plane,
            pltpu.VMEM((ROWS + 16, 128), f32),
            pltpu.VMEM((MEMBERS * SLOT, 128), f32),
            pltpu.VMEM((MEMBERS * SLOT, 128), f32),
            pltpu.VMEM((4 * TOTALS, 128), f32),
            pltpu.VMEM((REGION * PIECE, 128), f32),
            pltpu.VMEM((BLOCKS * PIECE, 128), f32),
            dma((2,)), dma((2,)), dma((2, 2)), dma((2, 2, CHUNKS)),
            dma, dma, dma((4,)), dma, dma, dma,
        ],
        compiler_params=pltpu.CompilerParams(
            collective_id=0, has_side_effects=True, vmem_limit_bytes=32 * 1024 * 1024
        ),
        cost_estimate=pl.CostEstimate(flops=20_000_000, bytes_accessed=4_000_000, transcendentals=2_000_000),
    )(pltpu.with_memory_space_constraint(species, pltpu.HBM))
    return fresh, frame


def solution(mesh):
    return jax.shard_map(
        shards,
        mesh=mesh,
        in_specs=(P(None, ("sim", "grp"), None, None),),
        out_specs=(P(None, ("sim", "grp"), None, None), P(None, "sim", "grp")),
        check_vma=False,
    )
```

```python
import math

import jax
import jax.numpy as jnp
from jax import lax
from jax.experimental import pallas as pl
from jax.experimental.pallas import tpu as pltpu
from jax.sharding import PartitionSpec as P

MESH = pl.DeviceIdType.MESH

ROWS = 128
COLS = 1024
GRP = 4
SIMS = 128
SUB = 8
BLOCKS = SIMS // SUB
MEMBERS = GRP * SUB
REGION = ROWS // SUB
CHUNKS = 8
CHUNK = ROWS // CHUNKS
SLOT = 40
PIECE = 32
TEAM = MEMBERS // 4
TOTALS = 64 * 8

DIFF_S, DIFF_C, FEED, KILL = 0.16, 0.08, 0.035, 0.065


def to(sim, grp):
    return {"sim": sim, "grp": grp}


def in_plane(buf, r):
    window = buf[pl.ds(r, 24), :]
    center = window[8:16]
    lane = lax.broadcasted_iota(jnp.int32, (8, COLS), 1)
    left = jnp.where(lane == 0, 0.0, pltpu.roll(center, 1, 1))
    right = jnp.where(lane == COLS - 1, 0.0, pltpu.roll(center, COLS - 1, 1))
    return center, window[7:15] + window[9:17] + left + right - 6.0 * center


def kernel(
    species, next_out, frame_out,
    sbuf, cbuf, s_up, s_dn, c_up, c_dn, s_new, c_new, edge_cols, sendbuf, recvbuf, totals, pack, parts,
    load_sem, store_sem, halo_send, halo_recv, own_sem, mix_send, mix_recv, part_own, part_send, part_recv,
):
    sim, grp = lax.axis_index("sim"), lax.axis_index("grp")
    plane = sim * GRP + grp
    block, member = lax.div(sim, SUB), lax.rem(sim, SUB)
    seat = member * GRP + grp
    turn = lax.div(block, 4) + lax.rem(block, 4)

    def region_of(m, turn):
        return 2 * lax.rem(lax.div(m, 2) + 8 - turn, 4) + lax.rem(m, 2)

    def member_of(q, turn):
        return 2 * lax.rem(lax.div(q, 2) + turn, 4) + lax.rem(q, 2)

    def first_chunk(sim):
        block = lax.div(sim, SUB)
        place = lax.div(lax.rem(sim, SUB), 2) + 1 + 8 - lax.div(block, 4) - lax.rem(block, 4)
        return 2 * lax.rem(place, 4)

    region = region_of(member, turn)
    team = lax.div(member, 2)

    def source(b):
        t = lax.div(b, 4) + lax.rem(b, 4)
        return b * SUB + member_of(lax.div(sim, REGION), t)

    loads = [
        pltpu.make_async_copy(species.at[i, 0], buf.at[pl.ds(8, ROWS), :], load_sem.at[i])
        for i, buf in ((0, sbuf), (1, cbuf))
    ]
    loads[1].start()
    loads[0].start()

    has_prev, has_next = plane > 0, plane < SIMS * GRP - 1
    prev = to(lax.div(plane - 1, GRP), lax.rem(plane - 1 + GRP, GRP))
    nxt = to(lax.div(plane + 1, GRP), lax.rem(plane + 1, GRP))
    barrier = pltpu.get_barrier_semaphore()

    @pl.when(has_prev)
    def _():
        pl.semaphore_signal(barrier, inc=1, device_id=prev, device_id_type=MESH)

    @pl.when(has_next)
    def _():
        pl.semaphore_signal(barrier, inc=1, device_id=nxt, device_id_type=MESH)

    def greet_member(d, _):
        other = lax.rem(seat + d, MEMBERS)
        there = to(block * SUB + lax.div(other, GRP), lax.rem(other, GRP))
        pl.semaphore_signal(barrier, inc=1, device_id=there, device_id_type=MESH)
        return 0

    lax.fori_loop(1, MEMBERS, greet_member, 0)

    def greet_source(b, _):
        there = source(b)

        @pl.when(there != sim)
        def _():
            pl.semaphore_signal(barrier, inc=1, device_id=to(there, grp), device_id_type=MESH)

        return 0

    lax.fori_loop(0, BLOCKS, greet_source, 0)

    for buf in (sbuf, cbuf):
        buf[0:8, :] = jnp.zeros((8, COLS), jnp.float32)
        buf[ROWS + 8 : ROWS + 16, :] = jnp.zeros((8, COLS), jnp.float32)

    @pl.when(plane == 0)
    def _():
        s_up[...] = jnp.zeros_like(s_up)
        c_up[...] = jnp.zeros_like(c_up)

    @pl.when(plane == SIMS * GRP - 1)
    def _():
        s_dn[...] = jnp.zeros_like(s_dn)
        c_dn[...] = jnp.zeros_like(c_dn)

    self_part = lax.div(sim, REGION) == region
    expected = MEMBERS - 1 + BLOCKS - self_part.astype(jnp.int32)
    expected = expected + has_prev.astype(jnp.int32) + has_next.astype(jnp.int32)
    pl.semaphore_wait(barrier, expected)

    def halo(i, way, rows):
        target = ((s_up, s_dn), (c_up, c_dn))[i][way]
        return lambda chunk: pltpu.make_async_remote_copy(
            src_ref=(sbuf, cbuf)[i].at[pl.ds(pl.multiple_of(rows.start + 8, 8), rows.size), :],
            dst_ref=target.at[rows, :],
            send_sem=halo_send.at[i, way],
            recv_sem=halo_recv.at[i, way, chunk],
            device_id=(nxt, prev)[way],
            device_id_type=MESH,
        )

    def chunk_rows(k):
        return pl.ds(pl.multiple_of(k * CHUNK, CHUNK), CHUNK)

    whole = pl.ds(0, ROWS)

    first_next, first_prev = first_chunk(nxt["sim"]), first_chunk(prev["sim"])

    def send_catalyst(n, _):
        @pl.when(has_next)
        def _():
            k = lax.rem(first_next + n, CHUNKS)
            halo(1, 0, chunk_rows(k))(k).start()

        @pl.when(has_prev)
        def _():
            k = lax.rem(first_prev + n, CHUNKS)
            halo(1, 1, chunk_rows(k))(k).start()

        return 0

    loads[1].wait()
    ahead = 2
    lax.fori_loop(0, ahead, send_catalyst, 0)
    loads[0].wait()

    def catalyst_rows(i, _):
        r = pl.multiple_of(8 * i, 8)
        c, lap = in_plane(cbuf, r)
        s = sbuf[pl.ds(pl.multiple_of(r + 8, 8), 8), :]
        c_new[pl.ds(r, 8), :] = c + DIFF_C * lap + s * c * c - (FEED + KILL) * c
        return 0

    lax.fori_loop(0, ROWS // 8, catalyst_rows, 0, unroll=4)

    lane = lax.broadcasted_iota(jnp.int32, (8, 128), 1)
    row = lax.broadcasted_iota(jnp.int32, (8, 128), 0)
    beside = [(0, 0), (2, 0), (1, 127), (4, 0), (3, 127), (6, 0), (5, 127), (7, 127)]

    def mix(k, x, start, length):
        m = member_of(k, turn)
        source_rows = pl.ds(pl.multiple_of((k * GRP + x) * SLOT + start, 8), length)
        target_rows = pl.ds(pl.multiple_of(seat * SLOT + start, 8), length)
        away = pltpu.make_async_remote_copy(
            src_ref=sendbuf.at[source_rows, :],
            dst_ref=recvbuf.at[target_rows, :],
            send_sem=mix_send,
            recv_sem=mix_recv.at[team],
            device_id=to(block * SUB + m, x),
            device_id_type=MESH,
        )
        here = pltpu.make_async_copy(sendbuf.at[source_rows, :], recvbuf.at[target_rows, :], own_sem)
        return away, here

    def send_tiles(k, start, length):
        copies = [mix(k, lax.rem(grp + dx, GRP), start, length) for dx in range(1, GRP + 1)]

        @pl.when(k != region)
        def _():
            for away, _ in copies:
                away.start()

        @pl.when(k == region)
        def _():
            for away, _ in copies[:-1]:
                away.start()
            copies[-1][1].start()

    def rim(k):
        top = c_new[pl.ds(pl.multiple_of(jnp.maximum(k * REGION - 8, 0), 8), 8), :]
        bottom = c_new[pl.ds(pl.multiple_of(jnp.minimum(k * REGION + REGION, ROWS - 8), 8), 8), :]
        above = jnp.where(k == 0, top[0:1], top[7:8])
        below = jnp.where(k == SUB - 1, bottom[7:8], bottom[0:1])
        window = edge_cols[pl.ds(pl.multiple_of(k * REGION, 8), 32), :]
        window = jnp.concatenate([window, jnp.zeros((96, 128), jnp.float32)], axis=0)
        raw = jnp.transpose(window)[0:8]
        cols = pltpu.roll(raw, 121, 1)
        cols = jnp.where((lane == 0) & (k == 0), pltpu.roll(raw, 120, 1), cols)
        cols = jnp.where((lane == REGION + 1) & (k == SUB - 1), pltpu.roll(raw, 122, 1), cols)
        for x in range(GRP):
            c = 2 * x * 128
            tile = pltpu.roll(cols, (4 - 2 * x) % 8, 0)
            tile = jnp.where(row == 0, above[:, c : c + 128], tile)
            tile = jnp.where(row == 1, above[:, c + 128 : c + 256], tile)
            tile = jnp.where(row == 2, below[:, c : c + 128], tile)
            tile = jnp.where(row == 3, below[:, c + 128 : c + 256], tile)
            sendbuf[pl.ds(pl.multiple_of((k * GRP + x) * SLOT + 32, 8), 8), :] = tile

    first = first_chunk(sim)

    def chunk_at(n):
        return lax.rem(first + n, CHUNKS)

    def catalyst_chunk(n, _):
        k = chunk_at(n)

        @pl.when(has_prev)
        def _():
            halo(1, 0, chunk_rows(k))(k).wait_recv()

        @pl.when(has_next)
        def _():
            halo(1, 1, chunk_rows(k))(k).wait_recv()

        @pl.when(n < CHUNKS - ahead)
        def _():
            send_catalyst(n + ahead, 0)

        rim(chunk_at(n + CHUNKS - 2))
        for h in range(CHUNK // 8):
            r = pl.multiple_of(k * CHUNK + 8 * h, 8)
            rows = pl.ds(r, 8)
            new = c_new[rows, :] + DIFF_C * (c_up[rows, :] + c_dn[rows, :])
            c_new[rows, :] = new
            columns = jnp.zeros((8, 128), jnp.float32)
            for i, (tile, at) in enumerate(beside):
                moved = pltpu.roll(new[:, tile * 128 : tile * 128 + 128], (i - at) % 128, 1)
                columns = jnp.where(lane == i, moved, columns)
            edge_cols[pl.ds(pl.multiple_of(r + 8, 8), 8), :] = columns
            for tile in range(COLS // 128):
                slot = (k * GRP + tile // 2) * SLOT + (h * 2 + tile % 2) * 8
                sendbuf[pl.ds(pl.multiple_of(slot, 8), 8), :] = new[:, tile * 128 : tile * 128 + 128]

        send_tiles(k, 0, 32)

        @pl.when(n >= 3)
        def _():
            send_tiles(chunk_at(n - 2), 32, 8)

        return 0

    lax.fori_loop(0, CHUNKS, catalyst_chunk, 0)
    for n in (CHUNKS - 2, CHUNKS - 1, CHUNKS):
        rim(chunk_at(n))
    for n in (CHUNKS - 2, CHUNKS - 1, CHUNKS):
        send_tiles(chunk_at(n), 32, 8)

    store_c = pltpu.make_async_copy(c_new, next_out.at[1, 0], store_sem.at[1])
    store_c.start()

    @pl.when(has_next)
    def _():
        halo(0, 0, whole)(0).start()

    @pl.when(has_prev)
    def _():
        halo(0, 1, whole)(0).start()

    def wait_mixed(count, t):
        some = pl.ds(0, count * SLOT)
        return pltpu.make_async_remote_copy(
            src_ref=sendbuf.at[some, :], dst_ref=recvbuf.at[some, :],
            send_sem=mix_send, recv_sem=mix_recv.at[t], device_id=to(sim, grp), device_id_type=MESH,
        )

    extinct = 6.0 / (BLOCKS * MEMBERS)
    log2e = math.log2(math.e)
    thin, narrow = -extinct * log2e / 256.0, -8.0 * log2e / 256.0

    def render(i, _):
        t_now = lax.rem(team + 6 - i, 4)

        @pl.when(t_now == team)
        def _():
            one_slot = pl.ds(0, SLOT)
            pltpu.make_async_copy(sendbuf.at[one_slot, :], recvbuf.at[one_slot, :], own_sem).wait()
            wait_mixed(TEAM - 1, team).wait_recv()

        @pl.when(t_now != team)
        def _():
            wait_mixed(TEAM, t_now).wait_recv()

        base = t_now * (TEAM * SLOT)
        sides = jnp.concatenate(
            [
                recvbuf[pl.ds(base + 36, TEAM, stride=SLOT), :],
                recvbuf[pl.ds(base + 37, TEAM, stride=SLOT), :],
                jnp.zeros((128 - 2 * TEAM, 128), jnp.float32),
            ],
            axis=0,
        )
        sides = jnp.transpose(sides)

        for h in range(2):
            for par in range(2):
                near = 2 * par + 8 * h
                side = 3.0 * sides[1 + 8 * h : 9 + 8 * h] + sides[near : near + 8]

                def layer(p, sums, h=h, par=par, side=side):
                    at = pl.multiple_of(base + p * SLOT, 8)
                    rim = recvbuf[pl.ds(at + 32, 8), :]
                    rows = []
                    for t in range(2):
                        mine = recvbuf[pl.ds(at + (2 * h + t) * 8, 8), :]
                        across = recvbuf[pl.ds(at + (2 - 2 * h + t) * 8, 8), :]
                        if par == 0:
                            beyond = rim[t : t + 1] if h == 0 else across[7:8]
                            shifted = jnp.where(row == 0, beyond, pltpu.roll(mine, 1, 0))
                        else:
                            beyond = rim[2 + t : 3 + t] if h == 1 else across[0:1]
                            shifted = jnp.where(row == 7, beyond, pltpu.roll(mine, 7, 0))
                        rows.append(3.0 * mine + shifted)
                    leftmost = pltpu.roll(side, (128 - p) % 128, 1)
                    rightmost = pltpu.roll(side, 127 - TEAM - p, 1)
                    fwd = [pltpu.roll(v, 1, 1) for v in rows]
                    bwd = [pltpu.roll(v, 127, 1) for v in rows]
                    low = [jnp.where(lane == 0, leftmost, fwd[0]), jnp.where(lane == 0, fwd[0], fwd[1])]
                    high = [jnp.where(lane == 127, bwd[1], bwd[0]), jnp.where(lane == 127, rightmost, bwd[1])]
                    result = []
                    for cpar in range(2):
                        for t in range(2):
                            q = 3.0 * rows[t] + (low, high)[cpar][t]
                            red, green, blue, clear = sums[(cpar * 2 + t) * 4 : (cpar * 2 + t) * 4 + 4]
                            after = clear * jnp.exp2((q * q) * thin)
                            weight = clear - after
                            mid = q - 8.0
                            warm = mid * (3.0 / 16.0)
                            red = red + weight * jnp.tanh(warm)
                            green = green + weight * jnp.exp2((mid * mid) * narrow)
                            blue = blue + weight * jnp.tanh(warm + 0.6)
                            result += [red, green, blue, after]
                    return tuple(result)

                zero, one = jnp.zeros((8, 128), jnp.float32), jnp.ones((8, 128), jnp.float32)
                sums = (zero, zero, zero, one) * 4
                for p in range(TEAM):
                    sums = layer(p, sums)
                for j in range(16):
                    at = t_now * TOTALS + ((h * 2 + par) * 16 + j) * 8
                    totals[pl.ds(pl.multiple_of(at, 8), 8), :] = sums[j]
        return 0

    lax.fori_loop(0, 4, render, 0)

    def piece_rows(n):
        return pl.ds(pl.multiple_of(n * PIECE, PIECE), PIECE)

    for h in range(2):
        for par in range(2):
            for cpar in range(2):
                for t in range(2):
                    base = ((h * 2 + par) * 16 + (cpar * 2 + t) * 4) * 8
                    got = [[totals[i * TOTALS + base + 8 * ch : i * TOTALS + base + 8 * ch + 8, :] for ch in range(4)] for i in range(4)]
                    red, green, blue, clear = got[0]
                    for i in range(1, 4):
                        red = red + clear * got[i][0]
                        green = green + clear * got[i][1]
                        blue = blue + clear * got[i][2]
                        clear = clear * got[i][3]
                    for ch, value in enumerate((red, green, blue, clear)):
                        at = 8 * h * PIECE + ch * 8 + cpar * 4 + par * 2 + t
                        pack[pl.ds(at, 8, stride=PIECE), :] = value

        def send_piece(n, _, h=h):
            j = 8 * h + lax.rem(n + sim, 8)
            there = region * REGION + j

            @pl.when(there != sim)
            def _():
                pltpu.make_async_remote_copy(
                    src_ref=pack.at[piece_rows(j), :],
                    dst_ref=parts.at[piece_rows(block), :],
                    send_sem=part_send,
                    recv_sem=part_recv,
                    device_id=to(there, grp),
                    device_id_type=MESH,
                ).start()

            return 0

        lax.fori_loop(0, 8, send_piece, 0)

    @pl.when(self_part)
    def _():
        mine = pltpu.make_async_copy(
            pack.at[piece_rows(lax.rem(sim, REGION)), :], parts.at[piece_rows(block), :], part_own
        )
        mine.start()
        mine.wait()

    @pl.when(has_prev)
    def _():
        halo(0, 0, whole)(0).wait_recv()

    @pl.when(has_next)
    def _():
        halo(0, 1, whole)(0).wait_recv()

    def substrate_rows(k, _):
        r = pl.multiple_of(8 * k, 8)
        rows = pl.ds(r, 8)
        s, lap = in_plane(sbuf, r)
        lap = lap + s_up[rows, :] + s_dn[rows, :]
        c = cbuf[pl.ds(pl.multiple_of(r + 8, 8), 8), :]
        s_new[rows, :] = s + DIFF_S * lap - s * c * c + FEED * (1.0 - s)
        return 0

    lax.fori_loop(0, ROWS // 8, substrate_rows, 0, unroll=4)
    store_s = pltpu.make_async_copy(s_new, next_out.at[0, 0], store_sem.at[0])
    store_s.start()

    old = lax.broadcasted_iota(jnp.int32, (256, 256), 0)
    new = lax.broadcasted_iota(jnp.int32, (256, 256), 1)
    spread = jnp.where(new == 2 * lax.rem(old, 128) + lax.div(old, 128), 1.0, 0.0).astype(jnp.bfloat16)

    def wait_parts(count):
        some = pl.ds(0, count * PIECE)
        return pltpu.make_async_remote_copy(
            src_ref=pack.at[some, :], dst_ref=parts.at[some, :],
            send_sem=part_send, recv_sem=part_recv, device_id=to(sim, grp), device_id_type=MESH,
        )

    @pl.when(self_part)
    def _():
        wait_parts(BLOCKS - 1).wait_recv()

    @pl.when(jnp.logical_not(self_part))
    def _():
        wait_parts(BLOCKS).wait_recv()

    def add_block(b, totals):
        base = pl.multiple_of(b * PIECE, 8)
        red, green, blue, clear = totals
        got = [parts[pl.ds(base + 8 * ch, 8), :] for ch in range(4)]
        return (
            red + clear * got[0], green + clear * got[1], blue + clear * got[2], clear * got[3],
        )

    zero, one = jnp.zeros((8, 128), jnp.float32), jnp.ones((8, 128), jnp.float32)
    red, green, blue, clear = lax.fori_loop(0, BLOCKS, add_block, (zero, zero, zero, one), unroll=True)
    opaque = 1.0 - clear
    channels = [0.5 * (opaque + red), green, 0.5 * (opaque - blue), opaque]
    flat = jnp.concatenate([jnp.concatenate([v[0:4], v[4:8]], axis=1) for v in channels], axis=0)
    bf16 = jnp.bfloat16
    high = flat.astype(bf16)
    rest = flat - high.astype(jnp.float32)
    middle = rest.astype(bf16)
    low = (rest - middle.astype(jnp.float32)).astype(bf16)
    split = jnp.dot(
        jnp.concatenate([high, middle, low], axis=0), spread, preferred_element_type=jnp.float32
    )
    mixed = split[0:16] + (split[16:32] + split[32:48])
    for ch in range(4):
        for par in range(2):
            for t in range(2):
                n = ch * 4 + par * 2 + t
                frame_out[ch, par : par + 1, t * 256 : t * 256 + 256] = mixed[n : n + 1]

    for i in range(2):
        @pl.when(has_next)
        def _(i=i):
            halo(i, 0, whole)(0).wait_send()

        @pl.when(has_prev)
        def _(i=i):
            halo(i, 1, whole)(0).wait_send()

    wait_mixed(MEMBERS - 1, team).wait_send()

    @pl.when(self_part)
    def _():
        wait_parts(BLOCKS - 1).wait_send()

    @pl.when(jnp.logical_not(self_part))
    def _():
        wait_parts(BLOCKS).wait_send()

    store_c.wait()
    store_s.wait()


def shards(species):
    f32 = jnp.float32
    plane = pltpu.VMEM((ROWS, COLS), f32)
    padded = pltpu.VMEM((ROWS + 16, COLS), f32)
    dma = pltpu.SemaphoreType.DMA
    fresh, frame = pl.pallas_call(
        kernel,
        out_shape=(
            jax.ShapeDtypeStruct((2, 1, ROWS, COLS), f32),
            jax.ShapeDtypeStruct((4, 2 * ROWS // SIMS, 2 * COLS // GRP), f32),
        ),
        in_specs=[pl.BlockSpec(memory_space=pltpu.HBM)],
        out_specs=(pl.BlockSpec(memory_space=pl.ANY), pl.BlockSpec(memory_space=pltpu.VMEM)),
        scratch_shapes=[
            padded, padded, plane, plane, plane, plane,
            plane, plane,
            pltpu.VMEM((ROWS + 16, 128), f32),
            pltpu.VMEM((MEMBERS * SLOT, 128), f32),
            pltpu.VMEM((MEMBERS * SLOT, 128), f32),
            pltpu.VMEM((4 * TOTALS, 128), f32),
            pltpu.VMEM((REGION * PIECE, 128), f32),
            pltpu.VMEM((BLOCKS * PIECE, 128), f32),
            dma((2,)), dma((2,)), dma((2, 2)), dma((2, 2, CHUNKS)),
            dma, dma, dma((4,)), dma, dma, dma,
        ],
        compiler_params=pltpu.CompilerParams(
            collective_id=0, has_side_effects=True, vmem_limit_bytes=32 * 1024 * 1024
        ),
        cost_estimate=pl.CostEstimate(flops=20_000_000, bytes_accessed=4_000_000, transcendentals=2_000_000),
    )(pltpu.with_memory_space_constraint(species, pltpu.HBM))
    return fresh, frame


def solution(mesh):
    return jax.shard_map(
        shards,
        mesh=mesh,
        in_specs=(P(None, ("sim", "grp"), None, None),),
        out_specs=(P(None, ("sim", "grp"), None, None), P(None, "sim", "grp")),
        check_vma=False,
    )
```

```python
import math

import jax
import jax.numpy as jnp
from jax import lax
from jax.experimental import pallas as pl
from jax.experimental.pallas import tpu as pltpu
from jax.sharding import PartitionSpec as P

MESH = pl.DeviceIdType.MESH

ROWS = 128
COLS = 1024
GRP = 4
SIMS = 128
SUB = 8
BLOCKS = SIMS // SUB
MEMBERS = GRP * SUB
REGION = ROWS // SUB
CHUNKS = 8
CHUNK = ROWS // CHUNKS
SLOT = 40
PIECE = 32
TEAM = MEMBERS // 4
TOTALS = 64 * 8

DIFF_S, DIFF_C, FEED, KILL = 0.16, 0.08, 0.035, 0.065


def to(sim, grp):
    return {"sim": sim, "grp": grp}


def laplacian(buf, up, dn, r):
    window = buf[pl.ds(r, 24), :]
    center = window[8:16]
    lane = lax.broadcasted_iota(jnp.int32, (8, COLS), 1)
    left = jnp.where(lane == 0, 0.0, pltpu.roll(center, 1, 1))
    right = jnp.where(lane == COLS - 1, 0.0, pltpu.roll(center, COLS - 1, 1))
    total = up[pl.ds(r, 8), :] + dn[pl.ds(r, 8), :]
    total = total + window[7:15] + window[9:17] + left + right
    return center, total - 6.0 * center


def kernel(
    species, next_out, frame_out,
    sbuf, cbuf, s_up, s_dn, c_up, c_dn, s_new, c_new, edge_cols, sendbuf, recvbuf, totals, pack, parts,
    load_sem, store_sem, halo_send, halo_recv, own_sem, mix_send, mix_recv, part_own, part_send, part_recv,
):
    sim, grp = lax.axis_index("sim"), lax.axis_index("grp")
    plane = sim * GRP + grp
    block, member = lax.div(sim, SUB), lax.rem(sim, SUB)
    seat = member * GRP + grp
    turn = lax.div(block, 4) + lax.rem(block, 4)

    def region_of(m, turn):
        return 2 * lax.rem(lax.div(m, 2) + 8 - turn, 4) + lax.rem(m, 2)

    def member_of(q, turn):
        return 2 * lax.rem(lax.div(q, 2) + turn, 4) + lax.rem(q, 2)

    def first_chunk(sim):
        block = lax.div(sim, SUB)
        place = lax.div(lax.rem(sim, SUB), 2) + 1 + 8 - lax.div(block, 4) - lax.rem(block, 4)
        return 2 * lax.rem(place, 4)

    region = region_of(member, turn)
    team = lax.div(member, 2)

    def source(b):
        t = lax.div(b, 4) + lax.rem(b, 4)
        return b * SUB + member_of(lax.div(sim, REGION), t)

    loads = [
        pltpu.make_async_copy(species.at[i, 0], buf.at[pl.ds(8, ROWS), :], load_sem.at[i])
        for i, buf in ((0, sbuf), (1, cbuf))
    ]
    loads[1].start()
    loads[0].start()

    has_prev, has_next = plane > 0, plane < SIMS * GRP - 1
    prev = to(lax.div(plane - 1, GRP), lax.rem(plane - 1 + GRP, GRP))
    nxt = to(lax.div(plane + 1, GRP), lax.rem(plane + 1, GRP))
    barrier = pltpu.get_barrier_semaphore()

    @pl.when(has_prev)
    def _():
        pl.semaphore_signal(barrier, inc=1, device_id=prev, device_id_type=MESH)

    @pl.when(has_next)
    def _():
        pl.semaphore_signal(barrier, inc=1, device_id=nxt, device_id_type=MESH)

    def greet_member(d, _):
        other = lax.rem(seat + d, MEMBERS)
        there = to(block * SUB + lax.div(other, GRP), lax.rem(other, GRP))
        pl.semaphore_signal(barrier, inc=1, device_id=there, device_id_type=MESH)
        return 0

    lax.fori_loop(1, MEMBERS, greet_member, 0)

    def greet_source(b, _):
        there = source(b)

        @pl.when(there != sim)
        def _():
            pl.semaphore_signal(barrier, inc=1, device_id=to(there, grp), device_id_type=MESH)

        return 0

    lax.fori_loop(0, BLOCKS, greet_source, 0)

    for buf in (sbuf, cbuf):
        buf[0:8, :] = jnp.zeros((8, COLS), jnp.float32)
        buf[ROWS + 8 : ROWS + 16, :] = jnp.zeros((8, COLS), jnp.float32)

    @pl.when(plane == 0)
    def _():
        s_up[...] = jnp.zeros_like(s_up)
        c_up[...] = jnp.zeros_like(c_up)

    @pl.when(plane == SIMS * GRP - 1)
    def _():
        s_dn[...] = jnp.zeros_like(s_dn)
        c_dn[...] = jnp.zeros_like(c_dn)

    self_part = lax.div(sim, REGION) == region
    expected = MEMBERS - 1 + BLOCKS - self_part.astype(jnp.int32)
    expected = expected + has_prev.astype(jnp.int32) + has_next.astype(jnp.int32)
    pl.semaphore_wait(barrier, expected)

    def halo(i, way, rows):
        target = ((s_up, s_dn), (c_up, c_dn))[i][way]
        return lambda chunk: pltpu.make_async_remote_copy(
            src_ref=species.at[i, 0, rows, :],
            dst_ref=target.at[rows, :],
            send_sem=halo_send.at[i, way],
            recv_sem=halo_recv.at[i, way, chunk],
            device_id=(nxt, prev)[way],
            device_id_type=MESH,
        )

    def chunk_rows(k):
        return pl.ds(pl.multiple_of(k * CHUNK, CHUNK), CHUNK)

    whole = pl.ds(0, ROWS)

    first_next, first_prev = first_chunk(nxt["sim"]), first_chunk(prev["sim"])

    def send_catalyst(n, _):
        @pl.when(has_next)
        def _():
            k = lax.rem(first_next + n, CHUNKS)
            halo(1, 0, chunk_rows(k))(k).start()

        @pl.when(has_prev)
        def _():
            k = lax.rem(first_prev + n, CHUNKS)
            halo(1, 1, chunk_rows(k))(k).start()

        return 0

    lax.fori_loop(0, CHUNKS, send_catalyst, 0)
    loads[1].wait()
    loads[0].wait()

    lane = lax.broadcasted_iota(jnp.int32, (8, 128), 1)
    row = lax.broadcasted_iota(jnp.int32, (8, 128), 0)
    beside = [(0, 0), (2, 0), (1, 127), (4, 0), (3, 127), (6, 0), (5, 127), (7, 127)]

    def mix(k, x, start, length):
        m = member_of(k, turn)
        source_rows = pl.ds(pl.multiple_of((k * GRP + x) * SLOT + start, 8), length)
        target_rows = pl.ds(pl.multiple_of(seat * SLOT + start, 8), length)
        away = pltpu.make_async_remote_copy(
            src_ref=sendbuf.at[source_rows, :],
            dst_ref=recvbuf.at[target_rows, :],
            send_sem=mix_send,
            recv_sem=mix_recv.at[team],
            device_id=to(block * SUB + m, x),
            device_id_type=MESH,
        )
        here = pltpu.make_async_copy(sendbuf.at[source_rows, :], recvbuf.at[target_rows, :], own_sem)
        return away, here, m * GRP + x == seat

    def send_tiles(k, start, length):
        for dx in range(1, GRP + 1):
            away, here, stays = mix(k, lax.rem(grp + dx, GRP), start, length)

            @pl.when(stays)
            def _(here=here):
                here.start()

            @pl.when(jnp.logical_not(stays))
            def _(away=away):
                away.start()

    def send_rim(k):
        top = c_new[pl.ds(pl.multiple_of(jnp.maximum(k * REGION - 8, 0), 8), 8), :]
        bottom = c_new[pl.ds(pl.multiple_of(jnp.minimum(k * REGION + REGION, ROWS - 8), 8), 8), :]
        above = jnp.where(k == 0, top[0:1], top[7:8])
        below = jnp.where(k == SUB - 1, bottom[7:8], bottom[0:1])
        window = edge_cols[pl.ds(pl.multiple_of(k * REGION, 8), 32), :]
        window = jnp.concatenate([window, jnp.zeros((96, 128), jnp.float32)], axis=0)
        cols = pltpu.roll(jnp.transpose(window)[0:8], 121, 1)
        for x in range(GRP):
            c = 2 * x * 128
            tile = pltpu.roll(cols, (4 - 2 * x) % 8, 0)
            tile = jnp.where(row == 0, above[:, c : c + 128], tile)
            tile = jnp.where(row == 1, above[:, c + 128 : c + 256], tile)
            tile = jnp.where(row == 2, below[:, c : c + 128], tile)
            tile = jnp.where(row == 3, below[:, c + 128 : c + 256], tile)
            sendbuf[pl.ds(pl.multiple_of((k * GRP + x) * SLOT + 32, 8), 8), :] = tile
        send_tiles(k, 32, 8)

    first = first_chunk(sim)

    def catalyst_chunk(n, _):
        k = lax.rem(first + n, CHUNKS)

        @pl.when(has_prev)
        def _():
            halo(1, 0, chunk_rows(k))(k).wait_recv()

        @pl.when(has_next)
        def _():
            halo(1, 1, chunk_rows(k))(k).wait_recv()

        for h in range(CHUNK // 8):
            r = pl.multiple_of(k * CHUNK + 8 * h, 8)
            c, lap = laplacian(cbuf, c_up, c_dn, r)
            s = sbuf[pl.ds(pl.multiple_of(r + 8, 8), 8), :]
            new = c + DIFF_C * lap + s * c * c - (FEED + KILL) * c
            c_new[pl.ds(r, 8), :] = new
            columns = jnp.zeros((8, 128), jnp.float32)
            for i, (tile, at) in enumerate(beside):
                moved = pltpu.roll(new[:, tile * 128 : tile * 128 + 128], (i - at) % 128, 1)
                columns = jnp.where(lane == i, moved, columns)
            edge_cols[pl.ds(pl.multiple_of(r + 8, 8), 8), :] = columns
            if h == 0:
                @pl.when(k == 0)
                def _(columns=columns):
                    edge_cols[0:8, :] = jnp.broadcast_to(columns[0:1], (8, 128))
            else:
                @pl.when(k == CHUNKS - 1)
                def _(columns=columns):
                    edge_cols[ROWS + 8 : ROWS + 16, :] = jnp.broadcast_to(columns[7:8], (8, 128))
            for tile in range(COLS // 128):
                slot = (k * GRP + tile // 2) * SLOT + (h * 2 + tile % 2) * 8
                sendbuf[pl.ds(pl.multiple_of(slot, 8), 8), :] = new[:, tile * 128 : tile * 128 + 128]

        send_tiles(k, 0, 32)

        @pl.when(n >= 2)
        def _():
            send_rim(lax.rem(first + n - 1, CHUNKS))

        return 0

    lax.fori_loop(0, CHUNKS, catalyst_chunk, 0)
    last_rims = lambda n, _: (send_rim(lax.rem(first + CHUNKS - 1 + n, CHUNKS)), 0)[1]
    lax.fori_loop(0, 2, last_rims, 0)

    store_c = pltpu.make_async_copy(c_new, next_out.at[1, 0], store_sem.at[1])
    store_c.start()

    @pl.when(has_next)
    def _():
        halo(0, 0, whole)(0).start()

    @pl.when(has_prev)
    def _():
        halo(0, 1, whole)(0).start()

    def wait_mixed(count, t):
        some = pl.ds(0, count * SLOT)
        return pltpu.make_async_remote_copy(
            src_ref=sendbuf.at[some, :], dst_ref=recvbuf.at[some, :],
            send_sem=mix_send, recv_sem=mix_recv.at[t], device_id=to(sim, grp), device_id_type=MESH,
        )

    extinct = 6.0 / (BLOCKS * MEMBERS)
    log2e = math.log2(math.e)
    thin, narrow = -extinct * log2e / 256.0, -8.0 * log2e / 256.0

    def render(i, _):
        t_now = lax.rem(team + 6 - i, 4)

        @pl.when(t_now == team)
        def _():
            one_slot = pl.ds(0, SLOT)
            pltpu.make_async_copy(sendbuf.at[one_slot, :], recvbuf.at[one_slot, :], own_sem).wait()
            wait_mixed(TEAM - 1, team).wait_recv()

        @pl.when(t_now != team)
        def _():
            wait_mixed(TEAM, t_now).wait_recv()

        base = t_now * (TEAM * SLOT)
        sides = jnp.concatenate(
            [
                recvbuf[pl.ds(base + 36, TEAM, stride=SLOT), :],
                recvbuf[pl.ds(base + 37, TEAM, stride=SLOT), :],
                jnp.zeros((128 - 2 * TEAM, 128), jnp.float32),
            ],
            axis=0,
        )
        sides = jnp.transpose(sides)

        for h in range(2):
            for par in range(2):
                near = 2 * par + 8 * h
                side = 3.0 * sides[1 + 8 * h : 9 + 8 * h] + sides[near : near + 8]

                def layer(p, sums, h=h, par=par, side=side):
                    at = pl.multiple_of(base + p * SLOT, 8)
                    rim = recvbuf[pl.ds(at + 32, 8), :]
                    rows = []
                    for t in range(2):
                        mine = recvbuf[pl.ds(at + (2 * h + t) * 8, 8), :]
                        across = recvbuf[pl.ds(at + (2 - 2 * h + t) * 8, 8), :]
                        if par == 0:
                            beyond = rim[t : t + 1] if h == 0 else across[7:8]
                            shifted = jnp.where(row == 0, beyond, pltpu.roll(mine, 1, 0))
                        else:
                            beyond = rim[2 + t : 3 + t] if h == 1 else across[0:1]
                            shifted = jnp.where(row == 7, beyond, pltpu.roll(mine, 7, 0))
                        rows.append(3.0 * mine + shifted)
                    leftmost = pltpu.roll(side, lax.rem(128 - p, 128), 1)
                    rightmost = pltpu.roll(side, 127 - TEAM - p, 1)
                    fwd = [pltpu.roll(v, 1, 1) for v in rows]
                    bwd = [pltpu.roll(v, 127, 1) for v in rows]
                    low = [jnp.where(lane == 0, leftmost, fwd[0]), jnp.where(lane == 0, fwd[0], fwd[1])]
                    high = [jnp.where(lane == 127, bwd[1], bwd[0]), jnp.where(lane == 127, rightmost, bwd[1])]
                    result = []
                    for cpar in range(2):
                        for t in range(2):
                            q = 3.0 * rows[t] + (low, high)[cpar][t]
                            red, green, blue, clear = sums[(cpar * 2 + t) * 4 : (cpar * 2 + t) * 4 + 4]
                            after = clear * jnp.exp2((q * q) * thin)
                            weight = clear - after
                            mid = q - 8.0
                            warm = mid * (3.0 / 16.0)
                            red = red + weight * jnp.tanh(warm)
                            green = green + weight * jnp.exp2((mid * mid) * narrow)
                            blue = blue + weight * jnp.tanh(warm + 0.6)
                            result += [red, green, blue, after]
                    return tuple(result)

                zero, one = jnp.zeros((8, 128), jnp.float32), jnp.ones((8, 128), jnp.float32)
                sums = lax.fori_loop(0, TEAM, layer, (zero, zero, zero, one) * 4, unroll=True)
                for j in range(16):
                    at = t_now * TOTALS + ((h * 2 + par) * 16 + j) * 8
                    totals[pl.ds(pl.multiple_of(at, 8), 8), :] = sums[j]
        return 0

    lax.fori_loop(0, 4, render, 0)

    for h in range(2):
        for par in range(2):
            for cpar in range(2):
                for t in range(2):
                    base = ((h * 2 + par) * 16 + (cpar * 2 + t) * 4) * 8
                    got = [[totals[i * TOTALS + base + 8 * ch : i * TOTALS + base + 8 * ch + 8, :] for ch in range(4)] for i in range(4)]
                    red, green, blue, clear = got[0]
                    for i in range(1, 4):
                        red = red + clear * got[i][0]
                        green = green + clear * got[i][1]
                        blue = blue + clear * got[i][2]
                        clear = clear * got[i][3]
                    for ch, value in enumerate((red, green, blue, clear)):
                        at = 8 * h * PIECE + ch * 8 + cpar * 4 + par * 2 + t
                        pack[pl.ds(at, 8, stride=PIECE), :] = value

    def piece_rows(n):
        return pl.ds(pl.multiple_of(n * PIECE, PIECE), PIECE)

    def send_piece(n, _):
        j = n + lax.rem(region, 2) * (REGION - 1 - 2 * n)
        there = region * REGION + j

        @pl.when(there != sim)
        def _():
            pltpu.make_async_remote_copy(
                src_ref=pack.at[piece_rows(j), :],
                dst_ref=parts.at[piece_rows(block), :],
                send_sem=part_send,
                recv_sem=part_recv,
                device_id=to(there, grp),
                device_id_type=MESH,
            ).start()

        return 0

    lax.fori_loop(0, REGION, send_piece, 0)

    @pl.when(self_part)
    def _():
        mine = pltpu.make_async_copy(
            pack.at[piece_rows(lax.rem(sim, REGION)), :], parts.at[piece_rows(block), :], part_own
        )
        mine.start()
        mine.wait()

    @pl.when(has_prev)
    def _():
        halo(0, 0, whole)(0).wait_recv()

    @pl.when(has_next)
    def _():
        halo(0, 1, whole)(0).wait_recv()

    def substrate_rows(k, _):
        r = pl.multiple_of(8 * k, 8)
        s, lap = laplacian(sbuf, s_up, s_dn, r)
        c = cbuf[pl.ds(pl.multiple_of(r + 8, 8), 8), :]
        s_new[pl.ds(r, 8), :] = s + DIFF_S * lap - s * c * c + FEED * (1.0 - s)
        return 0

    lax.fori_loop(0, ROWS // 8, substrate_rows, 0, unroll=4)
    store_s = pltpu.make_async_copy(s_new, next_out.at[0, 0], store_sem.at[0])
    store_s.start()

    old = lax.broadcasted_iota(jnp.int32, (256, 256), 0)
    new = lax.broadcasted_iota(jnp.int32, (256, 256), 1)
    spread = jnp.where(new == 2 * lax.rem(old, 128) + lax.div(old, 128), 1.0, 0.0).astype(jnp.bfloat16)

    def wait_parts(count):
        some = pl.ds(0, count * PIECE)
        return pltpu.make_async_remote_copy(
            src_ref=pack.at[some, :], dst_ref=parts.at[some, :],
            send_sem=part_send, recv_sem=part_recv, device_id=to(sim, grp), device_id_type=MESH,
        )

    @pl.when(self_part)
    def _():
        wait_parts(BLOCKS - 1).wait_recv()

    @pl.when(jnp.logical_not(self_part))
    def _():
        wait_parts(BLOCKS).wait_recv()

    def add_block(b, totals):
        base = pl.multiple_of(b * PIECE, 8)
        red, green, blue, clear = totals
        got = [parts[pl.ds(base + 8 * ch, 8), :] for ch in range(4)]
        return (
            red + clear * got[0], green + clear * got[1], blue + clear * got[2], clear * got[3],
        )

    zero, one = jnp.zeros((8, 128), jnp.float32), jnp.ones((8, 128), jnp.float32)
    red, green, blue, clear = lax.fori_loop(0, BLOCKS, add_block, (zero, zero, zero, one), unroll=True)
    opaque = 1.0 - clear
    channels = [0.5 * (opaque + red), green, 0.5 * (opaque - blue), opaque]
    flat = jnp.concatenate([jnp.concatenate([v[0:4], v[4:8]], axis=1) for v in channels], axis=0)
    bf16 = jnp.bfloat16
    high = flat.astype(bf16)
    rest = flat - high.astype(jnp.float32)
    middle = rest.astype(bf16)
    low = (rest - middle.astype(jnp.float32)).astype(bf16)
    split = jnp.dot(
        jnp.concatenate([high, middle, low], axis=0), spread, preferred_element_type=jnp.float32
    )
    mixed = split[0:16] + (split[16:32] + split[32:48])
    for ch in range(4):
        for par in range(2):
            for t in range(2):
                n = ch * 4 + par * 2 + t
                frame_out[ch, par : par + 1, t * 256 : t * 256 + 256] = mixed[n : n + 1]

    for i in range(2):
        @pl.when(has_next)
        def _(i=i):
            halo(i, 0, whole)(0).wait_send()

        @pl.when(has_prev)
        def _(i=i):
            halo(i, 1, whole)(0).wait_send()

    wait_mixed(MEMBERS - 1, team).wait_send()

    @pl.when(self_part)
    def _():
        wait_parts(BLOCKS - 1).wait_send()

    @pl.when(jnp.logical_not(self_part))
    def _():
        wait_parts(BLOCKS).wait_send()

    store_c.wait()
    store_s.wait()


def shards(species):
    f32 = jnp.float32
    plane = pltpu.VMEM((ROWS, COLS), f32)
    padded = pltpu.VMEM((ROWS + 16, COLS), f32)
    dma = pltpu.SemaphoreType.DMA
    fresh, frame = pl.pallas_call(
        kernel,
        out_shape=(
            jax.ShapeDtypeStruct((2, 1, ROWS, COLS), f32),
            jax.ShapeDtypeStruct((4, 2 * ROWS // SIMS, 2 * COLS // GRP), f32),
        ),
        in_specs=[pl.BlockSpec(memory_space=pltpu.HBM)],
        out_specs=(pl.BlockSpec(memory_space=pl.ANY), pl.BlockSpec(memory_space=pltpu.VMEM)),
        scratch_shapes=[
            padded, padded, plane, plane, plane, plane,
            plane, plane,
            pltpu.VMEM((ROWS + 16, 128), f32),
            pltpu.VMEM((MEMBERS * SLOT, 128), f32),
            pltpu.VMEM((MEMBERS * SLOT, 128), f32),
            pltpu.VMEM((4 * TOTALS, 128), f32),
            pltpu.VMEM((REGION * PIECE, 128), f32),
            pltpu.VMEM((BLOCKS * PIECE, 128), f32),
            dma((2,)), dma((2,)), dma((2, 2)), dma((2, 2, CHUNKS)),
            dma, dma, dma((4,)), dma, dma, dma,
        ],
        compiler_params=pltpu.CompilerParams(
            collective_id=0, has_side_effects=True, vmem_limit_bytes=32 * 1024 * 1024
        ),
        cost_estimate=pl.CostEstimate(flops=20_000_000, bytes_accessed=4_000_000, transcendentals=2_000_000),
    )(pltpu.with_memory_space_constraint(species, pltpu.HBM))
    return fresh, frame


def solution(mesh):
    return jax.shard_map(
        shards,
        mesh=mesh,
        in_specs=(P(None, ("sim", "grp"), None, None),),
        out_specs=(P(None, ("sim", "grp"), None, None), P(None, "sim", "grp")),
        check_vma=False,
    )
```

```python
import math

import jax
import jax.numpy as jnp
from jax import lax
from jax.experimental import pallas as pl
from jax.experimental.pallas import tpu as pltpu
from jax.sharding import PartitionSpec as P

MESH = pl.DeviceIdType.MESH

ROWS = 128
COLS = 1024
GRP = 4
SIMS = 128
SUB = 8
BLOCKS = SIMS // SUB
MEMBERS = GRP * SUB
REGION = ROWS // SUB
CHUNKS = 8
CHUNK = ROWS // CHUNKS
SLOT = 40
PIECE = 32
TEAM = MEMBERS // 4
TOTALS = 64 * 8

DIFF_S, DIFF_C, FEED, KILL = 0.16, 0.08, 0.035, 0.065


def to(sim, grp):
    return {"sim": sim, "grp": grp}


def laplacian(buf, up, dn, r):
    window = buf[pl.ds(r, 24), :]
    center = window[8:16]
    lane = lax.broadcasted_iota(jnp.int32, (8, COLS), 1)
    left = jnp.where(lane == 0, 0.0, pltpu.roll(center, 1, 1))
    right = jnp.where(lane == COLS - 1, 0.0, pltpu.roll(center, COLS - 1, 1))
    total = up[pl.ds(r, 8), :] + dn[pl.ds(r, 8), :]
    total = total + window[7:15] + window[9:17] + left + right
    return center, total - 6.0 * center


def kernel(
    species, next_out, frame_out,
    sbuf, cbuf, s_up, s_dn, c_up, c_dn, passing, c_new, edge_cols, sendbuf, recvbuf, totals, pack, parts,
    load_sem, halo_send, halo_recv, relay_send, relay_recv, own_sem, mix_send, mix_recv, part_own, part_send, part_recv,
):
    sim, grp = lax.axis_index("sim"), lax.axis_index("grp")
    plane = sim * GRP + grp
    block, member = lax.div(sim, SUB), lax.rem(sim, SUB)
    seat = member * GRP + grp
    turn = lax.div(block, 4) + lax.rem(block, 4)

    def region_of(m, turn):
        return 2 * lax.rem(lax.div(m, 2) + 8 - turn, 4) + lax.rem(m, 2)

    def member_of(q, turn):
        return 2 * lax.rem(lax.div(q, 2) + turn, 4) + lax.rem(q, 2)

    def first_chunk(sim):
        block = lax.div(sim, SUB)
        place = lax.div(lax.rem(sim, SUB), 2) + 1 + 8 - lax.div(block, 4) - lax.rem(block, 4)
        return 2 * lax.rem(place, 4)

    region = region_of(member, turn)
    team = lax.div(member, 2)

    def source(b):
        t = lax.div(b, 4) + lax.rem(b, 4)
        return b * SUB + member_of(lax.div(sim, REGION), t)

    loads = [
        pltpu.make_async_copy(species.at[i, 0], buf.at[pl.ds(8, ROWS), :], load_sem.at[i])
        for i, buf in ((0, sbuf), (1, cbuf))
    ]
    loads[1].start()
    loads[0].start()

    has_prev, has_next = plane > 0, plane < SIMS * GRP - 1
    prev = to(lax.div(plane - 1, GRP), lax.rem(plane - 1 + GRP, GRP))
    nxt = to(lax.div(plane + 1, GRP), lax.rem(plane + 1, GRP))

    odd = lax.rem(sim, 2)
    partner = to(sim + 2 * odd - 1, grp)
    crossing = (sim + odd > 0) & (sim + odd < SIMS)
    is_a, is_b = crossing & (odd == 1) & (grp == GRP - 1), crossing & (odd == 0) & (grp == 0)
    is_relay = crossing & (((odd == 0) & (grp == GRP - 1)) | ((odd == 1) & (grp == 0)))
    passes_up = is_relay & (odd == 0)
    passes_down = is_relay & (odd == 1)
    relayed_to = to(sim, GRP - 1 - grp)
    barrier = pltpu.get_barrier_semaphore()

    @pl.when(has_prev)
    def _():
        pl.semaphore_signal(barrier, inc=1, device_id=prev, device_id_type=MESH)

    @pl.when(has_next)
    def _():
        pl.semaphore_signal(barrier, inc=1, device_id=nxt, device_id_type=MESH)

    @pl.when(is_relay)
    def _():
        pl.semaphore_signal(barrier, inc=1, device_id=partner, device_id_type=MESH)

    def greet_member(d, _):
        other = lax.rem(seat + d, MEMBERS)
        there = to(block * SUB + lax.div(other, GRP), lax.rem(other, GRP))
        pl.semaphore_signal(barrier, inc=1, device_id=there, device_id_type=MESH)
        return 0

    lax.fori_loop(1, MEMBERS, greet_member, 0)

    def greet_source(b, _):
        there = source(b)

        @pl.when(there != sim)
        def _():
            pl.semaphore_signal(barrier, inc=1, device_id=to(there, grp), device_id_type=MESH)

        return 0

    lax.fori_loop(0, BLOCKS, greet_source, 0)

    for buf in (sbuf, cbuf):
        buf[0:8, :] = jnp.zeros((8, COLS), jnp.float32)
        buf[ROWS + 8 : ROWS + 16, :] = jnp.zeros((8, COLS), jnp.float32)

    @pl.when(plane == 0)
    def _():
        s_up[...] = jnp.zeros_like(s_up)
        c_up[...] = jnp.zeros_like(c_up)

    @pl.when(plane == SIMS * GRP - 1)
    def _():
        s_dn[...] = jnp.zeros_like(s_dn)
        c_dn[...] = jnp.zeros_like(c_dn)

    self_part = lax.div(sim, REGION) == region
    expected = MEMBERS - 1 + BLOCKS - self_part.astype(jnp.int32)
    for wanted in (has_prev, has_next, is_a, is_b):
        expected = expected + wanted.astype(jnp.int32)
    pl.semaphore_wait(barrier, expected)

    def halo(i, way, rows):
        target = ((s_up, s_dn), (c_up, c_dn))[i][way]
        return lambda chunk: pltpu.make_async_remote_copy(
            src_ref=species.at[i, 0, rows, :],
            dst_ref=target.at[rows, :],
            send_sem=halo_send.at[i, way],
            recv_sem=halo_recv.at[i, way, chunk],
            device_id=(nxt, prev)[way],
            device_id_type=MESH,
        )

    def chunk_rows(k):
        return pl.ds(pl.multiple_of(k * CHUNK, CHUNK), CHUNK)

    whole = pl.ds(0, ROWS)

    first_next, first_prev = first_chunk(nxt["sim"]), first_chunk(prev["sim"])

    def send_catalyst(n, _):
        @pl.when(has_next)
        def _():
            k = lax.rem(first_next + n, CHUNKS)
            halo(1, 0, chunk_rows(k))(k).start()

        @pl.when(has_prev)
        def _():
            k = lax.rem(first_prev + n, CHUNKS)
            halo(1, 1, chunk_rows(k))(k).start()

        return 0

    lax.fori_loop(0, CHUNKS, send_catalyst, 0)
    loads[1].wait()
    loads[0].wait()

    lane = lax.broadcasted_iota(jnp.int32, (8, 128), 1)
    row = lax.broadcasted_iota(jnp.int32, (8, 128), 0)
    beside = [(0, 0), (2, 0), (1, 127), (4, 0), (3, 127), (6, 0), (5, 127), (7, 127)]

    def mix(k, x, start, length):
        m = member_of(k, turn)
        source_rows = pl.ds(pl.multiple_of((k * GRP + x) * SLOT + start, 8), length)
        target_rows = pl.ds(pl.multiple_of(seat * SLOT + start, 8), length)
        away = pltpu.make_async_remote_copy(
            src_ref=sendbuf.at[source_rows, :],
            dst_ref=recvbuf.at[target_rows, :],
            send_sem=mix_send,
            recv_sem=mix_recv.at[team],
            device_id=to(block * SUB + m, x),
            device_id_type=MESH,
        )
        here = pltpu.make_async_copy(sendbuf.at[source_rows, :], recvbuf.at[target_rows, :], own_sem)
        return away, here, m * GRP + x == seat

    def send_tiles(k, start, length):
        for dx in range(1, GRP + 1):
            away, here, stays = mix(k, lax.rem(grp + dx, GRP), start, length)

            @pl.when(stays)
            def _(here=here):
                here.start()

            @pl.when(jnp.logical_not(stays))
            def _(away=away):
                away.start()

    def send_rim(k):
        top = c_new[pl.ds(pl.multiple_of(jnp.maximum(k * REGION - 8, 0), 8), 8), :]
        bottom = c_new[pl.ds(pl.multiple_of(jnp.minimum(k * REGION + REGION, ROWS - 8), 8), 8), :]
        above = jnp.where(k == 0, top[0:1], top[7:8])
        below = jnp.where(k == SUB - 1, bottom[7:8], bottom[0:1])
        window = edge_cols[pl.ds(pl.multiple_of(k * REGION, 8), 32), :]
        window = jnp.concatenate([window, jnp.zeros((96, 128), jnp.float32)], axis=0)
        cols = pltpu.roll(jnp.transpose(window)[0:8], 121, 1)
        for x in range(GRP):
            c = 2 * x * 128
            tile = pltpu.roll(cols, (4 - 2 * x) % 8, 0)
            tile = jnp.where(row == 0, above[:, c : c + 128], tile)
            tile = jnp.where(row == 1, above[:, c + 128 : c + 256], tile)
            tile = jnp.where(row == 2, below[:, c : c + 128], tile)
            tile = jnp.where(row == 3, below[:, c + 128 : c + 256], tile)
            sendbuf[pl.ds(pl.multiple_of((k * GRP + x) * SLOT + 32, 8), 8), :] = tile
        send_tiles(k, 32, 8)

    first = first_chunk(sim)

    def catalyst_chunk(n, _):
        k = lax.rem(first + n, CHUNKS)

        @pl.when(has_prev)
        def _():
            halo(1, 0, chunk_rows(k))(k).wait_recv()

        @pl.when(has_next)
        def _():
            halo(1, 1, chunk_rows(k))(k).wait_recv()

        for h in range(CHUNK // 8):
            r = pl.multiple_of(k * CHUNK + 8 * h, 8)
            c, lap = laplacian(cbuf, c_up, c_dn, r)
            s = sbuf[pl.ds(pl.multiple_of(r + 8, 8), 8), :]
            new = c + DIFF_C * lap + s * c * c - (FEED + KILL) * c
            c_new[pl.ds(r, 8), :] = new
            next_out[1, 0, pl.ds(r, 8), :] = new
            columns = jnp.zeros((8, 128), jnp.float32)
            for i, (tile, at) in enumerate(beside):
                moved = pltpu.roll(new[:, tile * 128 : tile * 128 + 128], (i - at) % 128, 1)
                columns = jnp.where(lane == i, moved, columns)
            edge_cols[pl.ds(pl.multiple_of(r + 8, 8), 8), :] = columns
            if h == 0:
                @pl.when(k == 0)
                def _(columns=columns):
                    edge_cols[0:8, :] = jnp.broadcast_to(columns[0:1], (8, 128))
            else:
                @pl.when(k == CHUNKS - 1)
                def _(columns=columns):
                    edge_cols[ROWS + 8 : ROWS + 16, :] = jnp.broadcast_to(columns[7:8], (8, 128))
            for tile in range(COLS // 128):
                slot = (k * GRP + tile // 2) * SLOT + (h * 2 + tile % 2) * 8
                sendbuf[pl.ds(pl.multiple_of(slot, 8), 8), :] = new[:, tile * 128 : tile * 128 + 128]

        send_tiles(k, 0, 32)

        @pl.when(n >= 2)
        def _():
            send_rim(lax.rem(first + n - 1, CHUNKS))

        return 0

    lax.fori_loop(0, CHUNKS, catalyst_chunk, 0)
    last_rims = lambda n, _: (send_rim(lax.rem(first + CHUNKS - 1 + n, CHUNKS)), 0)[1]
    lax.fori_loop(0, 2, last_rims, 0)

    near_half, far_half = pl.ds(0, ROWS // 2), pl.ds(ROWS // 2, ROWS // 2)

    def to_relay(way):
        return pltpu.make_async_remote_copy(
            src_ref=species.at[0, 0, far_half, :],
            dst_ref=passing,
            send_sem=halo_send.at[0, way],
            recv_sem=relay_recv,
            device_id=partner,
            device_id_type=MESH,
        )

    def from_relay(way):
        return pltpu.make_async_remote_copy(
            src_ref=passing,
            dst_ref=(s_up, s_dn)[way].at[far_half, :],
            send_sem=relay_send,
            recv_sem=halo_recv.at[0, way, 0],
            device_id=relayed_to,
            device_id_type=MESH,
        )

    for way, wanted, end in ((0, has_next, is_a), (1, has_prev, is_b)):
        @pl.when(wanted & jnp.logical_not(end))
        def _(way=way):
            halo(0, way, whole)(0).start()

        @pl.when(end)
        def _(way=way):
            to_relay(way).start()
            halo(0, way, near_half)(0).start()

    def wait_mixed(count, t):
        some = pl.ds(0, count * SLOT)
        return pltpu.make_async_remote_copy(
            src_ref=sendbuf.at[some, :], dst_ref=recvbuf.at[some, :],
            send_sem=mix_send, recv_sem=mix_recv.at[t], device_id=to(sim, grp), device_id_type=MESH,
        )

    extinct = 6.0 / (BLOCKS * MEMBERS)
    log2e = math.log2(math.e)
    thin, narrow = -extinct * log2e / 256.0, -8.0 * log2e / 256.0

    def render(i, _):
        t_now = lax.rem(team + 6 - i, 4)

        @pl.when(t_now == team)
        def _():
            one_slot = pl.ds(0, SLOT)
            pltpu.make_async_copy(sendbuf.at[one_slot, :], recvbuf.at[one_slot, :], own_sem).wait()
            wait_mixed(TEAM - 1, team).wait_recv()

        @pl.when(t_now != team)
        def _():
            wait_mixed(TEAM, t_now).wait_recv()

        base = t_now * (TEAM * SLOT)
        sides = jnp.concatenate(
            [
                recvbuf[pl.ds(base + 36, TEAM, stride=SLOT), :],
                recvbuf[pl.ds(base + 37, TEAM, stride=SLOT), :],
                jnp.zeros((128 - 2 * TEAM, 128), jnp.float32),
            ],
            axis=0,
        )
        sides = jnp.transpose(sides)

        for h in range(2):
            for par in range(2):
                near = 2 * par + 8 * h
                side = 3.0 * sides[1 + 8 * h : 9 + 8 * h] + sides[near : near + 8]

                def layer(p, sums, h=h, par=par, side=side):
                    at = pl.multiple_of(base + p * SLOT, 8)
                    rim = recvbuf[pl.ds(at + 32, 8), :]
                    rows = []
                    for t in range(2):
                        mine = recvbuf[pl.ds(at + (2 * h + t) * 8, 8), :]
                        across = recvbuf[pl.ds(at + (2 - 2 * h + t) * 8, 8), :]
                        if par == 0:
                            beyond = rim[t : t + 1] if h == 0 else across[7:8]
                            shifted = jnp.where(row == 0, beyond, pltpu.roll(mine, 1, 0))
                        else:
                            beyond = rim[2 + t : 3 + t] if h == 1 else across[0:1]
                            shifted = jnp.where(row == 7, beyond, pltpu.roll(mine, 7, 0))
                        rows.append(3.0 * mine + shifted)
                    leftmost = pltpu.roll(side, lax.rem(128 - p, 128), 1)
                    rightmost = pltpu.roll(side, 127 - TEAM - p, 1)
                    fwd = [pltpu.roll(v, 1, 1) for v in rows]
                    bwd = [pltpu.roll(v, 127, 1) for v in rows]
                    low = [jnp.where(lane == 0, leftmost, fwd[0]), jnp.where(lane == 0, fwd[0], fwd[1])]
                    high = [jnp.where(lane == 127, bwd[1], bwd[0]), jnp.where(lane == 127, rightmost, bwd[1])]
                    result = []
                    for cpar in range(2):
                        for t in range(2):
                            q = 3.0 * rows[t] + (low, high)[cpar][t]
                            red, green, blue, clear = sums[(cpar * 2 + t) * 4 : (cpar * 2 + t) * 4 + 4]
                            after = clear * jnp.exp2((q * q) * thin)
                            weight = clear - after
                            mid = q - 8.0
                            warm = mid * (3.0 / 16.0)
                            red = red + weight * jnp.tanh(warm)
                            green = green + weight * jnp.exp2((mid * mid) * narrow)
                            blue = blue + weight * jnp.tanh(warm + 0.6)
                            result += [red, green, blue, after]
                    return tuple(result)

                zero, one = jnp.zeros((8, 128), jnp.float32), jnp.ones((8, 128), jnp.float32)
                sums = lax.fori_loop(0, TEAM, layer, (zero, zero, zero, one) * 4, unroll=True)
                for j in range(16):
                    at = t_now * TOTALS + ((h * 2 + par) * 16 + j) * 8
                    totals[pl.ds(pl.multiple_of(at, 8), 8), :] = sums[j]
        return 0

    lax.fori_loop(0, 4, render, 0)

    for h in range(2):
        for par in range(2):
            for cpar in range(2):
                for t in range(2):
                    base = ((h * 2 + par) * 16 + (cpar * 2 + t) * 4) * 8
                    got = [[totals[i * TOTALS + base + 8 * ch : i * TOTALS + base + 8 * ch + 8, :] for ch in range(4)] for i in range(4)]
                    red, green, blue, clear = got[0]
                    for i in range(1, 4):
                        red = red + clear * got[i][0]
                        green = green + clear * got[i][1]
                        blue = blue + clear * got[i][2]
                        clear = clear * got[i][3]
                    for ch, value in enumerate((red, green, blue, clear)):
                        at = 8 * h * PIECE + ch * 8 + cpar * 4 + par * 2 + t
                        pack[pl.ds(at, 8, stride=PIECE), :] = value

    def piece_rows(n):
        return pl.ds(pl.multiple_of(n * PIECE, PIECE), PIECE)

    def send_piece(n, _):
        j = n + lax.rem(region, 2) * (REGION - 1 - 2 * n)
        there = region * REGION + j

        @pl.when(there != sim)
        def _():
            pltpu.make_async_remote_copy(
                src_ref=pack.at[piece_rows(j), :],
                dst_ref=parts.at[piece_rows(block), :],
                send_sem=part_send,
                recv_sem=part_recv,
                device_id=to(there, grp),
                device_id_type=MESH,
            ).start()

        return 0

    lax.fori_loop(0, REGION, send_piece, 0)

    @pl.when(self_part)
    def _():
        mine = pltpu.make_async_copy(
            pack.at[piece_rows(lax.rem(sim, REGION)), :], parts.at[piece_rows(block), :], part_own
        )
        mine.start()
        mine.wait()

    for way, wanted in ((0, passes_up), (1, passes_down)):
        @pl.when(wanted)
        def _(way=way):
            to_relay(way).wait_recv()
            from_relay(way).start()

    @pl.when(has_prev)
    def _():
        halo(0, 0, whole)(0).wait_recv()

    @pl.when(has_next)
    def _():
        halo(0, 1, whole)(0).wait_recv()

    def substrate_rows(k, _):
        r = pl.multiple_of(8 * k, 8)
        s, lap = laplacian(sbuf, s_up, s_dn, r)
        c = cbuf[pl.ds(pl.multiple_of(r + 8, 8), 8), :]
        next_out[0, 0, pl.ds(r, 8), :] = s + DIFF_S * lap - s * c * c + FEED * (1.0 - s)
        return 0

    lax.fori_loop(0, ROWS // 8, substrate_rows, 0, unroll=4)

    old = lax.broadcasted_iota(jnp.int32, (256, 256), 0)
    new = lax.broadcasted_iota(jnp.int32, (256, 256), 1)
    spread = jnp.where(new == 2 * lax.rem(old, 128) + lax.div(old, 128), 1.0, 0.0).astype(jnp.bfloat16)

    def wait_parts(count):
        some = pl.ds(0, count * PIECE)
        return pltpu.make_async_remote_copy(
            src_ref=pack.at[some, :], dst_ref=parts.at[some, :],
            send_sem=part_send, recv_sem=part_recv, device_id=to(sim, grp), device_id_type=MESH,
        )

    @pl.when(self_part)
    def _():
        wait_parts(BLOCKS - 1).wait_recv()

    @pl.when(jnp.logical_not(self_part))
    def _():
        wait_parts(BLOCKS).wait_recv()

    def add_block(b, totals):
        base = pl.multiple_of(b * PIECE, 8)
        red, green, blue, clear = totals
        got = [parts[pl.ds(base + 8 * ch, 8), :] for ch in range(4)]
        return (
            red + clear * got[0], green + clear * got[1], blue + clear * got[2], clear * got[3],
        )

    zero, one = jnp.zeros((8, 128), jnp.float32), jnp.ones((8, 128), jnp.float32)
    red, green, blue, clear = lax.fori_loop(0, BLOCKS, add_block, (zero, zero, zero, one), unroll=True)
    opaque = 1.0 - clear
    channels = [0.5 * (opaque + red), green, 0.5 * (opaque - blue), opaque]
    flat = jnp.concatenate([jnp.concatenate([v[0:4], v[4:8]], axis=1) for v in channels], axis=0)
    bf16 = jnp.bfloat16
    high = flat.astype(bf16)
    rest = flat - high.astype(jnp.float32)
    middle = rest.astype(bf16)
    low = (rest - middle.astype(jnp.float32)).astype(bf16)
    split = jnp.dot(
        jnp.concatenate([high, middle, low], axis=0), spread, preferred_element_type=jnp.float32
    )
    mixed = split[0:16] + (split[16:32] + split[32:48])
    for ch in range(4):
        for par in range(2):
            for t in range(2):
                n = ch * 4 + par * 2 + t
                frame_out[ch, par : par + 1, t * 256 : t * 256 + 256] = mixed[n : n + 1]

    @pl.when(is_relay)
    def _():
        from_relay(0).wait_send()

    for i in range(2):
        @pl.when(has_next)
        def _(i=i):
            halo(i, 0, whole)(0).wait_send()

        @pl.when(has_prev)
        def _(i=i):
            halo(i, 1, whole)(0).wait_send()

    wait_mixed(MEMBERS - 1, team).wait_send()

    @pl.when(self_part)
    def _():
        wait_parts(BLOCKS - 1).wait_send()

    @pl.when(jnp.logical_not(self_part))
    def _():
        wait_parts(BLOCKS).wait_send()


def shards(species):
    f32 = jnp.float32
    plane = pltpu.VMEM((ROWS, COLS), f32)
    padded = pltpu.VMEM((ROWS + 16, COLS), f32)
    dma = pltpu.SemaphoreType.DMA
    fresh, frame = pl.pallas_call(
        kernel,
        out_shape=(
            jax.ShapeDtypeStruct((2, 1, ROWS, COLS), f32),
            jax.ShapeDtypeStruct((4, 2 * ROWS // SIMS, 2 * COLS // GRP), f32),
        ),
        in_specs=[pl.BlockSpec(memory_space=pltpu.HBM)],
        out_specs=(pl.BlockSpec(memory_space=pltpu.VMEM),) * 2,
        scratch_shapes=[
            padded, padded, plane, plane, plane, plane, pltpu.VMEM((ROWS // 2, COLS), f32),
            plane,
            pltpu.VMEM((ROWS + 16, 128), f32),
            pltpu.VMEM((MEMBERS * SLOT, 128), f32),
            pltpu.VMEM((MEMBERS * SLOT, 128), f32),
            pltpu.VMEM((4 * TOTALS, 128), f32),
            pltpu.VMEM((REGION * PIECE, 128), f32),
            pltpu.VMEM((BLOCKS * PIECE, 128), f32),
            dma((2,)), dma((2, 2)), dma((2, 2, CHUNKS)), dma, dma,
            dma, dma, dma((4,)), dma, dma, dma,
        ],
        compiler_params=pltpu.CompilerParams(
            collective_id=0, has_side_effects=True, vmem_limit_bytes=32 * 1024 * 1024
        ),
        cost_estimate=pl.CostEstimate(flops=20_000_000, bytes_accessed=4_000_000, transcendentals=2_000_000),
    )(pltpu.with_memory_space_constraint(species, pltpu.HBM))
    return fresh, frame


def solution(mesh):
    return jax.shard_map(
        shards,
        mesh=mesh,
        in_specs=(P(None, ("sim", "grp"), None, None),),
        out_specs=(P(None, ("sim", "grp"), None, None), P(None, "sim", "grp")),
        check_vma=False,
    )
```

```python
import math

import jax
import jax.numpy as jnp
from jax import lax
from jax.experimental import pallas as pl
from jax.experimental.pallas import tpu as pltpu
from jax.sharding import PartitionSpec as P

MESH = pl.DeviceIdType.MESH

ROWS = 128
COLS = 1024
GRP = 4
SIMS = 128
SUB = 8
BLOCKS = SIMS // SUB
MEMBERS = GRP * SUB
REGION = ROWS // SUB
CHUNKS = 8
CHUNK = ROWS // CHUNKS
SLOT = 40
PIECE = 32
TEAM = MEMBERS // 4
TOTALS = 64 * 8

DIFF_S, DIFF_C, FEED, KILL = 0.16, 0.08, 0.035, 0.065


def to(sim, grp):
    return {"sim": sim, "grp": grp}


def in_plane(buf, r):
    window = buf[pl.ds(r, 24), :]
    center = window[8:16]
    lane = lax.broadcasted_iota(jnp.int32, (8, COLS), 1)
    left = jnp.where(lane == 0, 0.0, pltpu.roll(center, 1, 1))
    right = jnp.where(lane == COLS - 1, 0.0, pltpu.roll(center, COLS - 1, 1))
    return center, window[7:15] + window[9:17] + left + right - 6.0 * center


def kernel(
    species, next_out, frame_out,
    sbuf, cbuf, s_up, s_dn, c_up, c_dn, passing, c_new, edge_cols, sendbuf, recvbuf, totals, pack, parts,
    load_sem, halo_send, halo_recv, relay_send, relay_recv, own_sem, mix_send, mix_recv, part_own, part_send, part_recv,
):
    sim, grp = lax.axis_index("sim"), lax.axis_index("grp")
    plane = sim * GRP + grp
    block, member = lax.div(sim, SUB), lax.rem(sim, SUB)
    seat = member * GRP + grp
    turn = lax.div(block, 4) + lax.rem(block, 4)

    def region_of(m, turn):
        return 2 * lax.rem(lax.div(m, 2) + 8 - turn, 4) + lax.rem(m, 2)

    def member_of(q, turn):
        return 2 * lax.rem(lax.div(q, 2) + turn, 4) + lax.rem(q, 2)

    def first_chunk(sim):
        block = lax.div(sim, SUB)
        place = lax.div(lax.rem(sim, SUB), 2) + 1 + 8 - lax.div(block, 4) - lax.rem(block, 4)
        return 2 * lax.rem(place, 4)

    region = region_of(member, turn)
    team = lax.div(member, 2)

    def source(b):
        t = lax.div(b, 4) + lax.rem(b, 4)
        return b * SUB + member_of(lax.div(sim, REGION), t)

    loads = [
        pltpu.make_async_copy(species.at[i, 0], buf.at[pl.ds(8, ROWS), :], load_sem.at[i])
        for i, buf in ((0, sbuf), (1, cbuf))
    ]
    loads[1].start()
    loads[0].start()

    has_prev, has_next = plane > 0, plane < SIMS * GRP - 1
    prev = to(lax.div(plane - 1, GRP), lax.rem(plane - 1 + GRP, GRP))
    nxt = to(lax.div(plane + 1, GRP), lax.rem(plane + 1, GRP))

    odd = lax.rem(sim, 2)
    partner = to(sim + 2 * odd - 1, grp)
    crossing = (sim + odd > 0) & (sim + odd < SIMS)
    is_a, is_b = crossing & (odd == 1) & (grp == GRP - 1), crossing & (odd == 0) & (grp == 0)
    is_relay = crossing & (((odd == 0) & (grp == GRP - 1)) | ((odd == 1) & (grp == 0)))
    passes_up = is_relay & (odd == 0)
    passes_down = is_relay & (odd == 1)
    relayed_to = to(sim, GRP - 1 - grp)
    barrier = pltpu.get_barrier_semaphore()

    @pl.when(has_prev)
    def _():
        pl.semaphore_signal(barrier, inc=1, device_id=prev, device_id_type=MESH)

    @pl.when(has_next)
    def _():
        pl.semaphore_signal(barrier, inc=1, device_id=nxt, device_id_type=MESH)

    @pl.when(is_relay)
    def _():
        pl.semaphore_signal(barrier, inc=1, device_id=partner, device_id_type=MESH)

    def greet_member(d, _):
        other = lax.rem(seat + d, MEMBERS)
        there = to(block * SUB + lax.div(other, GRP), lax.rem(other, GRP))
        pl.semaphore_signal(barrier, inc=1, device_id=there, device_id_type=MESH)
        return 0

    lax.fori_loop(1, MEMBERS, greet_member, 0)

    def greet_source(b, _):
        there = source(b)

        @pl.when(there != sim)
        def _():
            pl.semaphore_signal(barrier, inc=1, device_id=to(there, grp), device_id_type=MESH)

        return 0

    lax.fori_loop(0, BLOCKS, greet_source, 0)

    for buf in (sbuf, cbuf):
        buf[0:8, :] = jnp.zeros((8, COLS), jnp.float32)
        buf[ROWS + 8 : ROWS + 16, :] = jnp.zeros((8, COLS), jnp.float32)

    @pl.when(plane == 0)
    def _():
        s_up[...] = jnp.zeros_like(s_up)
        c_up[...] = jnp.zeros_like(c_up)

    @pl.when(plane == SIMS * GRP - 1)
    def _():
        s_dn[...] = jnp.zeros_like(s_dn)
        c_dn[...] = jnp.zeros_like(c_dn)

    self_part = lax.div(sim, REGION) == region
    expected = MEMBERS - 1 + BLOCKS - self_part.astype(jnp.int32)
    for wanted in (has_prev, has_next, is_a, is_b):
        expected = expected + wanted.astype(jnp.int32)
    pl.semaphore_wait(barrier, expected)

    def halo(i, way, rows):
        target = ((s_up, s_dn), (c_up, c_dn))[i][way]
        return lambda chunk: pltpu.make_async_remote_copy(
            src_ref=species.at[i, 0, rows, :],
            dst_ref=target.at[rows, :],
            send_sem=halo_send.at[i, way],
            recv_sem=halo_recv.at[i, way, chunk],
            device_id=(nxt, prev)[way],
            device_id_type=MESH,
        )

    def chunk_rows(k):
        return pl.ds(pl.multiple_of(k * CHUNK, CHUNK), CHUNK)

    whole = pl.ds(0, ROWS)

    first_next, first_prev = first_chunk(nxt["sim"]), first_chunk(prev["sim"])

    def send_catalyst(n, _):
        @pl.when(has_next)
        def _():
            k = lax.rem(first_next + n, CHUNKS)
            halo(1, 0, chunk_rows(k))(k).start()

        @pl.when(has_prev)
        def _():
            k = lax.rem(first_prev + n, CHUNKS)
            halo(1, 1, chunk_rows(k))(k).start()

        return 0

    lax.fori_loop(0, CHUNKS, send_catalyst, 0)
    loads[1].wait()
    loads[0].wait()

    lane = lax.broadcasted_iota(jnp.int32, (8, 128), 1)
    row = lax.broadcasted_iota(jnp.int32, (8, 128), 0)
    beside = [(0, 0), (2, 0), (1, 127), (4, 0), (3, 127), (6, 0), (5, 127), (7, 127)]

    def mix(k, x, start, length):
        m = member_of(k, turn)
        source_rows = pl.ds(pl.multiple_of((k * GRP + x) * SLOT + start, 8), length)
        target_rows = pl.ds(pl.multiple_of(seat * SLOT + start, 8), length)
        away = pltpu.make_async_remote_copy(
            src_ref=sendbuf.at[source_rows, :],
            dst_ref=recvbuf.at[target_rows, :],
            send_sem=mix_send,
            recv_sem=mix_recv.at[team],
            device_id=to(block * SUB + m, x),
            device_id_type=MESH,
        )
        here = pltpu.make_async_copy(sendbuf.at[source_rows, :], recvbuf.at[target_rows, :], own_sem)
        return away, here, m * GRP + x == seat

    def send_tiles(k, start, length):
        for dx in range(1, GRP + 1):
            away, here, stays = mix(k, lax.rem(grp + dx, GRP), start, length)

            @pl.when(stays)
            def _(here=here):
                here.start()

            @pl.when(jnp.logical_not(stays))
            def _(away=away):
                away.start()

    def make_rim(k):
        top = c_new[pl.ds(pl.multiple_of(jnp.maximum(k * REGION - 8, 0), 8), 8), :]
        bottom = c_new[pl.ds(pl.multiple_of(jnp.minimum(k * REGION + REGION, ROWS - 8), 8), 8), :]
        above = jnp.where(k == 0, top[0:1], top[7:8])
        below = jnp.where(k == SUB - 1, bottom[7:8], bottom[0:1])
        window = edge_cols[pl.ds(pl.multiple_of(k * REGION, 8), 32), :]
        window = jnp.concatenate([window, jnp.zeros((96, 128), jnp.float32)], axis=0)
        cols = pltpu.roll(jnp.transpose(window)[0:8], 121, 1)
        for x in range(GRP):
            c = 2 * x * 128
            tile = pltpu.roll(cols, (4 - 2 * x) % 8, 0)
            tile = jnp.where(row == 0, above[:, c : c + 128], tile)
            tile = jnp.where(row == 1, above[:, c + 128 : c + 256], tile)
            tile = jnp.where(row == 2, below[:, c : c + 128], tile)
            tile = jnp.where(row == 3, below[:, c + 128 : c + 256], tile)
            sendbuf[pl.ds(pl.multiple_of((k * GRP + x) * SLOT + 32, 8), 8), :] = tile

    first = first_chunk(sim)

    def catalyst_chunk(n, _):
        k = lax.rem(first + n, CHUNKS)

        @pl.when(has_prev)
        def _():
            halo(1, 0, chunk_rows(k))(k).wait_recv()

        @pl.when(has_next)
        def _():
            halo(1, 1, chunk_rows(k))(k).wait_recv()

        for h in range(CHUNK // 8):
            r = pl.multiple_of(k * CHUNK + 8 * h, 8)
            c, lap = in_plane(cbuf, r)
            lap = lap + c_up[pl.ds(r, 8), :] + c_dn[pl.ds(r, 8), :]
            s = sbuf[pl.ds(pl.multiple_of(r + 8, 8), 8), :]
            new = c + DIFF_C * lap + s * c * c - (FEED + KILL) * c
            c_new[pl.ds(r, 8), :] = new
            next_out[1, 0, pl.ds(r, 8), :] = new
            columns = jnp.zeros((8, 128), jnp.float32)
            for i, (tile, at) in enumerate(beside):
                moved = pltpu.roll(new[:, tile * 128 : tile * 128 + 128], (i - at) % 128, 1)
                columns = jnp.where(lane == i, moved, columns)
            edge_cols[pl.ds(pl.multiple_of(r + 8, 8), 8), :] = columns
            if h == 0:
                @pl.when(k == 0)
                def _(columns=columns):
                    edge_cols[0:8, :] = jnp.broadcast_to(columns[0:1], (8, 128))
            else:
                @pl.when(k == CHUNKS - 1)
                def _(columns=columns):
                    edge_cols[ROWS + 8 : ROWS + 16, :] = jnp.broadcast_to(columns[7:8], (8, 128))
            for tile in range(COLS // 128):
                slot = (k * GRP + tile // 2) * SLOT + (h * 2 + tile % 2) * 8
                sendbuf[pl.ds(pl.multiple_of(slot, 8), 8), :] = new[:, tile * 128 : tile * 128 + 128]

        send_tiles(k, 0, 32)

        @pl.when(n >= 2)
        def _():
            make_rim(lax.rem(first + n - 1, CHUNKS))
            send_tiles(lax.rem(first + n - 1, CHUNKS), 32, 8)

        return 0

    lax.fori_loop(0, CHUNKS, catalyst_chunk, 0)
    last_two = [lax.rem(first + CHUNKS - 1 + n, CHUNKS) for n in range(2)]
    for k in last_two:
        make_rim(k)
    for k in last_two:
        send_tiles(k, 32, 8)

    near_half, far_half = pl.ds(0, ROWS // 2), pl.ds(ROWS // 2, ROWS // 2)

    def to_relay(way):
        return pltpu.make_async_remote_copy(
            src_ref=species.at[0, 0, far_half, :],
            dst_ref=passing,
            send_sem=halo_send.at[0, way],
            recv_sem=relay_recv,
            device_id=partner,
            device_id_type=MESH,
        )

    def from_relay(way):
        return pltpu.make_async_remote_copy(
            src_ref=passing,
            dst_ref=(s_up, s_dn)[way].at[far_half, :],
            send_sem=relay_send,
            recv_sem=halo_recv.at[0, way, 0],
            device_id=relayed_to,
            device_id_type=MESH,
        )

    for way, wanted, end in ((0, has_next, is_a), (1, has_prev, is_b)):
        @pl.when(wanted & jnp.logical_not(end))
        def _(way=way):
            halo(0, way, whole)(0).start()

        @pl.when(end)
        def _(way=way):
            to_relay(way).start()
            halo(0, way, near_half)(0).start()

    def wait_mixed(count, t):
        some = pl.ds(0, count * SLOT)
        return pltpu.make_async_remote_copy(
            src_ref=sendbuf.at[some, :], dst_ref=recvbuf.at[some, :],
            send_sem=mix_send, recv_sem=mix_recv.at[t], device_id=to(sim, grp), device_id_type=MESH,
        )

    extinct = 6.0 / (BLOCKS * MEMBERS)
    log2e = math.log2(math.e)
    thin, narrow = -extinct * log2e / 256.0, -8.0 * log2e / 256.0

    def render(i, _):
        t_now = lax.rem(team + 6 - i, 4)

        @pl.when(t_now == team)
        def _():
            one_slot = pl.ds(0, SLOT)
            pltpu.make_async_copy(sendbuf.at[one_slot, :], recvbuf.at[one_slot, :], own_sem).wait()
            wait_mixed(TEAM - 1, team).wait_recv()

        @pl.when(t_now != team)
        def _():
            wait_mixed(TEAM, t_now).wait_recv()

        for way, wanted in ((0, passes_up), (1, passes_down)):
            @pl.when((i == 3) & wanted)
            def _(way=way):
                to_relay(way).wait_recv()
                from_relay(way).start()

        base = t_now * (TEAM * SLOT)
        sides = jnp.concatenate(
            [
                recvbuf[pl.ds(base + 36, TEAM, stride=SLOT), :],
                recvbuf[pl.ds(base + 37, TEAM, stride=SLOT), :],
                jnp.zeros((128 - 2 * TEAM, 128), jnp.float32),
            ],
            axis=0,
        )
        sides = jnp.transpose(sides)

        for h in range(2):
            for par in range(2):
                near = 2 * par + 8 * h
                side = 3.0 * sides[1 + 8 * h : 9 + 8 * h] + sides[near : near + 8]

                def layer(p, sums, h=h, par=par, side=side):
                    at = pl.multiple_of(base + p * SLOT, 8)
                    rim = recvbuf[pl.ds(at + 32, 8), :]
                    rows = []
                    for t in range(2):
                        mine = recvbuf[pl.ds(at + (2 * h + t) * 8, 8), :]
                        across = recvbuf[pl.ds(at + (2 - 2 * h + t) * 8, 8), :]
                        if par == 0:
                            beyond = rim[t : t + 1] if h == 0 else across[7:8]
                            shifted = jnp.where(row == 0, beyond, pltpu.roll(mine, 1, 0))
                        else:
                            beyond = rim[2 + t : 3 + t] if h == 1 else across[0:1]
                            shifted = jnp.where(row == 7, beyond, pltpu.roll(mine, 7, 0))
                        rows.append(3.0 * mine + shifted)
                    leftmost = pltpu.roll(side, lax.rem(128 - p, 128), 1)
                    rightmost = pltpu.roll(side, 127 - TEAM - p, 1)
                    fwd = [pltpu.roll(v, 1, 1) for v in rows]
                    bwd = [pltpu.roll(v, 127, 1) for v in rows]
                    low = [jnp.where(lane == 0, leftmost, fwd[0]), jnp.where(lane == 0, fwd[0], fwd[1])]
                    high = [jnp.where(lane == 127, bwd[1], bwd[0]), jnp.where(lane == 127, rightmost, bwd[1])]
                    result = []
                    for cpar in range(2):
                        for t in range(2):
                            q = 3.0 * rows[t] + (low, high)[cpar][t]
                            red, green, blue, clear = sums[(cpar * 2 + t) * 4 : (cpar * 2 + t) * 4 + 4]
                            after = clear * jnp.exp2((q * q) * thin)
                            weight = clear - after
                            mid = q - 8.0
                            warm = mid * (3.0 / 16.0)
                            red = red + weight * jnp.tanh(warm)
                            green = green + weight * jnp.exp2((mid * mid) * narrow)
                            blue = blue + weight * jnp.tanh(warm + 0.6)
                            result += [red, green, blue, after]
                    return tuple(result)

                zero, one = jnp.zeros((8, 128), jnp.float32), jnp.ones((8, 128), jnp.float32)
                sums = lax.fori_loop(0, TEAM, layer, (zero, zero, zero, one) * 4, unroll=True)
                for j in range(16):
                    at = t_now * TOTALS + ((h * 2 + par) * 16 + j) * 8
                    totals[pl.ds(pl.multiple_of(at, 8), 8), :] = sums[j]
        return 0

    lax.fori_loop(0, 4, render, 0)

    def piece_rows(n):
        return pl.ds(pl.multiple_of(n * PIECE, PIECE), PIECE)

    for h in range(2):
        for par in range(2):
            for cpar in range(2):
                for t in range(2):
                    base = ((h * 2 + par) * 16 + (cpar * 2 + t) * 4) * 8
                    got = [[totals[i * TOTALS + base + 8 * ch : i * TOTALS + base + 8 * ch + 8, :] for ch in range(4)] for i in range(4)]
                    red, green, blue, clear = got[0]
                    for i in range(1, 4):
                        red = red + clear * got[i][0]
                        green = green + clear * got[i][1]
                        blue = blue + clear * got[i][2]
                        clear = clear * got[i][3]
                    for ch, value in enumerate((red, green, blue, clear)):
                        at = 8 * h * PIECE + ch * 8 + cpar * 4 + par * 2 + t
                        pack[pl.ds(at, 8, stride=PIECE), :] = value

        def send_piece(n, _, h=h):
            j = 8 * h + n
            there = region * REGION + j

            @pl.when(there != sim)
            def _():
                pltpu.make_async_remote_copy(
                    src_ref=pack.at[piece_rows(j), :],
                    dst_ref=parts.at[piece_rows(block), :],
                    send_sem=part_send,
                    recv_sem=part_recv,
                    device_id=to(there, grp),
                    device_id_type=MESH,
                ).start()

            return 0

        lax.fori_loop(0, 8, send_piece, 0)

    @pl.when(self_part)
    def _():
        mine = pltpu.make_async_copy(
            pack.at[piece_rows(lax.rem(sim, REGION)), :], parts.at[piece_rows(block), :], part_own
        )
        mine.start()
        mine.wait()

    def substrate_part(k, _):
        r = pl.multiple_of(8 * k, 8)
        s, lap = in_plane(sbuf, r)
        c = cbuf[pl.ds(pl.multiple_of(r + 8, 8), 8), :]
        next_out[0, 0, pl.ds(r, 8), :] = s + DIFF_S * lap - s * c * c + FEED * (1.0 - s)
        return 0

    lax.fori_loop(0, ROWS // 8, substrate_part, 0, unroll=4)

    @pl.when(has_prev)
    def _():
        halo(0, 0, whole)(0).wait_recv()

    @pl.when(has_next)
    def _():
        halo(0, 1, whole)(0).wait_recv()

    def substrate_rows(k, _):
        rows = pl.ds(pl.multiple_of(8 * k, 8), 8)
        next_out[0, 0, rows, :] = next_out[0, 0, rows, :] + DIFF_S * (s_up[rows, :] + s_dn[rows, :])
        return 0

    lax.fori_loop(0, ROWS // 8, substrate_rows, 0, unroll=4)

    old = lax.broadcasted_iota(jnp.int32, (256, 256), 0)
    new = lax.broadcasted_iota(jnp.int32, (256, 256), 1)
    spread = jnp.where(new == 2 * lax.rem(old, 128) + lax.div(old, 128), 1.0, 0.0).astype(jnp.bfloat16)

    def wait_parts(count):
        some = pl.ds(0, count * PIECE)
        return pltpu.make_async_remote_copy(
            src_ref=pack.at[some, :], dst_ref=parts.at[some, :],
            send_sem=part_send, recv_sem=part_recv, device_id=to(sim, grp), device_id_type=MESH,
        )

    @pl.when(self_part)
    def _():
        wait_parts(BLOCKS - 1).wait_recv()

    @pl.when(jnp.logical_not(self_part))
    def _():
        wait_parts(BLOCKS).wait_recv()

    def add_block(b, totals):
        base = pl.multiple_of(b * PIECE, 8)
        red, green, blue, clear = totals
        got = [parts[pl.ds(base + 8 * ch, 8), :] for ch in range(4)]
        return (
            red + clear * got[0], green + clear * got[1], blue + clear * got[2], clear * got[3],
        )

    zero, one = jnp.zeros((8, 128), jnp.float32), jnp.ones((8, 128), jnp.float32)
    red, green, blue, clear = lax.fori_loop(0, BLOCKS, add_block, (zero, zero, zero, one), unroll=True)
    opaque = 1.0 - clear
    channels = [0.5 * (opaque + red), green, 0.5 * (opaque - blue), opaque]
    flat = jnp.concatenate([jnp.concatenate([v[0:4], v[4:8]], axis=1) for v in channels], axis=0)
    bf16 = jnp.bfloat16
    high = flat.astype(bf16)
    rest = flat - high.astype(jnp.float32)
    middle = rest.astype(bf16)
    low = (rest - middle.astype(jnp.float32)).astype(bf16)
    split = jnp.dot(
        jnp.concatenate([high, middle, low], axis=0), spread, preferred_element_type=jnp.float32
    )
    mixed = split[0:16] + (split[16:32] + split[32:48])
    for ch in range(4):
        for par in range(2):
            for t in range(2):
                n = ch * 4 + par * 2 + t
                frame_out[ch, par : par + 1, t * 256 : t * 256 + 256] = mixed[n : n + 1]

    @pl.when(is_relay)
    def _():
        from_relay(0).wait_send()

    for i in range(2):
        @pl.when(has_next)
        def _(i=i):
            halo(i, 0, whole)(0).wait_send()

        @pl.when(has_prev)
        def _(i=i):
            halo(i, 1, whole)(0).wait_send()

    wait_mixed(MEMBERS - 1, team).wait_send()

    @pl.when(self_part)
    def _():
        wait_parts(BLOCKS - 1).wait_send()

    @pl.when(jnp.logical_not(self_part))
    def _():
        wait_parts(BLOCKS).wait_send()


def shards(species):
    f32 = jnp.float32
    plane = pltpu.VMEM((ROWS, COLS), f32)
    padded = pltpu.VMEM((ROWS + 16, COLS), f32)
    dma = pltpu.SemaphoreType.DMA
    fresh, frame = pl.pallas_call(
        kernel,
        out_shape=(
            jax.ShapeDtypeStruct((2, 1, ROWS, COLS), f32),
            jax.ShapeDtypeStruct((4, 2 * ROWS // SIMS, 2 * COLS // GRP), f32),
        ),
        in_specs=[pl.BlockSpec(memory_space=pltpu.HBM)],
        out_specs=(pl.BlockSpec(memory_space=pltpu.VMEM),) * 2,
        scratch_shapes=[
            padded, padded, plane, plane, plane, plane, pltpu.VMEM((ROWS // 2, COLS), f32),
            plane,
            pltpu.VMEM((ROWS + 16, 128), f32),
            pltpu.VMEM((MEMBERS * SLOT, 128), f32),
            pltpu.VMEM((MEMBERS * SLOT, 128), f32),
            pltpu.VMEM((4 * TOTALS, 128), f32),
            pltpu.VMEM((REGION * PIECE, 128), f32),
            pltpu.VMEM((BLOCKS * PIECE, 128), f32),
            dma((2,)), dma((2, 2)), dma((2, 2, CHUNKS)), dma, dma,
            dma, dma, dma((4,)), dma, dma, dma,
        ],
        compiler_params=pltpu.CompilerParams(
            collective_id=0, has_side_effects=True, vmem_limit_bytes=32 * 1024 * 1024
        ),
        cost_estimate=pl.CostEstimate(flops=20_000_000, bytes_accessed=4_000_000, transcendentals=2_000_000),
    )(pltpu.with_memory_space_constraint(species, pltpu.HBM))
    return fresh, frame


def solution(mesh):
    return jax.shard_map(
        shards,
        mesh=mesh,
        in_specs=(P(None, ("sim", "grp"), None, None),),
        out_specs=(P(None, ("sim", "grp"), None, None), P(None, "sim", "grp")),
        check_vma=False,
    )
```

```python
import math

import jax
import jax.numpy as jnp
from jax import lax
from jax.experimental import pallas as pl
from jax.experimental.pallas import tpu as pltpu
from jax.sharding import PartitionSpec as P

MESH = pl.DeviceIdType.MESH

ROWS = 128
COLS = 1024
GRP = 4
SIMS = 128
SUB = 8
BLOCKS = SIMS // SUB
MEMBERS = GRP * SUB
REGION = ROWS // SUB
CHUNKS = 8
CHUNK = ROWS // CHUNKS
SLOT = 40
PIECE = 32
TEAM = MEMBERS // 4
TOTALS = 64 * 8

DIFF_S, DIFF_C, FEED, KILL = 0.16, 0.08, 0.035, 0.065


def to(sim, grp):
    return {"sim": sim, "grp": grp}


def in_plane(buf, r):
    window = buf[pl.ds(r, 24), :]
    center = window[8:16]
    lane = lax.broadcasted_iota(jnp.int32, (8, COLS), 1)
    left = jnp.where(lane == 0, 0.0, pltpu.roll(center, 1, 1))
    right = jnp.where(lane == COLS - 1, 0.0, pltpu.roll(center, COLS - 1, 1))
    return center, window[7:15] + window[9:17] + left + right - 6.0 * center


def kernel(
    species, next_out, frame_out,
    sbuf, cbuf, s_up, s_dn, c_up, c_dn, passing, c_new, edge_cols, sendbuf, recvbuf, totals, pack, parts,
    load_sem, halo_send, halo_recv, relay_send, relay_recv, own_sem, mix_send, mix_recv, part_own, part_send, part_recv,
):
    sim, grp = lax.axis_index("sim"), lax.axis_index("grp")
    plane = sim * GRP + grp
    block, member = lax.div(sim, SUB), lax.rem(sim, SUB)
    seat = member * GRP + grp
    turn = lax.div(block, 4) + lax.rem(block, 4)

    def region_of(m, turn):
        return 2 * lax.rem(lax.div(m, 2) + 8 - turn, 4) + lax.rem(m, 2)

    def member_of(q, turn):
        return 2 * lax.rem(lax.div(q, 2) + turn, 4) + lax.rem(q, 2)

    def first_chunk(sim):
        block = lax.div(sim, SUB)
        place = lax.div(lax.rem(sim, SUB), 2) + 1 + 8 - lax.div(block, 4) - lax.rem(block, 4)
        return 2 * lax.rem(place, 4)

    region = region_of(member, turn)
    team = lax.div(member, 2)

    def source(b):
        t = lax.div(b, 4) + lax.rem(b, 4)
        return b * SUB + member_of(lax.div(sim, REGION), t)

    loads = [
        pltpu.make_async_copy(species.at[i, 0], buf.at[pl.ds(8, ROWS), :], load_sem.at[i])
        for i, buf in ((0, sbuf), (1, cbuf))
    ]
    loads[1].start()
    loads[0].start()

    has_prev, has_next = plane > 0, plane < SIMS * GRP - 1
    prev = to(lax.div(plane - 1, GRP), lax.rem(plane - 1 + GRP, GRP))
    nxt = to(lax.div(plane + 1, GRP), lax.rem(plane + 1, GRP))

    odd = lax.rem(sim, 2)
    partner = to(sim + 2 * odd - 1, grp)
    crossing = (sim + odd > 0) & (sim + odd < SIMS)
    is_a, is_b = crossing & (odd == 1) & (grp == GRP - 1), crossing & (odd == 0) & (grp == 0)
    is_relay = crossing & (((odd == 0) & (grp == GRP - 1)) | ((odd == 1) & (grp == 0)))
    passes_up = is_relay & (odd == 0)
    passes_down = is_relay & (odd == 1)
    relayed_to = to(sim, GRP - 1 - grp)
    barrier = pltpu.get_barrier_semaphore()

    @pl.when(has_prev)
    def _():
        pl.semaphore_signal(barrier, inc=1, device_id=prev, device_id_type=MESH)

    @pl.when(has_next)
    def _():
        pl.semaphore_signal(barrier, inc=1, device_id=nxt, device_id_type=MESH)

    @pl.when(is_relay)
    def _():
        pl.semaphore_signal(barrier, inc=1, device_id=partner, device_id_type=MESH)

    def greet_member(d, _):
        other = lax.rem(seat + d, MEMBERS)
        there = to(block * SUB + lax.div(other, GRP), lax.rem(other, GRP))
        pl.semaphore_signal(barrier, inc=1, device_id=there, device_id_type=MESH)
        return 0

    lax.fori_loop(1, MEMBERS, greet_member, 0)

    def greet_source(b, _):
        there = source(b)

        @pl.when(there != sim)
        def _():
            pl.semaphore_signal(barrier, inc=1, device_id=to(there, grp), device_id_type=MESH)

        return 0

    lax.fori_loop(0, BLOCKS, greet_source, 0)

    for buf in (sbuf, cbuf):
        buf[0:8, :] = jnp.zeros((8, COLS), jnp.float32)
        buf[ROWS + 8 : ROWS + 16, :] = jnp.zeros((8, COLS), jnp.float32)

    @pl.when(plane == 0)
    def _():
        s_up[...] = jnp.zeros_like(s_up)
        c_up[...] = jnp.zeros_like(c_up)

    @pl.when(plane == SIMS * GRP - 1)
    def _():
        s_dn[...] = jnp.zeros_like(s_dn)
        c_dn[...] = jnp.zeros_like(c_dn)

    self_part = lax.div(sim, REGION) == region
    expected = MEMBERS - 1 + BLOCKS - self_part.astype(jnp.int32)
    for wanted in (has_prev, has_next, is_a, is_b):
        expected = expected + wanted.astype(jnp.int32)
    pl.semaphore_wait(barrier, expected)

    def halo(i, way, rows):
        target = ((s_up, s_dn), (c_up, c_dn))[i][way]
        return lambda chunk: pltpu.make_async_remote_copy(
            src_ref=species.at[i, 0, rows, :],
            dst_ref=target.at[rows, :],
            send_sem=halo_send.at[i, way],
            recv_sem=halo_recv.at[i, way, chunk],
            device_id=(nxt, prev)[way],
            device_id_type=MESH,
        )

    def chunk_rows(k):
        return pl.ds(pl.multiple_of(k * CHUNK, CHUNK), CHUNK)

    whole = pl.ds(0, ROWS)

    first_next, first_prev = first_chunk(nxt["sim"]), first_chunk(prev["sim"])

    def send_catalyst(n, _):
        @pl.when(has_next)
        def _():
            k = lax.rem(first_next + n, CHUNKS)
            halo(1, 0, chunk_rows(k))(k).start()

        @pl.when(has_prev)
        def _():
            k = lax.rem(first_prev + n, CHUNKS)
            halo(1, 1, chunk_rows(k))(k).start()

        return 0

    lax.fori_loop(0, CHUNKS, send_catalyst, 0)
    loads[1].wait()
    loads[0].wait()

    lane = lax.broadcasted_iota(jnp.int32, (8, 128), 1)
    row = lax.broadcasted_iota(jnp.int32, (8, 128), 0)
    beside = [(0, 0), (2, 0), (1, 127), (4, 0), (3, 127), (6, 0), (5, 127), (7, 127)]

    def mix(k, x, start, length):
        m = member_of(k, turn)
        source_rows = pl.ds(pl.multiple_of((k * GRP + x) * SLOT + start, 8), length)
        target_rows = pl.ds(pl.multiple_of(seat * SLOT + start, 8), length)
        away = pltpu.make_async_remote_copy(
            src_ref=sendbuf.at[source_rows, :],
            dst_ref=recvbuf.at[target_rows, :],
            send_sem=mix_send,
            recv_sem=mix_recv.at[team],
            device_id=to(block * SUB + m, x),
            device_id_type=MESH,
        )
        here = pltpu.make_async_copy(sendbuf.at[source_rows, :], recvbuf.at[target_rows, :], own_sem)
        return away, here, m * GRP + x == seat

    def send_tiles(k, start, length):
        for dx in range(1, GRP + 1):
            away, here, stays = mix(k, lax.rem(grp + dx, GRP), start, length)

            @pl.when(stays)
            def _(here=here):
                here.start()

            @pl.when(jnp.logical_not(stays))
            def _(away=away):
                away.start()

    def make_rim(k):
        top = c_new[pl.ds(pl.multiple_of(jnp.maximum(k * REGION - 8, 0), 8), 8), :]
        bottom = c_new[pl.ds(pl.multiple_of(jnp.minimum(k * REGION + REGION, ROWS - 8), 8), 8), :]
        above = jnp.where(k == 0, top[0:1], top[7:8])
        below = jnp.where(k == SUB - 1, bottom[7:8], bottom[0:1])
        window = edge_cols[pl.ds(pl.multiple_of(k * REGION, 8), 32), :]
        window = jnp.concatenate([window, jnp.zeros((96, 128), jnp.float32)], axis=0)
        cols = pltpu.roll(jnp.transpose(window)[0:8], 121, 1)
        for x in range(GRP):
            c = 2 * x * 128
            tile = pltpu.roll(cols, (4 - 2 * x) % 8, 0)
            tile = jnp.where(row == 0, above[:, c : c + 128], tile)
            tile = jnp.where(row == 1, above[:, c + 128 : c + 256], tile)
            tile = jnp.where(row == 2, below[:, c : c + 128], tile)
            tile = jnp.where(row == 3, below[:, c + 128 : c + 256], tile)
            sendbuf[pl.ds(pl.multiple_of((k * GRP + x) * SLOT + 32, 8), 8), :] = tile

    first = first_chunk(sim)

    def own_part(k):
        for h in range(CHUNK // 8):
            r = pl.multiple_of(k * CHUNK + 8 * h, 8)
            c, lap = in_plane(cbuf, r)
            s = sbuf[pl.ds(pl.multiple_of(r + 8, 8), 8), :]
            c_new[pl.ds(r, 8), :] = c + DIFF_C * lap + s * c * c - (FEED + KILL) * c

    own_part(first)

    def catalyst_chunk(n, _):
        k = lax.rem(first + n, CHUNKS)

        @pl.when(has_prev)
        def _():
            halo(1, 0, chunk_rows(k))(k).wait_recv()

        @pl.when(has_next)
        def _():
            halo(1, 1, chunk_rows(k))(k).wait_recv()

        for h in range(CHUNK // 8):
            r = pl.multiple_of(k * CHUNK + 8 * h, 8)
            rows = pl.ds(r, 8)
            new = c_new[rows, :] + DIFF_C * (c_up[rows, :] + c_dn[rows, :])
            c_new[pl.ds(r, 8), :] = new
            next_out[1, 0, pl.ds(r, 8), :] = new
            columns = jnp.zeros((8, 128), jnp.float32)
            for i, (tile, at) in enumerate(beside):
                moved = pltpu.roll(new[:, tile * 128 : tile * 128 + 128], (i - at) % 128, 1)
                columns = jnp.where(lane == i, moved, columns)
            edge_cols[pl.ds(pl.multiple_of(r + 8, 8), 8), :] = columns
            if h == 0:
                @pl.when(k == 0)
                def _(columns=columns):
                    edge_cols[0:8, :] = jnp.broadcast_to(columns[0:1], (8, 128))
            else:
                @pl.when(k == CHUNKS - 1)
                def _(columns=columns):
                    edge_cols[ROWS + 8 : ROWS + 16, :] = jnp.broadcast_to(columns[7:8], (8, 128))
            for tile in range(COLS // 128):
                slot = (k * GRP + tile // 2) * SLOT + (h * 2 + tile % 2) * 8
                sendbuf[pl.ds(pl.multiple_of(slot, 8), 8), :] = new[:, tile * 128 : tile * 128 + 128]

        send_tiles(k, 0, 32)

        @pl.when(n >= 2)
        def _():
            make_rim(lax.rem(first + n - 1, CHUNKS))
            send_tiles(lax.rem(first + n - 1, CHUNKS), 32, 8)

        @pl.when(n < CHUNKS - 1)
        def _():
            own_part(lax.rem(first + n + 1, CHUNKS))

        return 0

    lax.fori_loop(0, CHUNKS, catalyst_chunk, 0)
    last_two = [lax.rem(first + CHUNKS - 1 + n, CHUNKS) for n in range(2)]
    for k in last_two:
        make_rim(k)
    for k in last_two:
        send_tiles(k, 32, 8)

    def to_relay(way):
        return pltpu.make_async_remote_copy(
            src_ref=species.at[0, 0],
            dst_ref=passing,
            send_sem=halo_send.at[0, way],
            recv_sem=relay_recv,
            device_id=partner,
            device_id_type=MESH,
        )

    def from_relay(way):
        return pltpu.make_async_remote_copy(
            src_ref=passing,
            dst_ref=(s_up, s_dn)[way],
            send_sem=relay_send,
            recv_sem=halo_recv.at[0, way, 0],
            device_id=relayed_to,
            device_id_type=MESH,
        )

    for way, wanted, end in ((0, has_next, is_a), (1, has_prev, is_b)):
        @pl.when(wanted & jnp.logical_not(end))
        def _(way=way):
            halo(0, way, whole)(0).start()

        @pl.when(end)
        def _(way=way):
            to_relay(way).start()

    def wait_mixed(count, t):
        some = pl.ds(0, count * SLOT)
        return pltpu.make_async_remote_copy(
            src_ref=sendbuf.at[some, :], dst_ref=recvbuf.at[some, :],
            send_sem=mix_send, recv_sem=mix_recv.at[t], device_id=to(sim, grp), device_id_type=MESH,
        )

    extinct = 6.0 / (BLOCKS * MEMBERS)
    log2e = math.log2(math.e)
    thin, narrow = -extinct * log2e / 256.0, -8.0 * log2e / 256.0

    def render(i, _):
        t_now = lax.rem(team + 6 - i, 4)

        @pl.when(t_now == team)
        def _():
            one_slot = pl.ds(0, SLOT)
            pltpu.make_async_copy(sendbuf.at[one_slot, :], recvbuf.at[one_slot, :], own_sem).wait()
            wait_mixed(TEAM - 1, team).wait_recv()

        @pl.when(t_now != team)
        def _():
            wait_mixed(TEAM, t_now).wait_recv()

        for way, wanted in ((0, passes_up), (1, passes_down)):
            @pl.when((i == 3) & wanted)
            def _(way=way):
                to_relay(way).wait_recv()
                from_relay(way).start()

        base = t_now * (TEAM * SLOT)
        sides = jnp.concatenate(
            [
                recvbuf[pl.ds(base + 36, TEAM, stride=SLOT), :],
                recvbuf[pl.ds(base + 37, TEAM, stride=SLOT), :],
                jnp.zeros((128 - 2 * TEAM, 128), jnp.float32),
            ],
            axis=0,
        )
        sides = jnp.transpose(sides)

        for h in range(2):
            for par in range(2):
                near = 2 * par + 8 * h
                side = 3.0 * sides[1 + 8 * h : 9 + 8 * h] + sides[near : near + 8]

                def layer(p, sums, h=h, par=par, side=side):
                    at = pl.multiple_of(base + p * SLOT, 8)
                    rim = recvbuf[pl.ds(at + 32, 8), :]
                    rows = []
                    for t in range(2):
                        mine = recvbuf[pl.ds(at + (2 * h + t) * 8, 8), :]
                        across = recvbuf[pl.ds(at + (2 - 2 * h + t) * 8, 8), :]
                        if par == 0:
                            beyond = rim[t : t + 1] if h == 0 else across[7:8]
                            shifted = jnp.where(row == 0, beyond, pltpu.roll(mine, 1, 0))
                        else:
                            beyond = rim[2 + t : 3 + t] if h == 1 else across[0:1]
                            shifted = jnp.where(row == 7, beyond, pltpu.roll(mine, 7, 0))
                        rows.append(3.0 * mine + shifted)
                    leftmost = pltpu.roll(side, lax.rem(128 - p, 128), 1)
                    rightmost = pltpu.roll(side, 127 - TEAM - p, 1)
                    fwd = [pltpu.roll(v, 1, 1) for v in rows]
                    bwd = [pltpu.roll(v, 127, 1) for v in rows]
                    low = [jnp.where(lane == 0, leftmost, fwd[0]), jnp.where(lane == 0, fwd[0], fwd[1])]
                    high = [jnp.where(lane == 127, bwd[1], bwd[0]), jnp.where(lane == 127, rightmost, bwd[1])]
                    result = []
                    for cpar in range(2):
                        for t in range(2):
                            q = 3.0 * rows[t] + (low, high)[cpar][t]
                            red, green, blue, clear = sums[(cpar * 2 + t) * 4 : (cpar * 2 + t) * 4 + 4]
                            after = clear * jnp.exp2((q * q) * thin)
                            weight = clear - after
                            mid = q - 8.0
                            warm = mid * (3.0 / 16.0)
                            red = red + weight * jnp.tanh(warm)
                            green = green + weight * jnp.exp2((mid * mid) * narrow)
                            blue = blue + weight * jnp.tanh(warm + 0.6)
                            result += [red, green, blue, after]
                    return tuple(result)

                zero, one = jnp.zeros((8, 128), jnp.float32), jnp.ones((8, 128), jnp.float32)
                sums = lax.fori_loop(0, TEAM, layer, (zero, zero, zero, one) * 4, unroll=True)
                for j in range(16):
                    at = t_now * TOTALS + ((h * 2 + par) * 16 + j) * 8
                    totals[pl.ds(pl.multiple_of(at, 8), 8), :] = sums[j]
        return 0

    lax.fori_loop(0, 4, render, 0)

    def piece_rows(n):
        return pl.ds(pl.multiple_of(n * PIECE, PIECE), PIECE)

    for h in range(2):
        for par in range(2):
            for cpar in range(2):
                for t in range(2):
                    base = ((h * 2 + par) * 16 + (cpar * 2 + t) * 4) * 8
                    got = [[totals[i * TOTALS + base + 8 * ch : i * TOTALS + base + 8 * ch + 8, :] for ch in range(4)] for i in range(4)]
                    red, green, blue, clear = got[0]
                    for i in range(1, 4):
                        red = red + clear * got[i][0]
                        green = green + clear * got[i][1]
                        blue = blue + clear * got[i][2]
                        clear = clear * got[i][3]
                    for ch, value in enumerate((red, green, blue, clear)):
                        at = 8 * h * PIECE + ch * 8 + cpar * 4 + par * 2 + t
                        pack[pl.ds(at, 8, stride=PIECE), :] = value

        def send_piece(n, _, h=h):
            j = 8 * h + n
            there = region * REGION + j

            @pl.when(there != sim)
            def _():
                pltpu.make_async_remote_copy(
                    src_ref=pack.at[piece_rows(j), :],
                    dst_ref=parts.at[piece_rows(block), :],
                    send_sem=part_send,
                    recv_sem=part_recv,
                    device_id=to(there, grp),
                    device_id_type=MESH,
                ).start()

            return 0

        lax.fori_loop(0, 8, send_piece, 0)

    @pl.when(self_part)
    def _():
        mine = pltpu.make_async_copy(
            pack.at[piece_rows(lax.rem(sim, REGION)), :], parts.at[piece_rows(block), :], part_own
        )
        mine.start()
        mine.wait()

    def substrate_part(k, _):
        r = pl.multiple_of(8 * k, 8)
        s, lap = in_plane(sbuf, r)
        c = cbuf[pl.ds(pl.multiple_of(r + 8, 8), 8), :]
        next_out[0, 0, pl.ds(r, 8), :] = s + DIFF_S * lap - s * c * c + FEED * (1.0 - s)
        return 0

    lax.fori_loop(0, ROWS // 8, substrate_part, 0, unroll=4)

    @pl.when(has_prev)
    def _():
        halo(0, 0, whole)(0).wait_recv()

    @pl.when(has_next)
    def _():
        halo(0, 1, whole)(0).wait_recv()

    def substrate_rows(k, _):
        rows = pl.ds(pl.multiple_of(8 * k, 8), 8)
        next_out[0, 0, rows, :] = next_out[0, 0, rows, :] + DIFF_S * (s_up[rows, :] + s_dn[rows, :])
        return 0

    lax.fori_loop(0, ROWS // 8, substrate_rows, 0, unroll=4)

    old = lax.broadcasted_iota(jnp.int32, (256, 256), 0)
    new = lax.broadcasted_iota(jnp.int32, (256, 256), 1)
    spread = jnp.where(new == 2 * lax.rem(old, 128) + lax.div(old, 128), 1.0, 0.0).astype(jnp.bfloat16)

    def wait_parts(count):
        some = pl.ds(0, count * PIECE)
        return pltpu.make_async_remote_copy(
            src_ref=pack.at[some, :], dst_ref=parts.at[some, :],
            send_sem=part_send, recv_sem=part_recv, device_id=to(sim, grp), device_id_type=MESH,
        )

    @pl.when(self_part)
    def _():
        wait_parts(BLOCKS - 1).wait_recv()

    @pl.when(jnp.logical_not(self_part))
    def _():
        wait_parts(BLOCKS).wait_recv()

    def add_block(b, totals):
        base = pl.multiple_of(b * PIECE, 8)
        red, green, blue, clear = totals
        got = [parts[pl.ds(base + 8 * ch, 8), :] for ch in range(4)]
        return (
            red + clear * got[0], green + clear * got[1], blue + clear * got[2], clear * got[3],
        )

    zero, one = jnp.zeros((8, 128), jnp.float32), jnp.ones((8, 128), jnp.float32)
    red, green, blue, clear = lax.fori_loop(0, BLOCKS, add_block, (zero, zero, zero, one), unroll=True)
    opaque = 1.0 - clear
    channels = [0.5 * (opaque + red), green, 0.5 * (opaque - blue), opaque]
    flat = jnp.concatenate([jnp.concatenate([v[0:4], v[4:8]], axis=1) for v in channels], axis=0)
    bf16 = jnp.bfloat16
    high = flat.astype(bf16)
    rest = flat - high.astype(jnp.float32)
    middle = rest.astype(bf16)
    low = (rest - middle.astype(jnp.float32)).astype(bf16)
    split = jnp.dot(
        jnp.concatenate([high, middle, low], axis=0), spread, preferred_element_type=jnp.float32
    )
    mixed = split[0:16] + (split[16:32] + split[32:48])
    for ch in range(4):
        for par in range(2):
            for t in range(2):
                n = ch * 4 + par * 2 + t
                frame_out[ch, par : par + 1, t * 256 : t * 256 + 256] = mixed[n : n + 1]

    @pl.when(is_relay)
    def _():
        from_relay(0).wait_send()

    for i in range(2):
        @pl.when(has_next)
        def _(i=i):
            halo(i, 0, whole)(0).wait_send()

        @pl.when(has_prev)
        def _(i=i):
            halo(i, 1, whole)(0).wait_send()

    wait_mixed(MEMBERS - 1, team).wait_send()

    @pl.when(self_part)
    def _():
        wait_parts(BLOCKS - 1).wait_send()

    @pl.when(jnp.logical_not(self_part))
    def _():
        wait_parts(BLOCKS).wait_send()


def shards(species):
    f32 = jnp.float32
    plane = pltpu.VMEM((ROWS, COLS), f32)
    padded = pltpu.VMEM((ROWS + 16, COLS), f32)
    dma = pltpu.SemaphoreType.DMA
    fresh, frame = pl.pallas_call(
        kernel,
        out_shape=(
            jax.ShapeDtypeStruct((2, 1, ROWS, COLS), f32),
            jax.ShapeDtypeStruct((4, 2 * ROWS // SIMS, 2 * COLS // GRP), f32),
        ),
        in_specs=[pl.BlockSpec(memory_space=pltpu.HBM)],
        out_specs=(pl.BlockSpec(memory_space=pltpu.VMEM),) * 2,
        scratch_shapes=[
            padded, padded, plane, plane, plane, plane, plane,
            plane,
            pltpu.VMEM((ROWS + 16, 128), f32),
            pltpu.VMEM((MEMBERS * SLOT, 128), f32),
            pltpu.VMEM((MEMBERS * SLOT, 128), f32),
            pltpu.VMEM((4 * TOTALS, 128), f32),
            pltpu.VMEM((REGION * PIECE, 128), f32),
            pltpu.VMEM((BLOCKS * PIECE, 128), f32),
            dma((2,)), dma((2, 2)), dma((2, 2, CHUNKS)), dma, dma,
            dma, dma, dma((4,)), dma, dma, dma,
        ],
        compiler_params=pltpu.CompilerParams(
            collective_id=0, has_side_effects=True, vmem_limit_bytes=32 * 1024 * 1024
        ),
        cost_estimate=pl.CostEstimate(flops=20_000_000, bytes_accessed=4_000_000, transcendentals=2_000_000),
    )(pltpu.with_memory_space_constraint(species, pltpu.HBM))
    return fresh, frame


def solution(mesh):
    return jax.shard_map(
        shards,
        mesh=mesh,
        in_specs=(P(None, ("sim", "grp"), None, None),),
        out_specs=(P(None, ("sim", "grp"), None, None), P(None, "sim", "grp")),
        check_vma=False,
    )
```

```python
import math

import jax
import jax.numpy as jnp
from jax import lax
from jax.experimental import pallas as pl
from jax.experimental.pallas import tpu as pltpu
from jax.sharding import PartitionSpec as P

MESH = pl.DeviceIdType.MESH

ROWS = 128
COLS = 1024
GRP = 4
SIMS = 128
SUB = 8
BLOCKS = SIMS // SUB
MEMBERS = GRP * SUB
REGION = ROWS // SUB
CHUNKS = 8
CHUNK = ROWS // CHUNKS
SLOT = 40
PIECE = 32
TEAM = MEMBERS // 4
TOTALS = 64 * 8

DIFF_S, DIFF_C, FEED, KILL = 0.16, 0.08, 0.035, 0.065


def to(sim, grp):
    return {"sim": sim, "grp": grp}


def in_plane(buf, r):
    window = buf[pl.ds(r, 24), :]
    center = window[8:16]
    lane = lax.broadcasted_iota(jnp.int32, (8, COLS), 1)
    left = jnp.where(lane == 0, 0.0, pltpu.roll(center, 1, 1))
    right = jnp.where(lane == COLS - 1, 0.0, pltpu.roll(center, COLS - 1, 1))
    return center, window[7:15] + window[9:17] + left + right - 6.0 * center


def kernel(
    species, next_out, frame_out,
    sbuf, cbuf, s_up, s_dn, c_up, c_dn, passing, c_new, edge_cols, sendbuf, recvbuf, totals, pack, parts,
    load_sem, halo_send, halo_recv, relay_send, relay_recv, own_sem, mix_send, mix_recv, part_own, part_send, part_recv,
):
    sim, grp = lax.axis_index("sim"), lax.axis_index("grp")
    plane = sim * GRP + grp
    block, member = lax.div(sim, SUB), lax.rem(sim, SUB)
    seat = member * GRP + grp
    turn = lax.div(block, 4) + lax.rem(block, 4)

    def region_of(m, turn):
        return 2 * lax.rem(lax.div(m, 2) + 8 - turn, 4) + lax.rem(m, 2)

    def member_of(q, turn):
        return 2 * lax.rem(lax.div(q, 2) + turn, 4) + lax.rem(q, 2)

    def first_chunk(sim):
        block = lax.div(sim, SUB)
        place = lax.div(lax.rem(sim, SUB), 2) + 1 + 8 - lax.div(block, 4) - lax.rem(block, 4)
        return 2 * lax.rem(place, 4)

    region = region_of(member, turn)
    team = lax.div(member, 2)

    def source(b):
        t = b // 4 + b % 4
        return b * SUB + member_of(lax.div(sim, REGION), t)

    loads = [
        pltpu.make_async_copy(species.at[i, 0], buf.at[pl.ds(8, ROWS), :], load_sem.at[i])
        for i, buf in ((0, sbuf), (1, cbuf))
    ]
    loads[1].start()
    loads[0].start()

    has_prev, has_next = plane > 0, plane < SIMS * GRP - 1
    prev = to(lax.div(plane - 1, GRP), lax.rem(plane - 1 + GRP, GRP))
    nxt = to(lax.div(plane + 1, GRP), lax.rem(plane + 1, GRP))

    odd = lax.rem(sim, 2)
    partner = to(sim + 2 * odd - 1, grp)
    crossing = (sim + odd > 0) & (sim + odd < SIMS)
    is_a, is_b = crossing & (odd == 1) & (grp == GRP - 1), crossing & (odd == 0) & (grp == 0)
    is_relay = crossing & (((odd == 0) & (grp == GRP - 1)) | ((odd == 1) & (grp == 0)))
    passes_up = is_relay & (odd == 0)
    passes_down = is_relay & (odd == 1)
    relayed_to = to(sim, GRP - 1 - grp)
    barrier = pltpu.get_barrier_semaphore()
    for b in range(BLOCKS):
        there = source(b)

        @pl.when(there != sim)
        def _(there=there):
            pl.semaphore_signal(barrier, inc=1, device_id=to(there, grp), device_id_type=MESH)


    @pl.when(has_prev)
    def _():
        pl.semaphore_signal(barrier, inc=1, device_id=prev, device_id_type=MESH)

    @pl.when(has_next)
    def _():
        pl.semaphore_signal(barrier, inc=1, device_id=nxt, device_id_type=MESH)

    @pl.when(is_relay)
    def _():
        pl.semaphore_signal(barrier, inc=1, device_id=partner, device_id_type=MESH)

    def greet_member(d, _):
        other = lax.rem(seat + d, MEMBERS)
        there = to(block * SUB + lax.div(other, GRP), lax.rem(other, GRP))
        pl.semaphore_signal(barrier, inc=1, device_id=there, device_id_type=MESH)
        return 0

    lax.fori_loop(1, MEMBERS, greet_member, 0)

    for buf in (sbuf, cbuf):
        buf[0:8, :] = jnp.zeros((8, COLS), jnp.float32)
        buf[ROWS + 8 : ROWS + 16, :] = jnp.zeros((8, COLS), jnp.float32)

    @pl.when(plane == 0)
    def _():
        s_up[...] = jnp.zeros_like(s_up)
        c_up[...] = jnp.zeros_like(c_up)

    @pl.when(plane == SIMS * GRP - 1)
    def _():
        s_dn[...] = jnp.zeros_like(s_dn)
        c_dn[...] = jnp.zeros_like(c_dn)

    self_part = lax.div(sim, REGION) == region
    expected = MEMBERS - 1 + BLOCKS - self_part.astype(jnp.int32)
    for wanted in (has_prev, has_next, is_a, is_b):
        expected = expected + wanted.astype(jnp.int32)
    pl.semaphore_wait(barrier, expected)

    def halo(i, way, rows):
        target = ((s_up, s_dn), (c_up, c_dn))[i][way]
        return lambda chunk: pltpu.make_async_remote_copy(
            src_ref=species.at[i, 0, rows, :],
            dst_ref=target.at[rows, :],
            send_sem=halo_send.at[i, way],
            recv_sem=halo_recv.at[i, way, chunk],
            device_id=(nxt, prev)[way],
            device_id_type=MESH,
        )

    def chunk_rows(k):
        return pl.ds(pl.multiple_of(k * CHUNK, CHUNK), CHUNK)

    whole = pl.ds(0, ROWS)

    first_next, first_prev = first_chunk(nxt["sim"]), first_chunk(prev["sim"])

    def send_catalyst(n, _):
        @pl.when(has_next)
        def _():
            k = lax.rem(first_next + n, CHUNKS)
            halo(1, 0, chunk_rows(k))(k).start()

        @pl.when(has_prev)
        def _():
            k = lax.rem(first_prev + n, CHUNKS)
            halo(1, 1, chunk_rows(k))(k).start()

        return 0

    lax.fori_loop(0, CHUNKS, send_catalyst, 0)
    loads[1].wait()
    loads[0].wait()

    lane = lax.broadcasted_iota(jnp.int32, (8, 128), 1)
    row = lax.broadcasted_iota(jnp.int32, (8, 128), 0)
    beside = [(0, 0), (2, 0), (1, 127), (4, 0), (3, 127), (6, 0), (5, 127), (7, 127)]

    def mix(k, x, start, length):
        m = member_of(k, turn)
        source_rows = pl.ds(pl.multiple_of((k * GRP + x) * SLOT + start, 8), length)
        target_rows = pl.ds(pl.multiple_of(seat * SLOT + start, 8), length)
        away = pltpu.make_async_remote_copy(
            src_ref=sendbuf.at[source_rows, :],
            dst_ref=recvbuf.at[target_rows, :],
            send_sem=mix_send,
            recv_sem=mix_recv.at[team],
            device_id=to(block * SUB + m, x),
            device_id_type=MESH,
        )
        here = pltpu.make_async_copy(sendbuf.at[source_rows, :], recvbuf.at[target_rows, :], own_sem)
        return away, here, m * GRP + x == seat

    def send_tiles(k, start, length):
        for dx in range(1, GRP + 1):
            away, here, stays = mix(k, lax.rem(grp + dx, GRP), start, length)

            @pl.when(stays)
            def _(here=here):
                here.start()

            @pl.when(jnp.logical_not(stays))
            def _(away=away):
                away.start()

    def make_rim(k):
        top = c_new[pl.ds(pl.multiple_of(jnp.maximum(k * REGION - 8, 0), 8), 8), :]
        bottom = c_new[pl.ds(pl.multiple_of(jnp.minimum(k * REGION + REGION, ROWS - 8), 8), 8), :]
        above = jnp.where(k == 0, top[0:1], top[7:8])
        below = jnp.where(k == SUB - 1, bottom[7:8], bottom[0:1])
        window = edge_cols[pl.ds(pl.multiple_of(k * REGION, 8), 32), :]
        window = jnp.concatenate([window, jnp.zeros((96, 128), jnp.float32)], axis=0)
        cols = pltpu.roll(jnp.transpose(window)[0:8], 121, 1)
        for x in range(GRP):
            c = 2 * x * 128
            tile = pltpu.roll(cols, (4 - 2 * x) % 8, 0)
            tile = jnp.where(row == 0, above[:, c : c + 128], tile)
            tile = jnp.where(row == 1, above[:, c + 128 : c + 256], tile)
            tile = jnp.where(row == 2, below[:, c : c + 128], tile)
            tile = jnp.where(row == 3, below[:, c + 128 : c + 256], tile)
            sendbuf[pl.ds(pl.multiple_of((k * GRP + x) * SLOT + 32, 8), 8), :] = tile

    first = first_chunk(sim)

    def catalyst_chunk(n, _):
        k = lax.rem(first + n, CHUNKS)

        @pl.when(has_prev)
        def _():
            halo(1, 0, chunk_rows(k))(k).wait_recv()

        @pl.when(has_next)
        def _():
            halo(1, 1, chunk_rows(k))(k).wait_recv()

        for h in range(CHUNK // 8):
            r = pl.multiple_of(k * CHUNK + 8 * h, 8)
            c, lap = in_plane(cbuf, r)
            lap = lap + c_up[pl.ds(r, 8), :] + c_dn[pl.ds(r, 8), :]
            s = sbuf[pl.ds(pl.multiple_of(r + 8, 8), 8), :]
            new = c + DIFF_C * lap + s * c * c - (FEED + KILL) * c
            c_new[pl.ds(r, 8), :] = new
            next_out[1, 0, pl.ds(r, 8), :] = new
            columns = jnp.zeros((8, 128), jnp.float32)
            for i, (tile, at) in enumerate(beside):
                moved = pltpu.roll(new[:, tile * 128 : tile * 128 + 128], (i - at) % 128, 1)
                columns = jnp.where(lane == i, moved, columns)
            edge_cols[pl.ds(pl.multiple_of(r + 8, 8), 8), :] = columns
            if h == 0:
                @pl.when(k == 0)
                def _(columns=columns):
                    edge_cols[0:8, :] = jnp.broadcast_to(columns[0:1], (8, 128))
            else:
                @pl.when(k == CHUNKS - 1)
                def _(columns=columns):
                    edge_cols[ROWS + 8 : ROWS + 16, :] = jnp.broadcast_to(columns[7:8], (8, 128))
            for tile in range(COLS // 128):
                slot = (k * GRP + tile // 2) * SLOT + (h * 2 + tile % 2) * 8
                sendbuf[pl.ds(pl.multiple_of(slot, 8), 8), :] = new[:, tile * 128 : tile * 128 + 128]

        send_tiles(k, 0, 32)

        @pl.when(n >= 2)
        def _():
            make_rim(lax.rem(first + n - 1, CHUNKS))
            send_tiles(lax.rem(first + n - 1, CHUNKS), 32, 8)

        return 0

    lax.fori_loop(0, CHUNKS, catalyst_chunk, 0)
    last_two = [lax.rem(first + CHUNKS - 1 + n, CHUNKS) for n in range(2)]
    for k in last_two:
        make_rim(k)
    for k in last_two:
        send_tiles(k, 32, 8)

    near_half, far_half = pl.ds(0, ROWS // 2), pl.ds(ROWS // 2, ROWS // 2)

    def to_relay(way):
        return pltpu.make_async_remote_copy(
            src_ref=species.at[0, 0, far_half, :],
            dst_ref=passing,
            send_sem=halo_send.at[0, way],
            recv_sem=relay_recv,
            device_id=partner,
            device_id_type=MESH,
        )

    def from_relay(way):
        return pltpu.make_async_remote_copy(
            src_ref=passing,
            dst_ref=(s_up, s_dn)[way].at[far_half, :],
            send_sem=relay_send,
            recv_sem=halo_recv.at[0, way, 0],
            device_id=relayed_to,
            device_id_type=MESH,
        )

    for way, wanted, end in ((0, has_next, is_a), (1, has_prev, is_b)):
        @pl.when(wanted & jnp.logical_not(end))
        def _(way=way):
            halo(0, way, whole)(0).start()

        @pl.when(end)
        def _(way=way):
            to_relay(way).start()
            halo(0, way, near_half)(0).start()

    def wait_mixed(count, t):
        some = pl.ds(0, count * SLOT)
        return pltpu.make_async_remote_copy(
            src_ref=sendbuf.at[some, :], dst_ref=recvbuf.at[some, :],
            send_sem=mix_send, recv_sem=mix_recv.at[t], device_id=to(sim, grp), device_id_type=MESH,
        )

    extinct = 6.0 / (BLOCKS * MEMBERS)
    log2e = math.log2(math.e)
    thin, narrow = -extinct * log2e / 256.0, -8.0 * log2e / 256.0

    def render(i, _):
        t_now = lax.rem(team + 6 - i, 4)

        @pl.when(t_now == team)
        def _():
            one_slot = pl.ds(0, SLOT)
            pltpu.make_async_copy(sendbuf.at[one_slot, :], recvbuf.at[one_slot, :], own_sem).wait()
            wait_mixed(TEAM - 1, team).wait_recv()

        @pl.when(t_now != team)
        def _():
            wait_mixed(TEAM, t_now).wait_recv()

        for way, wanted in ((0, passes_up), (1, passes_down)):
            @pl.when((i == 3) & wanted)
            def _(way=way):
                to_relay(way).wait_recv()
                from_relay(way).start()

        base = t_now * (TEAM * SLOT)
        sides = jnp.concatenate(
            [
                recvbuf[pl.ds(base + 36, TEAM, stride=SLOT), :],
                recvbuf[pl.ds(base + 37, TEAM, stride=SLOT), :],
                jnp.zeros((128 - 2 * TEAM, 128), jnp.float32),
            ],
            axis=0,
        )
        sides = jnp.transpose(sides)

        for h in range(2):
            for par in range(2):
                near = 2 * par + 8 * h
                side = 3.0 * sides[1 + 8 * h : 9 + 8 * h] + sides[near : near + 8]

                def layer(p, sums, h=h, par=par, side=side):
                    at = pl.multiple_of(base + p * SLOT, 8)
                    rim = recvbuf[pl.ds(at + 32, 8), :]
                    rows = []
                    for t in range(2):
                        mine = recvbuf[pl.ds(at + (2 * h + t) * 8, 8), :]
                        across = recvbuf[pl.ds(at + (2 - 2 * h + t) * 8, 8), :]
                        if par == 0:
                            beyond = rim[t : t + 1] if h == 0 else across[7:8]
                            shifted = jnp.where(row == 0, beyond, pltpu.roll(mine, 1, 0))
                        else:
                            beyond = rim[2 + t : 3 + t] if h == 1 else across[0:1]
                            shifted = jnp.where(row == 7, beyond, pltpu.roll(mine, 7, 0))
                        rows.append(3.0 * mine + shifted)
                    leftmost = pltpu.roll(side, lax.rem(128 - p, 128), 1)
                    rightmost = pltpu.roll(side, 127 - TEAM - p, 1)
                    fwd = [pltpu.roll(v, 1, 1) for v in rows]
                    bwd = [pltpu.roll(v, 127, 1) for v in rows]
                    low = [jnp.where(lane == 0, leftmost, fwd[0]), jnp.where(lane == 0, fwd[0], fwd[1])]
                    high = [jnp.where(lane == 127, bwd[1], bwd[0]), jnp.where(lane == 127, rightmost, bwd[1])]
                    result = []
                    for cpar in range(2):
                        for t in range(2):
                            q = 3.0 * rows[t] + (low, high)[cpar][t]
                            red, green, blue, clear = sums[(cpar * 2 + t) * 4 : (cpar * 2 + t) * 4 + 4]
                            after = clear * jnp.exp2((q * q) * thin)
                            weight = clear - after
                            mid = q - 8.0
                            warm = mid * (3.0 / 16.0)
                            red = red + weight * jnp.tanh(warm)
                            green = green + weight * jnp.exp2((mid * mid) * narrow)
                            blue = blue + weight * jnp.tanh(warm + 0.6)
                            result += [red, green, blue, after]
                    return tuple(result)

                zero, one = jnp.zeros((8, 128), jnp.float32), jnp.ones((8, 128), jnp.float32)
                sums = lax.fori_loop(0, TEAM, layer, (zero, zero, zero, one) * 4, unroll=True)
                for j in range(16):
                    at = t_now * TOTALS + ((h * 2 + par) * 16 + j) * 8
                    totals[pl.ds(pl.multiple_of(at, 8), 8), :] = sums[j]
        return 0

    lax.fori_loop(0, 4, render, 0)

    def piece_rows(n):
        return pl.ds(pl.multiple_of(n * PIECE, PIECE), PIECE)

    for h in range(2):
        for par in range(2):
            for cpar in range(2):
                for t in range(2):
                    base = ((h * 2 + par) * 16 + (cpar * 2 + t) * 4) * 8
                    got = [[totals[i * TOTALS + base + 8 * ch : i * TOTALS + base + 8 * ch + 8, :] for ch in range(4)] for i in range(4)]
                    red, green, blue, clear = got[0]
                    for i in range(1, 4):
                        red = red + clear * got[i][0]
                        green = green + clear * got[i][1]
                        blue = blue + clear * got[i][2]
                        clear = clear * got[i][3]
                    for ch, value in enumerate((red, green, blue, clear)):
                        at = 8 * h * PIECE + ch * 8 + cpar * 4 + par * 2 + t
                        pack[pl.ds(at, 8, stride=PIECE), :] = value

        def send_piece(n, _, h=h):
            j = 8 * h + n
            there = region * REGION + j

            @pl.when(there != sim)
            def _():
                pltpu.make_async_remote_copy(
                    src_ref=pack.at[piece_rows(j), :],
                    dst_ref=parts.at[piece_rows(block), :],
                    send_sem=part_send,
                    recv_sem=part_recv,
                    device_id=to(there, grp),
                    device_id_type=MESH,
                ).start()

            return 0

        lax.fori_loop(0, 8, send_piece, 0)

    @pl.when(self_part)
    def _():
        mine = pltpu.make_async_copy(
            pack.at[piece_rows(lax.rem(sim, REGION)), :], parts.at[piece_rows(block), :], part_own
        )
        mine.start()
        mine.wait()

    def substrate_part(k, _):
        r = pl.multiple_of(8 * k, 8)
        s, lap = in_plane(sbuf, r)
        c = cbuf[pl.ds(pl.multiple_of(r + 8, 8), 8), :]
        next_out[0, 0, pl.ds(r, 8), :] = s + DIFF_S * lap - s * c * c + FEED * (1.0 - s)
        return 0

    lax.fori_loop(0, ROWS // 8, substrate_part, 0, unroll=4)

    @pl.when(has_prev)
    def _():
        halo(0, 0, whole)(0).wait_recv()

    @pl.when(has_next)
    def _():
        halo(0, 1, whole)(0).wait_recv()

    def substrate_rows(k, _):
        rows = pl.ds(pl.multiple_of(8 * k, 8), 8)
        next_out[0, 0, rows, :] = next_out[0, 0, rows, :] + DIFF_S * (s_up[rows, :] + s_dn[rows, :])
        return 0

    lax.fori_loop(0, ROWS // 8, substrate_rows, 0, unroll=4)

    old = lax.broadcasted_iota(jnp.int32, (256, 256), 0)
    new = lax.broadcasted_iota(jnp.int32, (256, 256), 1)
    spread = jnp.where(new == 2 * lax.rem(old, 128) + lax.div(old, 128), 1.0, 0.0).astype(jnp.bfloat16)

    def wait_parts(count):
        some = pl.ds(0, count * PIECE)
        return pltpu.make_async_remote_copy(
            src_ref=pack.at[some, :], dst_ref=parts.at[some, :],
            send_sem=part_send, recv_sem=part_recv, device_id=to(sim, grp), device_id_type=MESH,
        )

    @pl.when(self_part)
    def _():
        wait_parts(BLOCKS - 1).wait_recv()

    @pl.when(jnp.logical_not(self_part))
    def _():
        wait_parts(BLOCKS).wait_recv()

    def add_block(b, totals):
        base = pl.multiple_of(b * PIECE, 8)
        red, green, blue, clear = totals
        got = [parts[pl.ds(base + 8 * ch, 8), :] for ch in range(4)]
        return (
            red + clear * got[0], green + clear * got[1], blue + clear * got[2], clear * got[3],
        )

    zero, one = jnp.zeros((8, 128), jnp.float32), jnp.ones((8, 128), jnp.float32)
    red, green, blue, clear = lax.fori_loop(0, BLOCKS, add_block, (zero, zero, zero, one), unroll=True)
    opaque = 1.0 - clear
    channels = [0.5 * (opaque + red), green, 0.5 * (opaque - blue), opaque]
    flat = jnp.concatenate([jnp.concatenate([v[0:4], v[4:8]], axis=1) for v in channels], axis=0)
    bf16 = jnp.bfloat16
    high = flat.astype(bf16)
    rest = flat - high.astype(jnp.float32)
    middle = rest.astype(bf16)
    low = (rest - middle.astype(jnp.float32)).astype(bf16)
    split = jnp.dot(
        jnp.concatenate([high, middle, low], axis=0), spread, preferred_element_type=jnp.float32
    )
    mixed = split[0:16] + (split[16:32] + split[32:48])
    for ch in range(4):
        for par in range(2):
            for t in range(2):
                n = ch * 4 + par * 2 + t
                frame_out[ch, par : par + 1, t * 256 : t * 256 + 256] = mixed[n : n + 1]

    @pl.when(is_relay)
    def _():
        from_relay(0).wait_send()

    for i in range(2):
        @pl.when(has_next)
        def _(i=i):
            halo(i, 0, whole)(0).wait_send()

        @pl.when(has_prev)
        def _(i=i):
            halo(i, 1, whole)(0).wait_send()

    wait_mixed(MEMBERS - 1, team).wait_send()

    @pl.when(self_part)
    def _():
        wait_parts(BLOCKS - 1).wait_send()

    @pl.when(jnp.logical_not(self_part))
    def _():
        wait_parts(BLOCKS).wait_send()


def shards(species):
    f32 = jnp.float32
    plane = pltpu.VMEM((ROWS, COLS), f32)
    padded = pltpu.VMEM((ROWS + 16, COLS), f32)
    dma = pltpu.SemaphoreType.DMA
    fresh, frame = pl.pallas_call(
        kernel,
        out_shape=(
            jax.ShapeDtypeStruct((2, 1, ROWS, COLS), f32),
            jax.ShapeDtypeStruct((4, 2 * ROWS // SIMS, 2 * COLS // GRP), f32),
        ),
        in_specs=[pl.BlockSpec(memory_space=pltpu.HBM)],
        out_specs=(pl.BlockSpec(memory_space=pltpu.VMEM),) * 2,
        scratch_shapes=[
            padded, padded, plane, plane, plane, plane, pltpu.VMEM((ROWS // 2, COLS), f32),
            plane,
            pltpu.VMEM((ROWS + 16, 128), f32),
            pltpu.VMEM((MEMBERS * SLOT, 128), f32),
            pltpu.VMEM((MEMBERS * SLOT, 128), f32),
            pltpu.VMEM((4 * TOTALS, 128), f32),
            pltpu.VMEM((REGION * PIECE, 128), f32),
            pltpu.VMEM((BLOCKS * PIECE, 128), f32),
            dma((2,)), dma((2, 2)), dma((2, 2, CHUNKS)), dma, dma,
            dma, dma, dma((4,)), dma, dma, dma,
        ],
        compiler_params=pltpu.CompilerParams(
            collective_id=0, has_side_effects=True, vmem_limit_bytes=32 * 1024 * 1024
        ),
        cost_estimate=pl.CostEstimate(flops=20_000_000, bytes_accessed=4_000_000, transcendentals=2_000_000),
    )(pltpu.with_memory_space_constraint(species, pltpu.HBM))
    return fresh, frame


def solution(mesh):
    return jax.shard_map(
        shards,
        mesh=mesh,
        in_specs=(P(None, ("sim", "grp"), None, None),),
        out_specs=(P(None, ("sim", "grp"), None, None), P(None, "sim", "grp")),
        check_vma=False,
    )
```

```python
import math

import jax
import jax.numpy as jnp
from jax import lax
from jax.experimental import pallas as pl
from jax.experimental.pallas import tpu as pltpu
from jax.sharding import PartitionSpec as P

MESH = pl.DeviceIdType.MESH

ROWS = 128
COLS = 1024
GRP = 4
SIMS = 128
SUB = 8
BLOCKS = SIMS // SUB
MEMBERS = GRP * SUB
REGION = ROWS // SUB
CHUNKS = 8
CHUNK = ROWS // CHUNKS
SLOT = 40
PIECE = 32
TEAM = MEMBERS // 4
TOTALS = 64 * 8

DIFF_S, DIFF_C, FEED, KILL = 0.16, 0.08, 0.035, 0.065


def to(sim, grp):
    return {"sim": sim, "grp": grp}


def in_plane(buf, r):
    window = buf[pl.ds(r, 24), :]
    center = window[8:16]
    lane = lax.broadcasted_iota(jnp.int32, (8, COLS), 1)
    left = jnp.where(lane == 0, 0.0, pltpu.roll(center, 1, 1))
    right = jnp.where(lane == COLS - 1, 0.0, pltpu.roll(center, COLS - 1, 1))
    return center, window[7:15] + window[9:17] + left + right - 6.0 * center


def kernel(
    species, next_out, frame_out,
    sbuf, cbuf, s_up, s_dn, c_up, c_dn, passing, c_new, edge_cols, sendbuf, recvbuf, totals, pack, parts,
    load_sem, halo_send, halo_recv, relay_send, relay_recv, own_sem, mix_send, mix_recv, part_own, part_send, part_recv,
):
    sim, grp = lax.axis_index("sim"), lax.axis_index("grp")
    plane = sim * GRP + grp
    block, member = lax.div(sim, SUB), lax.rem(sim, SUB)
    seat = member * GRP + grp
    turn = lax.div(block, 4) + lax.rem(block, 4)

    def region_of(m, turn):
        return 2 * lax.rem(lax.div(m, 2) + 8 - turn, 4) + lax.rem(m, 2)

    def member_of(q, turn):
        return 2 * lax.rem(lax.div(q, 2) + turn, 4) + lax.rem(q, 2)

    def first_chunk(sim):
        block = lax.div(sim, SUB)
        place = lax.div(lax.rem(sim, SUB), 2) + 1 + 8 - lax.div(block, 4) - lax.rem(block, 4)
        return 2 * lax.rem(place, 4)

    region = region_of(member, turn)
    team = lax.div(member, 2)

    def source(b):
        t = b // 4 + b % 4
        return b * SUB + member_of(lax.div(sim, REGION), t)

    loads = [
        pltpu.make_async_copy(species.at[i, 0], buf.at[pl.ds(8, ROWS), :], load_sem.at[i])
        for i, buf in ((0, sbuf), (1, cbuf))
    ]
    loads[1].start()
    loads[0].start()

    has_prev, has_next = plane > 0, plane < SIMS * GRP - 1
    prev = to(lax.div(plane - 1, GRP), lax.rem(plane - 1 + GRP, GRP))
    nxt = to(lax.div(plane + 1, GRP), lax.rem(plane + 1, GRP))

    odd = lax.rem(sim, 2)
    partner = to(sim + 2 * odd - 1, grp)
    crossing = (sim + odd > 0) & (sim + odd < SIMS)
    is_a, is_b = crossing & (odd == 1) & (grp == GRP - 1), crossing & (odd == 0) & (grp == 0)
    is_relay = crossing & (((odd == 0) & (grp == GRP - 1)) | ((odd == 1) & (grp == 0)))
    passes_up = is_relay & (odd == 0)
    passes_down = is_relay & (odd == 1)
    relayed_to = to(sim, GRP - 1 - grp)
    barrier = pltpu.get_barrier_semaphore()
    for b in range(BLOCKS):
        there = source(b)

        @pl.when(there != sim)
        def _(there=there):
            pl.semaphore_signal(barrier, inc=1, device_id=to(there, grp), device_id_type=MESH)


    @pl.when(has_prev)
    def _():
        pl.semaphore_signal(barrier, inc=1, device_id=prev, device_id_type=MESH)

    @pl.when(has_next)
    def _():
        pl.semaphore_signal(barrier, inc=1, device_id=nxt, device_id_type=MESH)

    @pl.when(is_relay)
    def _():
        pl.semaphore_signal(barrier, inc=1, device_id=partner, device_id_type=MESH)

    def greet_member(d, _):
        other = lax.rem(seat + d, MEMBERS)
        there = to(block * SUB + lax.div(other, GRP), lax.rem(other, GRP))
        pl.semaphore_signal(barrier, inc=1, device_id=there, device_id_type=MESH)
        return 0

    lax.fori_loop(1, MEMBERS, greet_member, 0)

    for buf in (sbuf, cbuf):
        buf[0:8, :] = jnp.zeros((8, COLS), jnp.float32)
        buf[ROWS + 8 : ROWS + 16, :] = jnp.zeros((8, COLS), jnp.float32)

    @pl.when(plane == 0)
    def _():
        s_up[...] = jnp.zeros_like(s_up)
        c_up[...] = jnp.zeros_like(c_up)

    @pl.when(plane == SIMS * GRP - 1)
    def _():
        s_dn[...] = jnp.zeros_like(s_dn)
        c_dn[...] = jnp.zeros_like(c_dn)

    self_part = lax.div(sim, REGION) == region
    expected = MEMBERS - 1 + BLOCKS - self_part.astype(jnp.int32)
    for wanted in (has_prev, has_next, is_a, is_b):
        expected = expected + wanted.astype(jnp.int32)
    pl.semaphore_wait(barrier, expected)

    def halo(i, way, rows):
        target = ((s_up, s_dn), (c_up, c_dn))[i][way]
        return lambda chunk: pltpu.make_async_remote_copy(
            src_ref=species.at[i, 0, rows, :],
            dst_ref=target.at[rows, :],
            send_sem=halo_send.at[i, way],
            recv_sem=halo_recv.at[i, way, chunk],
            device_id=(nxt, prev)[way],
            device_id_type=MESH,
        )

    def chunk_rows(k):
        return pl.ds(pl.multiple_of(k * CHUNK, CHUNK), CHUNK)

    whole = pl.ds(0, ROWS)

    first_next, first_prev = first_chunk(nxt["sim"]), first_chunk(prev["sim"])

    def send_catalyst(n, _):
        @pl.when(has_next)
        def _():
            k = lax.rem(first_next + n, CHUNKS)
            halo(1, 0, chunk_rows(k))(k).start()

        @pl.when(has_prev)
        def _():
            k = lax.rem(first_prev + n, CHUNKS)
            halo(1, 1, chunk_rows(k))(k).start()

        return 0

    lax.fori_loop(0, CHUNKS, send_catalyst, 0)
    loads[1].wait()
    loads[0].wait()

    lane = lax.broadcasted_iota(jnp.int32, (8, 128), 1)
    row = lax.broadcasted_iota(jnp.int32, (8, 128), 0)
    beside = [(0, 0), (2, 0), (1, 127), (4, 0), (3, 127), (6, 0), (5, 127), (7, 127)]

    def mix(k, x, start, length):
        m = member_of(k, turn)
        source_rows = pl.ds(pl.multiple_of((k * GRP + x) * SLOT + start, 8), length)
        target_rows = pl.ds(pl.multiple_of(seat * SLOT + start, 8), length)
        away = pltpu.make_async_remote_copy(
            src_ref=sendbuf.at[source_rows, :],
            dst_ref=recvbuf.at[target_rows, :],
            send_sem=mix_send,
            recv_sem=mix_recv.at[team],
            device_id=to(block * SUB + m, x),
            device_id_type=MESH,
        )
        here = pltpu.make_async_copy(sendbuf.at[source_rows, :], recvbuf.at[target_rows, :], own_sem)
        return away, here, m * GRP + x == seat

    def send_tiles(k, start, length):
        for dx in range(1, GRP + 1):
            away, here, stays = mix(k, lax.rem(grp + dx, GRP), start, length)

            @pl.when(stays)
            def _(here=here):
                here.start()

            @pl.when(jnp.logical_not(stays))
            def _(away=away):
                away.start()

    def make_rim(k):
        top = c_new[pl.ds(pl.multiple_of(jnp.maximum(k * REGION - 8, 0), 8), 8), :]
        bottom = c_new[pl.ds(pl.multiple_of(jnp.minimum(k * REGION + REGION, ROWS - 8), 8), 8), :]
        above = jnp.where(k == 0, top[0:1], top[7:8])
        below = jnp.where(k == SUB - 1, bottom[7:8], bottom[0:1])
        window = edge_cols[pl.ds(pl.multiple_of(k * REGION, 8), 32), :]
        window = jnp.concatenate([window, jnp.zeros((96, 128), jnp.float32)], axis=0)
        cols = pltpu.roll(jnp.transpose(window)[0:8], 121, 1)
        for x in range(GRP):
            c = 2 * x * 128
            tile = pltpu.roll(cols, (4 - 2 * x) % 8, 0)
            tile = jnp.where(row == 0, above[:, c : c + 128], tile)
            tile = jnp.where(row == 1, above[:, c + 128 : c + 256], tile)
            tile = jnp.where(row == 2, below[:, c : c + 128], tile)
            tile = jnp.where(row == 3, below[:, c + 128 : c + 256], tile)
            sendbuf[pl.ds(pl.multiple_of((k * GRP + x) * SLOT + 32, 8), 8), :] = tile

    first = first_chunk(sim)

    def catalyst_chunk(n, _):
        k = lax.rem(first + n, CHUNKS)

        @pl.when(has_prev)
        def _():
            halo(1, 0, chunk_rows(k))(k).wait_recv()

        @pl.when(has_next)
        def _():
            halo(1, 1, chunk_rows(k))(k).wait_recv()

        for h in range(CHUNK // 8):
            r = pl.multiple_of(k * CHUNK + 8 * h, 8)
            c, lap = in_plane(cbuf, r)
            lap = lap + c_up[pl.ds(r, 8), :] + c_dn[pl.ds(r, 8), :]
            s = sbuf[pl.ds(pl.multiple_of(r + 8, 8), 8), :]
            new = c + DIFF_C * lap + s * c * c - (FEED + KILL) * c
            c_new[pl.ds(r, 8), :] = new
            next_out[1, 0, pl.ds(r, 8), :] = new
            columns = jnp.zeros((8, 128), jnp.float32)
            for i, (tile, at) in enumerate(beside):
                moved = pltpu.roll(new[:, tile * 128 : tile * 128 + 128], (i - at) % 128, 1)
                columns = jnp.where(lane == i, moved, columns)
            edge_cols[pl.ds(pl.multiple_of(r + 8, 8), 8), :] = columns
            if h == 0:
                @pl.when(k == 0)
                def _(columns=columns):
                    edge_cols[0:8, :] = jnp.broadcast_to(columns[0:1], (8, 128))
            else:
                @pl.when(k == CHUNKS - 1)
                def _(columns=columns):
                    edge_cols[ROWS + 8 : ROWS + 16, :] = jnp.broadcast_to(columns[7:8], (8, 128))
            for tile in range(COLS // 128):
                slot = (k * GRP + tile // 2) * SLOT + (h * 2 + tile % 2) * 8
                sendbuf[pl.ds(pl.multiple_of(slot, 8), 8), :] = new[:, tile * 128 : tile * 128 + 128]

        send_tiles(k, 0, 32)

        @pl.when(n >= 2)
        def _():
            make_rim(lax.rem(first + n - 1, CHUNKS))
            send_tiles(lax.rem(first + n - 1, CHUNKS), 32, 8)

        return 0

    lax.fori_loop(0, CHUNKS, catalyst_chunk, 0)
    last_two = [lax.rem(first + CHUNKS - 1 + n, CHUNKS) for n in range(2)]
    for k in last_two:
        make_rim(k)
    for k in last_two:
        send_tiles(k, 32, 8)

    near_half, far_half = pl.ds(0, ROWS // 2), pl.ds(ROWS // 2, ROWS // 2)

    def to_relay(way):
        return pltpu.make_async_remote_copy(
            src_ref=species.at[0, 0, far_half, :],
            dst_ref=passing,
            send_sem=halo_send.at[0, way],
            recv_sem=relay_recv,
            device_id=partner,
            device_id_type=MESH,
        )

    def from_relay(way):
        return pltpu.make_async_remote_copy(
            src_ref=passing,
            dst_ref=(s_up, s_dn)[way].at[far_half, :],
            send_sem=relay_send,
            recv_sem=halo_recv.at[0, way, 0],
            device_id=relayed_to,
            device_id_type=MESH,
        )

    for way, wanted, end in ((0, has_next, is_a), (1, has_prev, is_b)):
        @pl.when(wanted & jnp.logical_not(end))
        def _(way=way):
            halo(0, way, whole)(0).start()

        @pl.when(end)
        def _(way=way):
            to_relay(way).start()
            halo(0, way, near_half)(0).start()

    def wait_mixed(count, t):
        some = pl.ds(0, count * SLOT)
        return pltpu.make_async_remote_copy(
            src_ref=sendbuf.at[some, :], dst_ref=recvbuf.at[some, :],
            send_sem=mix_send, recv_sem=mix_recv.at[t], device_id=to(sim, grp), device_id_type=MESH,
        )

    extinct = 6.0 / (BLOCKS * MEMBERS)
    log2e = math.log2(math.e)
    thin, narrow = -extinct * log2e / 256.0, -8.0 * log2e / 256.0

    def render(i, _):
        t_now = lax.rem(team + 6 - i, 4)

        @pl.when(t_now == team)
        def _():
            one_slot = pl.ds(0, SLOT)
            pltpu.make_async_copy(sendbuf.at[one_slot, :], recvbuf.at[one_slot, :], own_sem).wait()
            wait_mixed(TEAM - 1, team).wait_recv()

        @pl.when(t_now != team)
        def _():
            wait_mixed(TEAM, t_now).wait_recv()

        for way, wanted in ((0, passes_up), (1, passes_down)):
            @pl.when((i == 2) & wanted)
            def _(way=way):
                to_relay(way).wait_recv()
                from_relay(way).start()

        base = t_now * (TEAM * SLOT)
        sides = jnp.concatenate(
            [
                recvbuf[pl.ds(base + 36, TEAM, stride=SLOT), :],
                recvbuf[pl.ds(base + 37, TEAM, stride=SLOT), :],
                jnp.zeros((128 - 2 * TEAM, 128), jnp.float32),
            ],
            axis=0,
        )
        sides = jnp.transpose(sides)

        for h in range(2):
            for par in range(2):
                near = 2 * par + 8 * h
                side = 3.0 * sides[1 + 8 * h : 9 + 8 * h] + sides[near : near + 8]

                def layer(p, sums, h=h, par=par, side=side):
                    at = pl.multiple_of(base + p * SLOT, 8)
                    rim = recvbuf[pl.ds(at + 32, 8), :]
                    rows = []
                    for t in range(2):
                        mine = recvbuf[pl.ds(at + (2 * h + t) * 8, 8), :]
                        across = recvbuf[pl.ds(at + (2 - 2 * h + t) * 8, 8), :]
                        if par == 0:
                            beyond = rim[t : t + 1] if h == 0 else across[7:8]
                            shifted = jnp.where(row == 0, beyond, pltpu.roll(mine, 1, 0))
                        else:
                            beyond = rim[2 + t : 3 + t] if h == 1 else across[0:1]
                            shifted = jnp.where(row == 7, beyond, pltpu.roll(mine, 7, 0))
                        rows.append(3.0 * mine + shifted)
                    leftmost = pltpu.roll(side, lax.rem(128 - p, 128), 1)
                    rightmost = pltpu.roll(side, 127 - TEAM - p, 1)
                    fwd = [pltpu.roll(v, 1, 1) for v in rows]
                    bwd = [pltpu.roll(v, 127, 1) for v in rows]
                    low = [jnp.where(lane == 0, leftmost, fwd[0]), jnp.where(lane == 0, fwd[0], fwd[1])]
                    high = [jnp.where(lane == 127, bwd[1], bwd[0]), jnp.where(lane == 127, rightmost, bwd[1])]
                    result = []
                    for cpar in range(2):
                        for t in range(2):
                            q = 3.0 * rows[t] + (low, high)[cpar][t]
                            red, green, blue, clear = sums[(cpar * 2 + t) * 4 : (cpar * 2 + t) * 4 + 4]
                            after = clear * jnp.exp2((q * q) * thin)
                            weight = clear - after
                            mid = q - 8.0
                            warm = mid * (3.0 / 16.0)
                            red = red + weight * jnp.tanh(warm)
                            green = green + weight * jnp.exp2((mid * mid) * narrow)
                            blue = blue + weight * jnp.tanh(warm + 0.6)
                            result += [red, green, blue, after]
                    return tuple(result)

                zero, one = jnp.zeros((8, 128), jnp.float32), jnp.ones((8, 128), jnp.float32)
                sums = lax.fori_loop(0, TEAM, layer, (zero, zero, zero, one) * 4, unroll=True)
                for j in range(16):
                    at = t_now * TOTALS + ((h * 2 + par) * 16 + j) * 8
                    totals[pl.ds(pl.multiple_of(at, 8), 8), :] = sums[j]
        return 0

    lax.fori_loop(0, 4, render, 0)

    def piece_rows(n):
        return pl.ds(pl.multiple_of(n * PIECE, PIECE), PIECE)

    for h in range(2):
        for par in range(2):
            for cpar in range(2):
                for t in range(2):
                    base = ((h * 2 + par) * 16 + (cpar * 2 + t) * 4) * 8
                    got = [[totals[i * TOTALS + base + 8 * ch : i * TOTALS + base + 8 * ch + 8, :] for ch in range(4)] for i in range(4)]
                    red, green, blue, clear = got[0]
                    for i in range(1, 4):
                        red = red + clear * got[i][0]
                        green = green + clear * got[i][1]
                        blue = blue + clear * got[i][2]
                        clear = clear * got[i][3]
                    for ch, value in enumerate((red, green, blue, clear)):
                        at = 8 * h * PIECE + ch * 8 + cpar * 4 + par * 2 + t
                        pack[pl.ds(at, 8, stride=PIECE), :] = value

        def send_piece(n, _, h=h):
            j = 8 * h + n
            there = region * REGION + j

            @pl.when(there != sim)
            def _():
                pltpu.make_async_remote_copy(
                    src_ref=pack.at[piece_rows(j), :],
                    dst_ref=parts.at[piece_rows(block), :],
                    send_sem=part_send,
                    recv_sem=part_recv,
                    device_id=to(there, grp),
                    device_id_type=MESH,
                ).start()

            return 0

        lax.fori_loop(0, 8, send_piece, 0)

    @pl.when(self_part)
    def _():
        mine = pltpu.make_async_copy(
            pack.at[piece_rows(lax.rem(sim, REGION)), :], parts.at[piece_rows(block), :], part_own
        )
        mine.start()
        mine.wait()

    def substrate_part(k, _):
        r = pl.multiple_of(8 * k, 8)
        s, lap = in_plane(sbuf, r)
        c = cbuf[pl.ds(pl.multiple_of(r + 8, 8), 8), :]
        next_out[0, 0, pl.ds(r, 8), :] = s + DIFF_S * lap - s * c * c + FEED * (1.0 - s)
        return 0

    lax.fori_loop(0, ROWS // 8, substrate_part, 0, unroll=4)

    @pl.when(has_prev)
    def _():
        halo(0, 0, whole)(0).wait_recv()

    @pl.when(has_next)
    def _():
        halo(0, 1, whole)(0).wait_recv()

    def substrate_rows(k, _):
        rows = pl.ds(pl.multiple_of(8 * k, 8), 8)
        next_out[0, 0, rows, :] = next_out[0, 0, rows, :] + DIFF_S * (s_up[rows, :] + s_dn[rows, :])
        return 0

    lax.fori_loop(0, ROWS // 8, substrate_rows, 0, unroll=4)

    old = lax.broadcasted_iota(jnp.int32, (256, 256), 0)
    new = lax.broadcasted_iota(jnp.int32, (256, 256), 1)
    spread = jnp.where(new == 2 * lax.rem(old, 128) + lax.div(old, 128), 1.0, 0.0).astype(jnp.bfloat16)

    def wait_parts(count):
        some = pl.ds(0, count * PIECE)
        return pltpu.make_async_remote_copy(
            src_ref=pack.at[some, :], dst_ref=parts.at[some, :],
            send_sem=part_send, recv_sem=part_recv, device_id=to(sim, grp), device_id_type=MESH,
        )

    @pl.when(self_part)
    def _():
        wait_parts(BLOCKS - 1).wait_recv()

    @pl.when(jnp.logical_not(self_part))
    def _():
        wait_parts(BLOCKS).wait_recv()

    def add_block(b, totals):
        base = pl.multiple_of(b * PIECE, 8)
        red, green, blue, clear = totals
        got = [parts[pl.ds(base + 8 * ch, 8), :] for ch in range(4)]
        return (
            red + clear * got[0], green + clear * got[1], blue + clear * got[2], clear * got[3],
        )

    zero, one = jnp.zeros((8, 128), jnp.float32), jnp.ones((8, 128), jnp.float32)
    red, green, blue, clear = lax.fori_loop(0, BLOCKS, add_block, (zero, zero, zero, one), unroll=True)
    opaque = 1.0 - clear
    channels = [0.5 * (opaque + red), green, 0.5 * (opaque - blue), opaque]
    flat = jnp.concatenate([jnp.concatenate([v[0:4], v[4:8]], axis=1) for v in channels], axis=0)
    bf16 = jnp.bfloat16
    high = flat.astype(bf16)
    rest = flat - high.astype(jnp.float32)
    middle = rest.astype(bf16)
    low = (rest - middle.astype(jnp.float32)).astype(bf16)
    split = jnp.dot(
        jnp.concatenate([high, middle, low], axis=0), spread, preferred_element_type=jnp.float32
    )
    mixed = split[0:16] + (split[16:32] + split[32:48])
    for ch in range(4):
        for par in range(2):
            for t in range(2):
                n = ch * 4 + par * 2 + t
                frame_out[ch, par : par + 1, t * 256 : t * 256 + 256] = mixed[n : n + 1]

    @pl.when(is_relay)
    def _():
        from_relay(0).wait_send()

    for i in range(2):
        @pl.when(has_next)
        def _(i=i):
            halo(i, 0, whole)(0).wait_send()

        @pl.when(has_prev)
        def _(i=i):
            halo(i, 1, whole)(0).wait_send()

    wait_mixed(MEMBERS - 1, team).wait_send()

    @pl.when(self_part)
    def _():
        wait_parts(BLOCKS - 1).wait_send()

    @pl.when(jnp.logical_not(self_part))
    def _():
        wait_parts(BLOCKS).wait_send()


def shards(species):
    f32 = jnp.float32
    plane = pltpu.VMEM((ROWS, COLS), f32)
    padded = pltpu.VMEM((ROWS + 16, COLS), f32)
    dma = pltpu.SemaphoreType.DMA
    fresh, frame = pl.pallas_call(
        kernel,
        out_shape=(
            jax.ShapeDtypeStruct((2, 1, ROWS, COLS), f32),
            jax.ShapeDtypeStruct((4, 2 * ROWS // SIMS, 2 * COLS // GRP), f32),
        ),
        in_specs=[pl.BlockSpec(memory_space=pltpu.HBM)],
        out_specs=(pl.BlockSpec(memory_space=pltpu.VMEM),) * 2,
        scratch_shapes=[
            padded, padded, plane, plane, plane, plane, pltpu.VMEM((ROWS // 2, COLS), f32),
            plane,
            pltpu.VMEM((ROWS + 16, 128), f32),
            pltpu.VMEM((MEMBERS * SLOT, 128), f32),
            pltpu.VMEM((MEMBERS * SLOT, 128), f32),
            pltpu.VMEM((4 * TOTALS, 128), f32),
            pltpu.VMEM((REGION * PIECE, 128), f32),
            pltpu.VMEM((BLOCKS * PIECE, 128), f32),
            dma((2,)), dma((2, 2)), dma((2, 2, CHUNKS)), dma, dma,
            dma, dma, dma((4,)), dma, dma, dma,
        ],
        compiler_params=pltpu.CompilerParams(
            collective_id=0, has_side_effects=True, vmem_limit_bytes=32 * 1024 * 1024
        ),
        cost_estimate=pl.CostEstimate(flops=20_000_000, bytes_accessed=4_000_000, transcendentals=2_000_000),
    )(pltpu.with_memory_space_constraint(species, pltpu.HBM))
    return fresh, frame


def solution(mesh):
    return jax.shard_map(
        shards,
        mesh=mesh,
        in_specs=(P(None, ("sim", "grp"), None, None),),
        out_specs=(P(None, ("sim", "grp"), None, None), P(None, "sim", "grp")),
        check_vma=False,
    )
```
